128 devices in a mesh: group: 8 (over z, core), member: 16 (over y, x).
Axes of the slice: x: 4, y: 4, z: 4, core: 2. Of those that a mesh axis runs over, the one named last changes fastest.
Arguments:
- query_hidden: bfloat16 [16384, 4096], P(('group', 'member')), may hold values from -8 to 8
- passage_hidden: bfloat16 [16384, 4096], P(('group', 'member')), may hold values from -8 to 8
- norm_gain: float32 [4096], replicated, may hold values from 0.5 to 1.5
- query_weight: float32 [16384], P(('group', 'member')), may hold values from 0.5 to 6
- hneg_ids: int32 [16384, 2], P(('group', 'member')), may hold values from 0 to 16383, as said below
Outputs:
- loss_rows: float32 [16384], P(('group', 'member'))
- query_grad: bfloat16 [16384, 4096], P(('group', 'member'))
- passage_grad: bfloat16 [16384, 4096], P(('group', 'member'))
- gain_grad: float32 [4096], replicated
The draws below stay inside these ranges and needn't reach their ends.
Inputs may be any that keep to these rules, and one draw needn't show every extreme that they name: `hneg_ids`: among the 256 ids of one device's queries, no owner device (id // 128) is named more than 4 times; one owner device, the same for all devices, is named exactly 4 times by every device. No id equals its own query's row.
All inputs are finite; a program needn't handle non-finite values.
Results may differ from the reference program's by a relative error of at most 0.015.
Values may be sent and summed in bfloat16 or wider, within the bound.
No kernel may reach another device: no remote copies, remote signals or barrier semaphores. Data moves between devices by JAX's collectives and lax.ppermute only.
A program may use at most 128 MiB of HBM per device.

```python
import math
import jax
import jax.numpy as jnp
from jax import lax

EMBED_WIDTH = 4096
Q_DEV = 128
HNEG = 2
QUERIES = 16384
CAP = 4
N_GROUP = 8
N_MEMBER = 16
DEVICES = 128


def shared_ids(key):
    key = jax.random.fold_in(key, 101)
    requests = Q_DEV * HNEG
    hot_owner = jax.random.randint(jax.random.fold_in(key, 1), (), 0, DEVICES)

    def per_device(device_index):
        dev_key = jax.random.fold_in(key, device_index + 2)
        first_key, second_key, third_key = jax.random.split(dev_key, 3)
        owner_pool = jnp.arange((DEVICES - 1) * CAP, dtype=jnp.int32) // CAP
        owner_pool = owner_pool + (owner_pool >= hot_owner).astype(jnp.int32)
        owner_pool = jax.random.permutation(first_key, owner_pool)[:requests - CAP]
        owners = jnp.concatenate([jnp.full((CAP,), hot_owner, jnp.int32), owner_pool])
        owners = jax.random.permutation(second_key, owners)
        local_row = jax.random.randint(third_key, (requests,), 0, Q_DEV)
        query_row = device_index * Q_DEV + jnp.arange(requests, dtype=jnp.int32) // HNEG
        picked = owners * Q_DEV + local_row
        picked = jnp.where(picked == query_row, owners * Q_DEV + (local_row + 1) % Q_DEV, picked)
        return picked.reshape(Q_DEV, HNEG)
    return jax.vmap(per_device)(jnp.arange(DEVICES, dtype=jnp.int32)).reshape(QUERIES, HNEG)


def shared_base(key, strength):
    key = jax.random.fold_in(key, 202)
    base_rows = jax.random.normal(key, (QUERIES, EMBED_WIDTH), jnp.float32)
    fresh = jax.random.normal(jax.random.fold_in(key, 1), (QUERIES, EMBED_WIDTH), jnp.float32)
    row_numbers = jnp.arange(QUERIES, dtype=jnp.int32)
    aligned = ((row_numbers % 97 == 5) & (row_numbers % Q_DEV != Q_DEV - 1)).astype(jnp.float32) * strength
    follower = jnp.roll(aligned, 1)
    base_rows = base_rows + follower[:, None] * (0.99 * jnp.roll(base_rows, 1, axis=0) + 0.14 * fresh - base_rows)
    return base_rows


def draw_hneg_ids(key, part):
    return shared_ids(key)


def draw_passage_hidden(key, part):
    base_rows = shared_base(key, 0.0)
    return jnp.clip(base_rows, -8.0, 8.0).astype(jnp.bfloat16)


def draw_query_hidden(key, part):
    picked = shared_ids(key)
    base_rows = shared_base(key, 0.0)
    key = jax.random.fold_in(key, 5)
    noise = jax.random.normal(key, (QUERIES, EMBED_WIDTH), jnp.float32)
    hard_sum = jnp.sum(jnp.take(base_rows, picked.reshape(-1), axis=0).reshape(QUERIES, HNEG, EMBED_WIDTH), axis=1)
    root_width = math.sqrt(EMBED_WIDTH)
    noise_share = math.sqrt(1.0 - (16.0 + 12.25 * HNEG) / EMBED_WIDTH)
    queries = (4.0 * base_rows + 3.5 * hard_sum) / root_width + noise_share * noise
    return jnp.clip(queries, -8.0, 8.0).astype(jnp.bfloat16)


def draw_query_weight(key, part):
    key = jax.random.fold_in(key, 7)
    device_of = (jnp.arange(QUERIES, dtype=jnp.int32) // Q_DEV).astype(jnp.float32)
    rising = jnp.exp(jnp.log(3.0) * device_of / (DEVICES - 1))
    factor = jax.random.uniform(key, (QUERIES,), jnp.float32, 0.5, 2.0)
    return rising * factor


def setup_inputs(seed: int = 0) -> dict:
    seeds = jax.random.split(jax.random.key(seed), 6)
    query_hidden = draw_query_hidden(jax.random.fold_in(seeds[5], 71), 0)
    passage_hidden = draw_passage_hidden(jax.random.fold_in(seeds[5], 71), 0)
    norm_gain = jnp.clip(1.0 + 0.1 * jax.random.normal(seeds[2], (EMBED_WIDTH,), jnp.float32), 0.5, 1.5)
    query_weight = draw_query_weight(jax.random.fold_in(seeds[5], 71), 0)
    hneg_ids = draw_hneg_ids(jax.random.fold_in(seeds[5], 71), 0)
    return {"query_hidden": query_hidden, "passage_hidden": passage_hidden, "norm_gain": norm_gain, "query_weight": query_weight, "hneg_ids": hneg_ids}


EPSILON = 1e-06
SOFTMAX_TEMPER = 0.28

def normalize(hidden, gain_vector):
    values = hidden.astype(jnp.float32)
    inverse = lax.rsqrt(lax.optimization_barrier(jnp.mean(values * values, axis=-1, keepdims=True)) + EPSILON)
    unit_rows = values * inverse
    return ((unit_rows * gain_vector).astype(jnp.bfloat16), unit_rows, inverse)

def norm_backward(upstream, unit_rows, inverse, gain_vector):
    scaled = upstream * gain_vector
    average_inner = lax.optimization_barrier(jnp.mean(scaled * unit_rows, axis=-1, keepdims=True))
    return ((inverse * (scaled - unit_rows * average_inner)).astype(jnp.bfloat16), lax.optimization_barrier(jnp.sum(upstream * unit_rows, axis=0)))

def rounded(values):
    return lax.optimization_barrier(values.astype(jnp.bfloat16)).astype(jnp.float32)

def reference(query_hidden, passage_hidden, norm_gain, query_weight, hneg_ids):
    logit_scale = 1.0 / (SOFTMAX_TEMPER * math.sqrt(EMBED_WIDTH))
    span = Q_DEV * N_MEMBER
    q_emb, q_unit, q_inv = normalize(query_hidden, norm_gain)
    p_emb, p_unit, p_inv = normalize(passage_hidden, norm_gain)
    hard_all = jnp.take(p_emb, hneg_ids.reshape(-1), axis=0).reshape(QUERIES, HNEG, EMBED_WIDTH)
    target = (jnp.arange(span, dtype=jnp.int32)[:, None] == jnp.arange(span, dtype=jnp.int32)[None, :]).astype(jnp.float32)

    def one_group(group_index):
        low_row = (group_index * span).astype(jnp.int32)
        q_rows = lax.dynamic_slice_in_dim(q_emb, low_row, span, 0)
        p_rows = lax.dynamic_slice_in_dim(p_emb, low_row, span, 0)
        row_weight = lax.dynamic_slice_in_dim(query_weight, low_row, span, 0)
        hard_rows = lax.dynamic_slice_in_dim(hard_all, low_row, span, 0)
        scores = logit_scale * jnp.dot(q_rows, p_rows.T, preferred_element_type=jnp.float32)
        hard_scores = logit_scale * jnp.einsum('qd,qkd->qk', q_rows.astype(jnp.float32), hard_rows.astype(jnp.float32))
        row_max = jnp.maximum(lax.optimization_barrier(jnp.max(scores, axis=1)), lax.optimization_barrier(jnp.max(hard_scores, axis=1)))
        exp_inner = jnp.exp(scores - row_max[:, None])
        exp_hard = jnp.exp(hard_scores - row_max[:, None])
        denominator = lax.optimization_barrier(jnp.sum(exp_inner, axis=1)) + lax.optimization_barrier(jnp.sum(exp_hard, axis=1))
        log_total = row_max + jnp.log(denominator)
        loss_rows = log_total - jnp.diagonal(scores)
        numerator = jnp.dot(exp_inner.astype(jnp.bfloat16), p_rows, preferred_element_type=jnp.float32)
        numerator = numerator + jnp.einsum('qk,qkd->qd', rounded(exp_hard), hard_rows.astype(jnp.float32))
        query_up = logit_scale * row_weight[:, None] * (numerator / denominator[:, None] - p_rows.astype(jnp.float32))
        coeff = (row_weight[:, None] * (jnp.exp(scores - log_total[:, None]) - target)).astype(jnp.bfloat16)
        hard_coeff = (row_weight[:, None] * jnp.exp(hard_scores - log_total[:, None])).astype(jnp.bfloat16)

        def add_member(member_index, grad_sum):
            first_row = (member_index * Q_DEV).astype(jnp.int32)
            coeff_part = lax.dynamic_slice_in_dim(coeff, first_row, Q_DEV, 0)
            query_part = lax.dynamic_slice_in_dim(q_rows, first_row, Q_DEV, 0)
            term_block = logit_scale * jnp.dot(coeff_part.T, query_part, preferred_element_type=jnp.float32)
            return grad_sum + rounded(term_block)
        in_batch = lax.fori_loop(0, N_MEMBER, add_member, jnp.zeros((span, EMBED_WIDTH), jnp.float32))
        partial_term = (logit_scale * hard_coeff.astype(jnp.float32)[:, :, None] * q_rows.astype(jnp.float32)[:, None, :]).astype(jnp.bfloat16)
        return (loss_rows, query_up, in_batch, partial_term)
    loss_rows, query_up, in_batch, partial_term = lax.map(one_group, jnp.arange(N_GROUP, dtype=jnp.int32))
    hard_grad = jnp.zeros((QUERIES, EMBED_WIDTH), jnp.float32).at[hneg_ids.reshape(-1)].add(partial_term.reshape(-1, EMBED_WIDTH).astype(jnp.float32))
    passage_up = in_batch.reshape(QUERIES, EMBED_WIDTH) + hard_grad
    query_grad, query_gain = norm_backward(query_up.reshape(QUERIES, EMBED_WIDTH), q_unit, q_inv, norm_gain)
    passage_grad, passage_gain = norm_backward(passage_up, p_unit, p_inv, norm_gain)
    return (loss_rows.reshape(QUERIES), query_grad, passage_grad, query_gain + passage_gain)
```

```python
import math

import jax
import jax.numpy as jnp
from jax import lax
from jax.sharding import Mesh, PartitionSpec as P

EPSILON = 1e-06
SOFTMAX_TEMPER = 0.28
RING = 4
CAP = 4
GROUPS = ("z", "c")
ALL_AXES = ("z", "c", "y", "x")


def normalize(hidden, gain_vector):
    values = hidden.astype(jnp.float32)
    inverse = lax.rsqrt(jnp.mean(values * values, axis=-1, keepdims=True) + EPSILON)
    unit_rows = values * inverse
    return ((unit_rows * gain_vector).astype(jnp.bfloat16), unit_rows, inverse)


def norm_backward(upstream, unit_rows, inverse, gain_vector):
    scaled = upstream * gain_vector
    average_inner = jnp.mean(scaled * unit_rows, axis=-1, keepdims=True)
    return (inverse * (scaled - unit_rows * average_inner)).astype(jnp.bfloat16)


def shift(value, axis, step):
    return lax.ppermute(value, axis, [(i, (i + step) % RING) for i in range(RING)])


def ring_gather(block, axis):
    half = block.shape[0] // 2
    up_one = shift(block, axis, -1)
    down_one = shift(block, axis, 1)
    first = shift(up_one[:half], axis, -1)
    second = shift(down_one[half:], axis, 1)
    return [block, up_one, jnp.concatenate([first, second], axis=0), down_one]


def ring_scatter(block_1, block_2, block_3, axis):
    half = block_2.shape[0] // 2
    far = block_2.astype(jnp.bfloat16)
    first = shift(far[:half], axis, 1)
    second = shift(far[half:], axis, -1)
    up = jnp.concatenate([block_1[:half] + first.astype(jnp.float32), block_1[half:]], axis=0)
    down = jnp.concatenate([block_3[:half], block_3[half:] + second.astype(jnp.float32)], axis=0)
    from_below = shift(up.astype(jnp.bfloat16), axis, 1)
    from_above = shift(down.astype(jnp.bfloat16), axis, -1)
    return from_below.astype(jnp.float32) + from_above.astype(jnp.float32)


def all_sum(value, z_size):
    value = value + lax.ppermute(value, "c", [(0, 1), (1, 0)])
    for axis, size in (("x", RING), ("y", RING), ("z", z_size)):
        value = value + lax.ppermute(value, axis, [(i, i ^ 1) for i in range(size)])
        value = value + lax.ppermute(value, axis, [(i, size - 1 - i) for i in range(size)])
    return value


def group_rows(rows, group_count):
    blocks = rows.reshape(group_count, rows.shape[0] // group_count, rows.shape[1])
    return lax.all_to_all(blocks, GROUPS, 0, 0, tiled=True).reshape(rows.shape)


def group_table(table, group_count):
    z_count = group_count // 2
    z_place, c_place = lax.axis_index("z"), lax.axis_index("c")
    got = jnp.zeros_like(table)
    places = jnp.arange(group_count, dtype=jnp.int32)[:, None]
    for z_step in range(z_count):
        for c_step in range(2):
            to_group = ((z_place + z_step) % z_count) * 2 + (c_place ^ c_step)
            from_group = ((z_place + z_count - z_step) % z_count) * 2 + (c_place ^ c_step)
            row = jnp.sum(jnp.where(places == to_group, table, 0), axis=0, keepdims=True)
            if z_step or c_step:
                row = lax.ppermute(
                    row,
                    GROUPS,
                    [
                        (z * 2 + c, ((z + z_step) % z_count) * 2 + (c ^ c_step))
                        for z in range(z_count)
                        for c in range(2)
                    ],
                )
            got = got + jnp.where(places == from_group, row, 0)
    return got


def dot(left, right, left_dim, right_dim):
    return lax.dot_general(
        left, right, (((left_dim,), (right_dim,)), ((), ())), preferred_element_type=jnp.float32
    )


def on_device(query_hidden, passage_hidden, norm_gain, query_weight, hneg_ids):
    rows, width = query_hidden.shape
    neg_count = hneg_ids.shape[1]
    z_count = lax.axis_size("z")
    group_count = 2 * z_count
    line = RING * rows
    scale = 1.0 / (SOFTMAX_TEMPER * math.sqrt(width))
    y_place, x_place = lax.axis_index("y"), lax.axis_index("x")

    flat_ids = hneg_ids.reshape(-1)
    id_count = rows * neg_count
    owners = flat_ids // rows
    local_row = flat_ids % rows
    number = jnp.arange(id_count, dtype=jnp.int32)
    same = (owners[:, None] == owners[None, :]) & (number[None, :] < number[:, None])
    rank = jnp.sum(same.astype(jnp.int32), axis=1)
    y_step = (owners // RING - y_place) % RING
    line_of = (owners // (RING * RING)) * RING + owners % RING
    slot = (line_of * RING + y_step) * CAP + rank
    slot_count = group_count * RING * RING * CAP
    hit = slot[None, :] == jnp.arange(slot_count, dtype=jnp.int32)[:, None]
    slot_row = jnp.sum(jnp.where(hit, local_row[None, :] + 1, 0), axis=1) - 1
    slot_query = jnp.sum(jnp.where(hit, number[None, :] // neg_count + 1, 0), axis=1) - 1
    asked = lax.all_to_all(
        slot_row.reshape(group_count * RING, RING * CAP), ("z", "c", "x"), 0, 0, tiled=True
    )
    asked = asked.reshape(group_count, RING, RING, CAP).transpose(0, 2, 1, 3)
    by_x = slot_query.reshape(group_count, RING, RING * CAP).transpose(1, 0, 2)
    asker = lax.all_to_all(
        by_x.reshape(RING, group_count * RING * CAP), "x", 0, 0, tiled=True
    ).reshape(RING, group_count, RING, CAP)
    x_step = (jnp.arange(RING, dtype=jnp.int32) - x_place) % RING
    asker = jnp.where(asker < 0, -1, asker + rows * x_step[:, None, None, None])
    asker = asker.transpose(1, 2, 0, 3)
    y_base = rows * jnp.arange(RING - 1, dtype=jnp.int32)
    asked_own = asked[:, 0].reshape(-1)
    asked_far = jnp.where(
        asked[:, 1:] < 0, -1, asked[:, 1:] + y_base[None, :, None, None]
    ).reshape(-1)
    asker_own = asker[:, 0].reshape(-1)
    asker_far = asker[:, 1:].reshape(-1)

    p_emb, p_unit, p_inv = normalize(passage_hidden, norm_gain)
    q_emb, q_unit, q_inv = normalize(query_hidden, norm_gain)
    p_line = ring_gather(p_emb, "y")
    q_line = jnp.concatenate(ring_gather(q_emb, "x"), axis=0)
    p_far = jnp.concatenate(p_line[1:], axis=0)

    place = jnp.arange(line, dtype=jnp.int32)
    pick_own = (asked_own[:, None] == place[None, :rows]).astype(jnp.bfloat16)
    pick_far = (asked_far[:, None] == place[None, : line - rows]).astype(jnp.bfloat16)
    hard_own = group_rows(dot(pick_own, p_emb, 1, 0).astype(jnp.bfloat16), group_count)
    hard_far = group_rows(dot(pick_far, p_far, 1, 0).astype(jnp.bfloat16), group_count)
    send_own = (asker_own[:, None] == place[None, :]).astype(jnp.bfloat16)
    send_far = (asker_far[:, None] == place[None, :]).astype(jnp.bfloat16)
    far_queries = group_rows(dot(send_far, q_line, 1, 0).astype(jnp.bfloat16), group_count)
    own_queries = group_rows(dot(send_own, q_line, 1, 0).astype(jnp.bfloat16), group_count)

    mine_own = place[:, None] == asker_own[None, :]
    mine_far = place[:, None] == asker_far[None, :]
    score_own = scale * dot(q_line, p_emb, 1, 1)
    score_far = scale * dot(q_line, p_far, 1, 1)
    score_hard_own = jnp.where(mine_own, scale * dot(q_line, hard_own, 1, 1), -jnp.inf)
    score_hard_far = jnp.where(mine_far, scale * dot(q_line, hard_far, 1, 1), -jnp.inf)
    blocks = (score_own, score_far, score_hard_own, score_hard_far)
    part_max = jnp.max(jnp.stack([jnp.max(block, axis=1) for block in blocks]), axis=0)
    part_sum = sum(jnp.sum(jnp.exp(block - part_max[:, None]), axis=1) for block in blocks)
    part_log = (part_max + jnp.log(part_sum)).reshape(RING, rows)
    message = jnp.concatenate([part_log, query_weight[None, :]], axis=0)
    logs, weights = [part_log], [query_weight]
    for step in range(1, RING):
        got = shift(message, "x", -step)
        logs.append(jnp.roll(got[:RING], step, axis=0))
        weights.append(got[RING])
    top = jnp.maximum(jnp.maximum(logs[0], logs[1]), jnp.maximum(logs[2], logs[3]))
    log_total = (top + jnp.log(sum(jnp.exp(part - top) for part in logs))).reshape(-1)
    weight = jnp.concatenate(weights, axis=0)
    own_diag = place[:, None] == place[None, :rows]
    positive = jnp.sum(jnp.where(own_diag[:rows], score_own[:rows], 0.0), axis=1)
    loss_rows = log_total[:rows] - positive

    def softmax_part(block):
        return jnp.exp(block - log_total[:, None])

    coeff_own = (weight[:, None] * (softmax_part(score_own) - own_diag.astype(jnp.float32))).astype(
        jnp.bfloat16
    )
    coeff_far = (weight[:, None] * softmax_part(score_far)).astype(jnp.bfloat16)
    hard_coeff_own = (weight[:, None] * softmax_part(score_hard_own)).astype(jnp.bfloat16)
    hard_coeff_far = (weight[:, None] * softmax_part(score_hard_far)).astype(jnp.bfloat16)
    slot_own = jnp.sum(hard_coeff_own.astype(jnp.float32), axis=0).reshape(group_count, -1)
    slot_far = jnp.sum(hard_coeff_far.astype(jnp.float32), axis=0).reshape(group_count, -1)
    slot_coeff = group_table(jnp.concatenate([slot_own, slot_far], axis=1), group_count)
    own_slots = slot_own.shape[1]
    coeff_in_own = slot_coeff[:, :own_slots].reshape(-1)
    coeff_in_far = slot_coeff[:, own_slots:].reshape(-1)

    query_part = scale * (
        dot(coeff_own, p_emb, 1, 0)
        + dot(coeff_far, p_far, 1, 0)
        + dot(hard_coeff_own, hard_own, 1, 0)
        + dot(hard_coeff_far, hard_far, 1, 0)
    )
    query_blocks = [query_part[i * rows : (i + 1) * rows] for i in range(RING)]
    query_up = query_blocks[0] + ring_scatter(*query_blocks[1:], "x")
    query_grad = norm_backward(query_up, q_unit, q_inv, norm_gain)
    gain_grad = 2.0 * all_sum(jnp.sum(query_up * q_unit, axis=0).reshape(-1, 128), z_count)

    put_far = jnp.where(
        place[: line - rows, None] == asked_far[None, :], coeff_in_far[None, :], 0.0
    ).astype(jnp.bfloat16)
    put_own = jnp.where(
        place[:rows, None] == asked_own[None, :], coeff_in_own[None, :], 0.0
    ).astype(jnp.bfloat16)
    far_part = scale * (dot(coeff_far, q_line, 0, 0) + dot(put_far, far_queries, 1, 0))
    own_part = scale * (dot(coeff_own, q_line, 0, 0) + dot(put_own, own_queries, 1, 0))
    far_blocks = [far_part[i * rows : (i + 1) * rows] for i in range(RING - 1)]
    passage_up = own_part + ring_scatter(*far_blocks, "y")
    passage_grad = norm_backward(passage_up, p_unit, p_inv, norm_gain)
    return (loss_rows, query_grad, passage_grad, gain_grad.reshape(-1))


def solution(mesh):
    torus = Mesh(mesh.devices.reshape(-1, 2, RING, RING), ALL_AXES)
    return jax.shard_map(
        on_device,
        mesh=torus,
        in_specs=(
            P(ALL_AXES, None),
            P(ALL_AXES, None),
            P(),
            P(ALL_AXES),
            P(ALL_AXES, None),
        ),
        out_specs=(
            P(ALL_AXES),
            P(ALL_AXES, None),
            P(ALL_AXES, None),
            P(),
        ),
        check_vma=False,
    )
```

```python
import math

import jax
import jax.numpy as jnp
from jax import lax
from jax.experimental import pallas as pl
from jax.experimental.pallas import tpu as pltpu
from jax.sharding import Mesh, PartitionSpec as P

EPSILON = 1e-06
SOFTMAX_TEMPER = 0.28
RING = 4
CAP = 4
GROUPS = ("z", "c")
ALL_AXES = ("z", "c", "y", "x")
VMEM_BYTES = 60 * 1024 * 1024
LOW = -1e30


def shift(value, axis, step):
    return lax.ppermute(value, axis, [(i, (i + step) % RING) for i in range(RING)])


def ring_gather(block, axis):
    half = block.shape[0] // 2
    low, high = block[:half], block[half:]
    up_low = shift(low, axis, -1)
    down_high = shift(high, axis, 1)
    up_high = shift(high, axis, -1)
    down_low = shift(low, axis, 1)
    far_low = shift(up_low, axis, -1)
    far_high = shift(down_high, axis, 1)
    return [up_low, up_high, far_low, far_high, down_low, down_high]


def ring_scatter(blocks, axis):
    low_1, high_1, low_2, high_2, low_3, high_3 = blocks
    passing_low = shift(low_2, axis, 1)
    passing_high = shift(high_2, axis, -1)
    from_below_high = shift(high_1, axis, 1)
    from_above_low = shift(low_3, axis, -1)
    wide = jnp.float32
    both_low = (low_1.astype(wide) + passing_low.astype(wide)).astype(jnp.bfloat16)
    both_high = (high_3.astype(wide) + passing_high.astype(wide)).astype(jnp.bfloat16)
    from_below_low = shift(both_low, axis, 1)
    from_above_high = shift(both_high, axis, -1)
    return [from_below_low, from_above_low], [from_below_high, from_above_high]


def all_sum(value, z_size):
    value = value + lax.ppermute(value, "c", [(0, 1), (1, 0)])
    for axis, size in (("x", RING), ("y", RING), ("z", z_size)):
        value = value + lax.ppermute(value, axis, [(i, i ^ 1) for i in range(size)])
        value = value + lax.ppermute(value, axis, [(i, size - 1 - i) for i in range(size)])
    return value


def group_rows(rows, group_count):
    blocks = rows.reshape(group_count, rows.shape[0] // group_count, rows.shape[1])
    return lax.all_to_all(blocks, GROUPS, 0, 0, tiled=True).reshape(rows.shape)


def group_table(table, group_count):
    z_count = group_count // 2
    z_place, c_place = lax.axis_index("z"), lax.axis_index("c")
    got = jnp.zeros_like(table)
    places = jnp.arange(group_count, dtype=jnp.int32)[:, None]
    for z_step in range(z_count):
        for c_step in range(2):
            to_group = ((z_place + z_step) % z_count) * 2 + (c_place ^ c_step)
            from_group = ((z_place + z_count - z_step) % z_count) * 2 + (c_place ^ c_step)
            row = jnp.sum(jnp.where(places == to_group, table, 0), axis=0, keepdims=True)
            if z_step or c_step:
                row = lax.ppermute(
                    row,
                    GROUPS,
                    [
                        (z * 2 + c, ((z + z_step) % z_count) * 2 + (c ^ c_step))
                        for z in range(z_count)
                        for c in range(2)
                    ],
                )
            got = got + jnp.where(places == from_group, row, 0)
    return got


def line_table(table):
    x_place = lax.axis_index("x")
    places = jnp.arange(RING, dtype=jnp.int32)[:, None]
    got = jnp.where(places == x_place, table, 0)
    for step in range(1, RING):
        chosen = places == (x_place + step) % RING
        row = jnp.sum(jnp.where(chosen, table, 0), axis=0, keepdims=True)
        row = shift(row, "x", step)
        got = got + jnp.where(places == (x_place + RING - step) % RING, row, 0)
    return got


def mxu(left, right, left_dim=1, right_dim=0):
    return lax.dot_general(
        left, right, (((left_dim,), (right_dim,)), ((), ())), preferred_element_type=jnp.float32
    )


def params(steps_kind="arbitrary"):
    return pltpu.CompilerParams(
        dimension_semantics=(steps_kind,), vmem_limit_bytes=VMEM_BYTES
    )


SMALL = pl.CostEstimate(flops=1, bytes_accessed=1, transcendentals=0)


def tile(width):
    return min(512, width)


def whole(shape):
    return pl.BlockSpec(shape, lambda i: (0,) * len(shape))


def columns(rows, width):
    return pl.BlockSpec((rows, tile(width)), lambda i: (0, i))


def joined(refs):
    blocks = [ref[...] for ref in refs]
    return blocks[0] if len(blocks) == 1 else jnp.concatenate(blocks, axis=0)


def inverse_norm(values):
    return lax.rsqrt(jnp.mean(values * values, axis=-1, keepdims=True) + EPSILON)


def embed(hidden, gain):
    def body(hidden_ref, gain_ref, out_ref):
        values = hidden_ref[...].astype(jnp.float32)
        unit_rows = values * inverse_norm(values)
        out_ref[...] = (unit_rows * gain_ref[...]).astype(jnp.bfloat16)

    rows, width = hidden.shape
    step = min(64, rows)
    block = pl.BlockSpec((step, width), lambda i: (i, 0))
    return pl.pallas_call(
        body,
        grid=(rows // step,),
        in_specs=[block, whole((1, width))],
        out_specs=block,
        out_shape=jax.ShapeDtypeStruct((rows, width), jnp.bfloat16),
        compiler_params=params(),
        cost_estimate=SMALL,
        name="embed",
    )(hidden, gain)


def finish(hidden, gain, terms, low_terms, high_terms):
    rows, width = hidden.shape
    half = rows // 2
    step = half // 2
    count, low_count = len(terms), len(low_terms)

    def body(hidden_ref, gain_ref, *refs):
        out_ref = refs[-1]
        upstream = refs[0][...].astype(jnp.float32)
        for ref in refs[1:count]:
            upstream += ref[...].astype(jnp.float32)

        def done(total):
            values = hidden_ref[...].astype(jnp.float32)
            inverse = inverse_norm(values)
            unit_rows = values * inverse
            scaled = total * gain_ref[...]
            inner = jnp.mean(scaled * unit_rows, axis=-1, keepdims=True)
            out_ref[...] = (inverse * (scaled - unit_rows * inner)).astype(jnp.bfloat16)

        def add(total, extra):
            for ref in extra:
                total += ref[...].astype(jnp.float32)
            return total

        if low_count:
            low_half = pl.program_id(0) < half // step

            @pl.when(low_half)
            def _():
                done(add(upstream, refs[count : count + low_count]))

            @pl.when(jnp.logical_not(low_half))
            def _():
                done(add(upstream, refs[count + low_count : -1]))

        else:
            done(upstream)

    block = pl.BlockSpec((step, width), lambda i: (i, 0))
    per_half = half // step
    low = pl.BlockSpec((step, width), lambda i: (jnp.minimum(i, per_half - 1), 0))
    high = pl.BlockSpec((step, width), lambda i: (jnp.maximum(i - per_half, 0), 0))
    return pl.pallas_call(
        body,
        grid=(rows // step,),
        in_specs=[block, whole((1, width))]
        + [block] * count
        + [low] * low_count
        + [high] * len(high_terms),
        out_specs=block,
        out_shape=jax.ShapeDtypeStruct((rows, width), jnp.bfloat16),
        compiler_params=params(),
        cost_estimate=SMALL,
        name="finish",
    )(hidden, gain, *terms, *low_terms, *high_terms)


def pick_rows(matrix, sources):
    width = sources[0].shape[1]

    def body(matrix_ref, *refs):
        refs[-1][...] = mxu(matrix_ref[...], joined(refs[:-1])).astype(jnp.bfloat16)

    return pl.pallas_call(
        body,
        grid=(width // tile(width),),
        in_specs=[whole(matrix.shape)] + [columns(s.shape[0], width) for s in sources],
        out_specs=columns(matrix.shape[0], width),
        out_shape=jax.ShapeDtypeStruct((matrix.shape[0], width), jnp.bfloat16),
        compiler_params=params(),
        cost_estimate=SMALL,
        name="pick_rows",
    )(matrix, *sources)


def line_scores(sources, queries, scale):
    width = queries.shape[1]
    steps = width // tile(width)

    def body(query_ref, *refs):
        step = pl.program_id(0)
        out_ref = refs[-1]

        @pl.when(step == 0)
        def _():
            out_ref[...] = jnp.zeros_like(out_ref)

        out_ref[...] += scale * mxu(joined(refs[:-1]), query_ref[...], 1, 1)

    out = (sum(s.shape[0] for s in sources), queries.shape[0])
    return pl.pallas_call(
        body,
        grid=(steps,),
        in_specs=[columns(queries.shape[0], width)]
        + [columns(s.shape[0], width) for s in sources],
        out_specs=whole(out),
        out_shape=jax.ShapeDtypeStruct(out, jnp.float32),
        compiler_params=params(),
        cost_estimate=SMALL,
        name="line_scores",
    )(queries, *sources)


def far_scores(near, far_rows, queries, asked_by, line, scale):
    width = queries.shape[1]
    query_count = queries.shape[0]
    steps = width // tile(width)
    near_slots = near.shape[0] - line

    def body(near_ref, mask_ref, rows_ref, query_ref, out_ref, log_ref):
        step = pl.program_id(0)

        @pl.when(step == 0)
        def _():
            out_ref[...] = jnp.zeros_like(out_ref)

        out_ref[...] += scale * mxu(rows_ref[...], query_ref[...], 1, 1)

        @pl.when(step == steps - 1)
        def _():
            inner = near_ref[:line, :]
            own = jnp.where(mask_ref[:near_slots, :] > 0, near_ref[line:, :], LOW)
            far = jnp.where(mask_ref[near_slots:, :] > 0, out_ref[...], LOW)
            parts = (inner, own, far)
            top = jnp.max(inner, axis=0, keepdims=True)
            for part in parts[1:]:
                top = jnp.maximum(top, jnp.max(part, axis=0, keepdims=True))
            total = jnp.zeros_like(top)
            for part in parts:
                total += jnp.sum(jnp.exp(part - top), axis=0, keepdims=True)
            log_ref[...] = top + jnp.log(total)

    return pl.pallas_call(
        body,
        grid=(steps,),
        in_specs=[
            whole(near.shape),
            whole(asked_by.shape),
            columns(far_rows.shape[0], width),
            columns(query_count, width),
        ],
        out_specs=[whole((far_rows.shape[0], query_count)), whole((1, query_count))],
        out_shape=[
            jax.ShapeDtypeStruct((far_rows.shape[0], query_count), jnp.float32),
            jax.ShapeDtypeStruct((1, query_count), jnp.float32),
        ],
        compiler_params=params(),
        cost_estimate=SMALL,
        name="far_scores",
    )(near, asked_by, far_rows, queries)


def query_side(near, far, asked_by, log_total, weight, target, queries, sources, line, scale):
    width = queries.shape[1]
    query_count = queries.shape[0]
    near_slots = near.shape[0] - line
    slot_count = asked_by.shape[0]
    count = len(sources)

    def body(near_ref, far_ref, mask_ref, log_ref, weight_ref, target_ref, query_ref, *refs):
        source_refs = refs[:count]
        part_ref, gain_ref, coeff_ref, slot_ref, positive_ref, turned_ref = refs[count:]

        @pl.when(pl.program_id(0) == 0)
        def _():
            log_row, weight_row = log_ref[...], weight_ref[...]
            inner = near_ref[:line, :]
            row_place = lax.broadcasted_iota(jnp.int32, inner.shape, 0)
            hit = row_place == target_ref[...]
            positive_ref[...] = jnp.sum(jnp.where(hit, inner, 0.0), axis=0, keepdims=True)
            inner_coeff = weight_row * (jnp.exp(inner - log_row) - jnp.where(hit, 1.0, 0.0))
            coeff_ref[...] = inner_coeff.astype(jnp.bfloat16)
            own = jnp.where(mask_ref[:near_slots, :] > 0, near_ref[line:, :], LOW)
            slots = jnp.where(mask_ref[near_slots:, :] > 0, far_ref[...], LOW)
            own_coeff = (weight_row * jnp.exp(own - log_row)).astype(jnp.bfloat16)
            far_coeff = (weight_row * jnp.exp(slots - log_row)).astype(jnp.bfloat16)
            ones = jnp.ones((8, query_count), jnp.bfloat16)
            slot_ref[:, :near_slots] = mxu(ones, own_coeff, 1, 1)
            slot_ref[:, near_slots:] = mxu(ones, far_coeff, 1, 1)
            turned_ref[:, :line] = jnp.transpose(inner_coeff).astype(jnp.bfloat16)
            turned_ref[:, line : line + near_slots] = jnp.transpose(
                own_coeff.astype(jnp.float32)
            ).astype(jnp.bfloat16)
            turned_ref[:, line + near_slots :] = jnp.transpose(
                far_coeff.astype(jnp.float32)
            ).astype(jnp.bfloat16)

        total = scale * mxu(turned_ref[...], joined(source_refs))
        part_ref[...] = total.astype(jnp.bfloat16)
        gain_ref[...] = jnp.sum(total * query_ref[...].astype(jnp.float32), axis=0, keepdims=True)

    row = whole((1, query_count))
    return pl.pallas_call(
        body,
        grid=(width // tile(width),),
        in_specs=[
            whole(near.shape),
            whole(far.shape),
            whole(asked_by.shape),
            row,
            row,
            row,
            columns(query_count, width),
        ]
        + [columns(s.shape[0], width) for s in sources],
        out_specs=[
            columns(query_count, width),
            columns(1, width),
            whole((line, query_count)),
            whole((8, slot_count)),
            row,
        ],
        out_shape=[
            jax.ShapeDtypeStruct((query_count, width), jnp.bfloat16),
            jax.ShapeDtypeStruct((1, width), jnp.float32),
            jax.ShapeDtypeStruct((line, query_count), jnp.bfloat16),
            jax.ShapeDtypeStruct((8, slot_count), jnp.float32),
            jax.ShapeDtypeStruct((1, query_count), jnp.float32),
        ],
        scratch_shapes=[pltpu.VMEM((query_count, line + slot_count), jnp.bfloat16)],
        compiler_params=params(),
        cost_estimate=SMALL,
        name="query_side",
    )(near, far, asked_by, log_total, weight, target, queries, *sources)


def passage_side(coeff, queries, put, arrived, scale, out_type, pieces):
    width = queries.shape[1]
    rows = coeff.shape[0] // pieces

    def body(coeff_ref, query_ref, put_ref, arrived_ref, *out_refs):
        total = mxu(coeff_ref[...], query_ref[...]) + mxu(put_ref[...], arrived_ref[...])
        total = scale * total
        for i, out_ref in enumerate(out_refs):
            out_ref[...] = total[i * rows : (i + 1) * rows].astype(out_type)

    return pl.pallas_call(
        body,
        grid=(width // tile(width),),
        in_specs=[
            whole(coeff.shape),
            columns(queries.shape[0], width),
            whole(put.shape),
            columns(arrived.shape[0], width),
        ],
        out_specs=[columns(rows, width)] * pieces,
        out_shape=[jax.ShapeDtypeStruct((rows, width), out_type)] * pieces,
        compiler_params=params(),
        cost_estimate=SMALL,
        name="passage_side",
    )(coeff, queries, put, arrived)


def on_device(query_hidden, passage_hidden, norm_gain, query_weight, hneg_ids):
    rows, width = query_hidden.shape
    neg_count = hneg_ids.shape[1]
    z_count = lax.axis_size("z")
    group_count = 2 * z_count
    line = RING * rows
    scale = 1.0 / (SOFTMAX_TEMPER * math.sqrt(width))
    y_place, x_place = lax.axis_index("y"), lax.axis_index("x")

    gain = norm_gain.reshape(1, width)
    p_emb = embed(passage_hidden, gain)
    p_far = ring_gather(p_emb, "y")

    flat_ids = hneg_ids.reshape(-1)
    id_count = rows * neg_count
    owners = flat_ids // rows
    local_row = flat_ids % rows
    number = jnp.arange(id_count, dtype=jnp.int32)
    same = (owners[:, None] == owners[None, :]) & (number[None, :] < number[:, None])
    rank = jnp.sum(same.astype(jnp.int32), axis=1)
    y_step = (owners // RING - y_place) % RING
    line_of = (owners // (RING * RING)) * RING + owners % RING
    slot = (line_of * RING + y_step) * CAP + rank
    slot_count = group_count * RING * RING * CAP
    hit = slot[None, :] == jnp.arange(slot_count, dtype=jnp.int32)[:, None]
    slot_row = jnp.sum(jnp.where(hit, local_row[None, :] + 1, 0), axis=1) - 1
    slot_query = jnp.sum(jnp.where(hit, number[None, :] // neg_count + 1, 0), axis=1)
    slot_row, p_emb = lax.optimization_barrier((slot_row, p_emb))
    asked = lax.all_to_all(
        slot_row.reshape(group_count * RING, RING * CAP), ("z", "c", "x"), 0, 0, tiled=True
    )
    asked = asked.reshape(group_count, RING, RING, CAP).transpose(0, 2, 1, 3)
    y_base = rows * jnp.arange(RING - 1, dtype=jnp.int32)
    asked_own = asked[:, 0].reshape(-1)
    asked_far = jnp.where(
        asked[:, 1:] < 0, -1, asked[:, 1:] + y_base[None, :, None, None]
    ).reshape(-1)
    place = jnp.arange(line, dtype=jnp.int32)
    pick_own = (asked_own[:, None] == place[None, :rows]).astype(jnp.bfloat16)
    pick_far = (asked_far[:, None] == place[None, : line - rows]).astype(jnp.bfloat16)
    hard_own = group_rows(pick_rows(pick_own, [p_emb]), group_count)

    q_emb = embed(query_hidden, gain)
    q_line = lax.all_gather(q_emb, "x", axis=0, tiled=True)

    hard_far = group_rows(pick_rows(pick_far, p_far), group_count)

    by_x = slot_query.reshape(group_count, RING, RING * CAP).transpose(1, 0, 2)
    asker = line_table(by_x.reshape(RING, -1)).reshape(RING, group_count, RING, CAP)
    x_base = rows * jnp.arange(RING, dtype=jnp.int32)
    asker = jnp.where(asker == 0, -1, asker - 1 + x_base[:, None, None, None])
    asker = asker.transpose(1, 2, 0, 3)
    asker_own = asker[:, 0].reshape(-1)
    asker_far = asker[:, 1:].reshape(-1)
    send_own = (asker_own[:, None] == place[None, :]).astype(jnp.bfloat16)
    send_far = (asker_far[:, None] == place[None, :]).astype(jnp.bfloat16)
    asked_by = jnp.concatenate([send_own, send_far], axis=0)
    leave_far = pick_rows(send_far, [q_line])
    leave_own = pick_rows(send_own, [q_line])
    q_line, leave_far, leave_own = lax.optimization_barrier((q_line, leave_far, leave_own))
    far_queries = group_rows(leave_far, group_count)
    own_queries = group_rows(leave_own, group_count)

    near = line_scores([p_emb, *p_far, hard_own], q_line, scale)
    far, part_log = far_scores(near, hard_far, q_line, asked_by, line, scale)
    part_log = part_log.reshape(RING, rows)
    own_place = jnp.arange(RING, dtype=jnp.int32)[:, None] == x_place
    own_weight = jnp.where(own_place, query_weight[None, :], 0.0)
    message = jnp.concatenate([part_log, own_weight], axis=0)
    messages = [message] + [shift(message, "x", step) for step in (1, 3, 2)]
    logs = [m[:RING] for m in messages]
    weight = sum(m[RING:] for m in messages).reshape(1, line)
    top = jnp.maximum(jnp.maximum(logs[0], logs[1]), jnp.maximum(logs[2], logs[3]))
    log_total = (top + jnp.log(sum(jnp.exp(part - top) for part in logs))).reshape(1, line)
    first_row = x_place * rows
    target = place[None, :] - first_row
    target = jnp.where((target >= 0) & (target < rows), target, -1)

    part, gain_part, coeff, slot_coeff, positive = query_side(
        near, far, asked_by, log_total, weight, target, q_line,
        [p_emb, *p_far, hard_own, hard_far], line, scale,
    )
    loss_rows = lax.dynamic_slice(log_total - positive, (0, first_row), (1, rows)).reshape(-1)

    gain_grad = all_sum(gain_part.reshape(-1, 128), z_count).reshape(-1)
    gain_grad = 2.0 * gain_grad / norm_gain

    query_up = lax.psum_scatter(part, "x", scatter_dimension=0, tiled=True)
    query_grad = finish(query_hidden, gain, [query_up], [], [])

    own_slots = asker_own.shape[0]
    slot_own = slot_coeff[0, :own_slots].reshape(group_count, -1)
    slot_far = slot_coeff[0, own_slots:].reshape(group_count, -1)
    got_coeff = group_table(jnp.concatenate([slot_own, slot_far], axis=1), group_count)
    per_group = own_slots // group_count
    coeff_in_own = got_coeff[:, :per_group].reshape(-1)
    coeff_in_far = got_coeff[:, per_group:].reshape(-1)
    put_far = jnp.where(
        place[: line - rows, None] == asked_far[None, :], coeff_in_far[None, :], 0.0
    ).astype(jnp.bfloat16)
    put_own = jnp.where(
        place[:rows, None] == asked_own[None, :], coeff_in_own[None, :], 0.0
    ).astype(jnp.bfloat16)
    far_part = passage_side(
        coeff[rows:], q_line, put_far, far_queries, scale, jnp.bfloat16, 2 * (RING - 1)
    )
    low_terms, high_terms = ring_scatter(far_part, "y")
    own_part = passage_side(coeff[:rows], q_line, put_own, own_queries, scale, jnp.float32, 1)[0]
    passage_grad = finish(passage_hidden, gain, [own_part], low_terms, high_terms)
    return (loss_rows, query_grad, passage_grad, gain_grad)


def solution(mesh):
    torus = Mesh(mesh.devices.reshape(-1, 2, RING, RING), ALL_AXES)
    return jax.shard_map(
        on_device,
        mesh=torus,
        in_specs=(
            P(ALL_AXES, None),
            P(ALL_AXES, None),
            P(),
            P(ALL_AXES),
            P(ALL_AXES, None),
        ),
        out_specs=(
            P(ALL_AXES),
            P(ALL_AXES, None),
            P(ALL_AXES, None),
            P(),
        ),
        check_vma=False,
    )
```

```python
import math

import jax
import jax.numpy as jnp
from jax import lax
from jax.experimental import pallas as pl
from jax.experimental.pallas import tpu as pltpu
from jax.sharding import Mesh, PartitionSpec as P

EPSILON = 1e-06
SOFTMAX_TEMPER = 0.28
RING = 4
CAP = 4
GROUPS = ("z", "c")
ALL_AXES = ("z", "c", "y", "x")
MIB = 1024 * 1024
LOW = -1e30


def shift(value, axis, step):
    return lax.ppermute(value, axis, [(i, (i + step) % RING) for i in range(RING)])


def ring_gather(low, high, axis):
    up_low = shift(low, axis, -1)
    down_high = shift(high, axis, 1)
    up_high = shift(high, axis, -1)
    down_low = shift(low, axis, 1)
    far_low = shift(up_low, axis, -1)
    far_high = shift(down_high, axis, 1)
    return [up_low, up_high, down_low, down_high], [far_low, far_high]


def ring_scatter(opposite, beside, axis):
    low_2, high_2 = opposite
    low_1, high_1, low_3, high_3 = beside
    passing_low = shift(low_2, axis, 1)
    passing_high = shift(high_2, axis, -1)
    from_below_high = shift(high_1, axis, 1)
    from_above_low = shift(low_3, axis, -1)
    wide = jnp.float32
    both_low = (low_1.astype(wide) + passing_low.astype(wide)).astype(jnp.bfloat16)
    both_high = (high_3.astype(wide) + passing_high.astype(wide)).astype(jnp.bfloat16)
    from_below_low = shift(both_low, axis, 1)
    from_above_high = shift(both_high, axis, -1)
    return [from_below_low, from_above_low], [from_below_high, from_above_high], both_high


def all_sum(value, z_size):
    value = value + lax.ppermute(value, "c", [(0, 1), (1, 0)])
    for axis, size in (("x", RING), ("z", z_size), ("y", RING)):
        value = value + lax.ppermute(value, axis, [(i, i ^ 1) for i in range(size)])
        value = value + lax.ppermute(value, axis, [(i, size - 1 - i) for i in range(size)])
    return value


def group_rows(rows, group_count):
    blocks = rows.reshape(group_count, rows.shape[0] // group_count, rows.shape[1])
    return lax.all_to_all(blocks, GROUPS, 0, 0, tiled=True).reshape(rows.shape)


def group_table(table, group_count):
    z_count = group_count // 2
    z_place, c_place = lax.axis_index("z"), lax.axis_index("c")
    got = jnp.zeros_like(table)
    places = jnp.arange(group_count, dtype=jnp.int32)[:, None]
    for z_step in range(z_count):
        for c_step in range(2):
            to_group = ((z_place + z_step) % z_count) * 2 + (c_place ^ c_step)
            from_group = ((z_place + z_count - z_step) % z_count) * 2 + (c_place ^ c_step)
            row = jnp.sum(jnp.where(places == to_group, table, 0), axis=0, keepdims=True)
            if z_step or c_step:
                row = lax.ppermute(
                    row,
                    GROUPS,
                    [
                        (z * 2 + c, ((z + z_step) % z_count) * 2 + (c ^ c_step))
                        for z in range(z_count)
                        for c in range(2)
                    ],
                )
            got = got + jnp.where(places == from_group, row, 0)
    return got


def line_table(table):
    x_place = lax.axis_index("x")
    places = jnp.arange(RING, dtype=jnp.int32)[:, None]
    got = jnp.where(places == x_place, table, 0)
    for step in range(1, RING):
        chosen = places == (x_place + step) % RING
        row = jnp.sum(jnp.where(chosen, table, 0), axis=0, keepdims=True)
        row = shift(row, "x", step)
        got = got + jnp.where(places == (x_place + RING - step) % RING, row, 0)
    return got


def mxu(left, right, left_dim=1, right_dim=0):
    return lax.dot_general(
        left, right, (((left_dim,), (right_dim,)), ((), ())), preferred_element_type=jnp.float32
    )


def params(mib):
    return pltpu.CompilerParams(dimension_semantics=("arbitrary",), vmem_limit_bytes=mib * MIB)


SMALL = pl.CostEstimate(flops=1, bytes_accessed=1, transcendentals=0)
LARGE = pl.CostEstimate(flops=10**11, bytes_accessed=10**8, transcendentals=0)


def tile(width):
    return min(1024, width)


def whole(shape):
    return pl.BlockSpec(shape, lambda i: (0,) * len(shape))


def columns(rows, width):
    return pl.BlockSpec((rows, tile(width)), lambda i: (0, i))


def joined(refs):
    blocks = [ref[...] for ref in refs]
    return blocks[0] if len(blocks) == 1 else jnp.concatenate(blocks, axis=0)


def inverse_norm(values):
    return lax.rsqrt(jnp.mean(values * values, axis=-1, keepdims=True) + EPSILON)


def embed(hidden, gain, pieces):
    def body(hidden_ref, gain_ref, *out_refs):
        values = hidden_ref[...].astype(jnp.float32)
        unit_rows = values * inverse_norm(values)
        rounded_rows = (unit_rows * gain_ref[...]).astype(jnp.bfloat16)
        for i, out_ref in enumerate(out_refs):

            @pl.when(pl.program_id(0) // per_piece == i)
            def _(out_ref=out_ref):
                out_ref[...] = rounded_rows

    rows, width = hidden.shape
    step = min(32, rows // pieces)
    per_piece = rows // pieces // step
    block = pl.BlockSpec((step, width), lambda i: (i, 0))

    def piece(at):
        return pl.BlockSpec(
            (step, width), lambda i: (jnp.clip(i - at * per_piece, 0, per_piece - 1), 0)
        )

    return pl.pallas_call(
        body,
        grid=(rows // step,),
        in_specs=[block, whole((1, width))],
        out_specs=[piece(at) for at in range(pieces)],
        out_shape=[jax.ShapeDtypeStruct((rows // pieces, width), jnp.bfloat16)] * pieces,
        compiler_params=params(12),
        cost_estimate=SMALL,
        name="embed",
    )(hidden, gain)


def finish(hidden, gain, terms, low_terms, high_terms):
    rows, width = hidden.shape
    half = rows // 2
    step = half // 2
    count, low_count = len(terms), len(low_terms)

    def body(hidden_ref, gain_ref, *refs):
        out_ref = refs[-1]
        upstream = refs[0][...].astype(jnp.float32)
        for ref in refs[1:count]:
            upstream += ref[...].astype(jnp.float32)

        def done(total):
            values = hidden_ref[...].astype(jnp.float32)
            inverse = inverse_norm(values)
            unit_rows = values * inverse
            scaled = total * gain_ref[...]
            inner = jnp.mean(scaled * unit_rows, axis=-1, keepdims=True)
            out_ref[...] = (inverse * (scaled - unit_rows * inner)).astype(jnp.bfloat16)

        def add(total, extra):
            for ref in extra:
                total += ref[...].astype(jnp.float32)
            return total

        if low_count:
            low_half = pl.program_id(0) < half // step

            @pl.when(low_half)
            def _():
                done(add(upstream, refs[count : count + low_count]))

            @pl.when(jnp.logical_not(low_half))
            def _():
                done(add(upstream, refs[count + low_count : -1]))

        else:
            done(upstream)

    block = pl.BlockSpec((step, width), lambda i: (i, 0))
    per_half = half // step
    low = pl.BlockSpec((step, width), lambda i: (jnp.minimum(i, per_half - 1), 0))
    high = pl.BlockSpec((step, width), lambda i: (jnp.maximum(i - per_half, 0), 0))
    return pl.pallas_call(
        body,
        grid=(rows // step,),
        in_specs=[block, whole((1, width))]
        + [block] * count
        + [low] * low_count
        + [high] * len(high_terms),
        out_specs=block,
        out_shape=jax.ShapeDtypeStruct((rows, width), jnp.bfloat16),
        compiler_params=params(16),
        cost_estimate=SMALL,
        name="finish",
    )(hidden, gain, *terms, *low_terms, *high_terms)


def pick_rows(matrix, sources):
    width = sources[0].shape[1]

    def body(matrix_ref, *refs):
        refs[-1][...] = mxu(matrix_ref[...], joined(refs[:-1])).astype(jnp.bfloat16)

    return pl.pallas_call(
        body,
        grid=(width // tile(width),),
        in_specs=[whole(matrix.shape)] + [columns(s.shape[0], width) for s in sources],
        out_specs=columns(matrix.shape[0], width),
        out_shape=jax.ShapeDtypeStruct((matrix.shape[0], width), jnp.bfloat16),
        compiler_params=params(16),
        cost_estimate=SMALL,
        name="pick_rows",
    )(matrix, *sources)


def line_scores(sources, queries, scale):
    width = queries.shape[1]
    steps = width // tile(width)

    def body(query_ref, *refs):
        step = pl.program_id(0)
        out_ref = refs[-1]

        @pl.when(step == 0)
        def _():
            out_ref[...] = jnp.zeros_like(out_ref)

        out_ref[...] += scale * mxu(joined(refs[:-1]), query_ref[...], 1, 1)

    out = (sum(s.shape[0] for s in sources), queries.shape[0])
    return pl.pallas_call(
        body,
        grid=(steps,),
        in_specs=[columns(queries.shape[0], width)]
        + [columns(s.shape[0], width) for s in sources],
        out_specs=whole(out),
        out_shape=jax.ShapeDtypeStruct(out, jnp.float32),
        compiler_params=params(20),
        cost_estimate=SMALL,
        name="line_scores",
    )(queries, *sources)


def far_scores(near, sources, queries, asked_by, line, scale):
    width = queries.shape[1]
    query_count = queries.shape[0]
    steps = width // tile(width)
    near_slots = near.shape[0] - line
    far_slots = asked_by.shape[0] - near_slots

    def body(near_ref, mask_ref, query_ref, *refs):
        out_ref, log_ref = refs[-2:]
        step = pl.program_id(0)

        @pl.when(step == 0)
        def _():
            out_ref[...] = jnp.zeros_like(out_ref)

        out_ref[...] += scale * mxu(joined(refs[:-2]), query_ref[...], 1, 1)

        @pl.when(step == steps - 1)
        def _():
            inner = near_ref[:line, :]
            own = jnp.where(mask_ref[:near_slots, :] > 0, near_ref[line:, :], LOW)
            far = jnp.where(mask_ref[near_slots:, :] > 0, out_ref[...], LOW)
            parts = (inner, own, far)
            top = jnp.max(inner, axis=0, keepdims=True)
            for part in parts[1:]:
                top = jnp.maximum(top, jnp.max(part, axis=0, keepdims=True))
            total = jnp.zeros_like(top)
            for part in parts:
                total += jnp.sum(jnp.exp(part - top), axis=0, keepdims=True)
            log_ref[...] = top + jnp.log(total)

    return pl.pallas_call(
        body,
        grid=(steps,),
        in_specs=[
            whole(near.shape),
            whole(asked_by.shape),
            columns(query_count, width),
        ]
        + [columns(s.shape[0], width) for s in sources],
        out_specs=[whole((far_slots, query_count)), whole((1, query_count))],
        out_shape=[
            jax.ShapeDtypeStruct((far_slots, query_count), jnp.float32),
            jax.ShapeDtypeStruct((1, query_count), jnp.float32),
        ],
        compiler_params=params(28),
        cost_estimate=LARGE,
        name="far_scores",
    )(near, asked_by, queries, *sources)


def query_side(near, far, asked_by, log_total, weight, target, queries, sources, line, scale):
    width = queries.shape[1]
    query_count = queries.shape[0]
    near_slots = near.shape[0] - line
    slot_count = asked_by.shape[0]
    count = len(sources)
    rows = line // RING
    cuts = (rows, 3 * rows)

    def body(near_ref, far_ref, mask_ref, log_ref, weight_ref, target_ref, query_ref, *refs):
        source_refs = refs[:count]
        part_ref, gain_ref, slot_ref, positive_ref = refs[count : count + 4]
        coeff_refs, turned_ref = refs[count + 4 : -1], refs[-1]

        @pl.when(pl.program_id(0) == 0)
        def _():
            log_row, weight_row = log_ref[...], weight_ref[...]
            inner = near_ref[:line, :]
            row_place = lax.broadcasted_iota(jnp.int32, inner.shape, 0)
            hit = row_place == target_ref[...]
            positive_ref[...] = jnp.sum(jnp.where(hit, inner, 0.0), axis=0, keepdims=True)
            inner_coeff = weight_row * (jnp.exp(inner - log_row) - jnp.where(hit, 1.0, 0.0))
            at = 0
            for coeff_ref, size in zip(coeff_refs, cuts):
                coeff_ref[...] = inner_coeff[at : at + size].astype(jnp.bfloat16)
                at += size
            own = jnp.where(mask_ref[:near_slots, :] > 0, near_ref[line:, :], LOW)
            slots = jnp.where(mask_ref[near_slots:, :] > 0, far_ref[...], LOW)
            own_coeff = (weight_row * jnp.exp(own - log_row)).astype(jnp.bfloat16)
            far_coeff = (weight_row * jnp.exp(slots - log_row)).astype(jnp.bfloat16)
            ones = jnp.ones((8, query_count), jnp.bfloat16)
            slot_ref[:, :near_slots] = mxu(ones, own_coeff, 1, 1)
            slot_ref[:, near_slots:] = mxu(ones, far_coeff, 1, 1)
            turned_ref[:, :line] = jnp.transpose(inner_coeff).astype(jnp.bfloat16)
            turned_ref[:, line : line + near_slots] = jnp.transpose(
                own_coeff.astype(jnp.float32)
            ).astype(jnp.bfloat16)
            turned_ref[:, line + near_slots :] = jnp.transpose(
                far_coeff.astype(jnp.float32)
            ).astype(jnp.bfloat16)

        total = scale * mxu(turned_ref[...], joined(source_refs))
        part_ref[...] = total.astype(jnp.bfloat16)
        gain_ref[...] = jnp.sum(total * query_ref[...].astype(jnp.float32), axis=0, keepdims=True)

    row = whole((1, query_count))
    return pl.pallas_call(
        body,
        grid=(width // tile(width),),
        in_specs=[
            whole(near.shape),
            whole(far.shape),
            whole(asked_by.shape),
            row,
            row,
            row,
            columns(query_count, width),
        ]
        + [columns(s.shape[0], width) for s in sources],
        out_specs=[
            columns(query_count, width),
            columns(1, width),
            whole((8, slot_count)),
            row,
        ]
        + [whole((size, query_count)) for size in cuts],
        out_shape=[
            jax.ShapeDtypeStruct((query_count, width), jnp.bfloat16),
            jax.ShapeDtypeStruct((1, width), jnp.float32),
            jax.ShapeDtypeStruct((8, slot_count), jnp.float32),
            jax.ShapeDtypeStruct((1, query_count), jnp.float32),
        ]
        + [jax.ShapeDtypeStruct((size, query_count), jnp.bfloat16) for size in cuts],
        scratch_shapes=[pltpu.VMEM((query_count, line + slot_count), jnp.bfloat16)],
        compiler_params=params(32),
        cost_estimate=SMALL,
        name="query_side",
    )(near, far, asked_by, log_total, weight, target, queries, *sources)


def passage_side(coeff, queries, put, arrived, scale, out_type, pieces):
    width = queries.shape[1]
    rows = coeff.shape[0] // pieces

    def body(coeff_ref, query_ref, put_ref, arrived_ref, *out_refs):
        total = mxu(coeff_ref[...], query_ref[...]) + mxu(put_ref[...], arrived_ref[...])
        total = scale * total
        for i, out_ref in enumerate(out_refs):
            out_ref[...] = total[i * rows : (i + 1) * rows].astype(out_type)

    return pl.pallas_call(
        body,
        grid=(width // tile(width),),
        in_specs=[
            whole(coeff.shape),
            columns(queries.shape[0], width),
            whole(put.shape),
            columns(arrived.shape[0], width),
        ],
        out_specs=[columns(rows, width)] * pieces,
        out_shape=[jax.ShapeDtypeStruct((rows, width), out_type)] * pieces,
        compiler_params=params(20),
        cost_estimate=LARGE if pieces > 1 else SMALL,
        name="passage_side",
    )(coeff, queries, put, arrived)


def on_device(query_hidden, passage_hidden, norm_gain, query_weight, hneg_ids):
    rows, width = query_hidden.shape
    neg_count = hneg_ids.shape[1]
    z_count = lax.axis_size("z")
    group_count = 2 * z_count
    line = RING * rows
    scale = 1.0 / (SOFTMAX_TEMPER * math.sqrt(width))
    y_place, x_place = lax.axis_index("y"), lax.axis_index("x")

    gain = norm_gain.reshape(1, width)
    p_own = embed(passage_hidden, gain, 2)
    p_mid, p_opp = ring_gather(*p_own, "y")

    flat_ids = hneg_ids.reshape(-1)
    id_count = rows * neg_count
    owners = flat_ids // rows
    local_row = flat_ids % rows
    number = jnp.arange(id_count, dtype=jnp.int32)
    same = (owners[:, None] == owners[None, :]) & (number[None, :] < number[:, None])
    rank = jnp.sum(same.astype(jnp.int32), axis=1)
    y_step = (owners // RING - y_place) % RING
    line_of = (owners // (RING * RING)) * RING + owners % RING
    slot = (line_of * RING + y_step) * CAP + rank
    slot_count = group_count * RING * RING * CAP
    hit = slot[None, :] == jnp.arange(slot_count, dtype=jnp.int32)[:, None]
    slot_row = jnp.sum(jnp.where(hit, local_row[None, :] + 1, 0), axis=1) - 1
    slot_query = jnp.sum(jnp.where(hit, number[None, :] // neg_count + 1, 0), axis=1)
    asked = lax.all_to_all(
        slot_row.reshape(group_count * RING, RING * CAP), ("z", "c", "x"), 0, 0, tiled=True
    )
    asked = asked.reshape(group_count, RING, RING, CAP).transpose(0, 2, 1, 3)
    place = jnp.arange(line, dtype=jnp.int32)
    asked, _ = lax.optimization_barrier((asked, p_mid))
    asked_own = asked[:, 0].reshape(-1)
    above = jnp.where(asked[:, 3:] < 0, -1, asked[:, 3:] + rows)
    opposite = jnp.where(asked[:, 2:3] < 0, -1, asked[:, 2:3] + 2 * rows)
    asked_far = jnp.concatenate([asked[:, 1:2], above, opposite], axis=1).reshape(-1)

    def one_hot(numbers, size):
        return (numbers[:, None] == place[None, :size]).astype(jnp.bfloat16)

    chosen_own = pick_rows(one_hot(asked_own, rows), p_own)
    hard_own = group_rows(chosen_own, group_count)
    chosen_far = pick_rows(one_hot(asked_far, 3 * rows), [*p_mid, *p_opp])
    hard_far = group_rows(chosen_far, group_count)

    q_emb = embed(query_hidden, gain, 1)[0]
    q_line = lax.all_gather(q_emb, "x", axis=0, tiled=True)

    by_x = slot_query.reshape(group_count, RING, RING * CAP).transpose(1, 0, 2)
    asker = line_table(by_x.reshape(RING, -1)).reshape(RING, group_count, RING, CAP)
    x_base = rows * jnp.arange(RING, dtype=jnp.int32)
    asker = jnp.where(asker == 0, -1, asker - 1 + x_base[:, None, None, None])
    asker = asker.transpose(1, 2, 0, 3)
    far_asker = jnp.concatenate([asker[:, 1:2], asker[:, 3:], asker[:, 2:3]], axis=1)
    send_own = one_hot(asker[:, 0].reshape(-1), line)
    send_far = one_hot(far_asker.reshape(-1), line)
    asked_by = jnp.concatenate([send_own, send_far], axis=0)
    leave_far = pick_rows(send_far, [q_line])
    leave_own = pick_rows(send_own, [q_line])
    q_line, leave_far, leave_own = lax.optimization_barrier((q_line, leave_far, leave_own))
    far_queries = group_rows(leave_far, group_count)
    own_queries = group_rows(leave_own, group_count)

    near = line_scores([*p_own, *p_mid, *p_opp, hard_own], q_line, scale)
    far, part_log = far_scores(near, [hard_far], q_line, asked_by, line, scale)
    part_log = part_log.reshape(RING, rows)
    own_place = jnp.arange(RING, dtype=jnp.int32)[:, None] == x_place
    own_weight = jnp.where(own_place, query_weight[None, :], 0.0)
    message = jnp.concatenate([part_log, own_weight], axis=0)
    messages = [message] + [shift(message, "x", step) for step in (1, 3, 2)]
    logs = [m[:RING] for m in messages]
    weight = sum(m[RING:] for m in messages).reshape(1, line)
    top = jnp.maximum(jnp.maximum(logs[0], logs[1]), jnp.maximum(logs[2], logs[3]))
    log_total = (top + jnp.log(sum(jnp.exp(part - top) for part in logs))).reshape(1, line)
    first_row = x_place * rows
    target = place[None, :] - first_row
    target = jnp.where((target >= 0) & (target < rows), target, -1)

    part, gain_part, slot_coeff, positive, coeff_own, coeff_far = query_side(
        near, far, asked_by, log_total, weight, target, q_line,
        [*p_own, *p_mid, *p_opp, hard_own, hard_far], line, scale,
    )
    loss_rows = lax.dynamic_slice(log_total - positive, (0, first_row), (1, rows)).reshape(-1)
    query_up = lax.psum_scatter(part, "x", scatter_dimension=0, tiled=True)
    query_grad = finish(query_hidden, gain, [query_up], [], [])

    own_end = group_count * RING * CAP
    pieces = (
        slot_coeff[0, :own_end].reshape(group_count, -1),
        slot_coeff[0, own_end:].reshape(group_count, -1),
    )
    got_coeff = group_table(jnp.concatenate(pieces, axis=1), group_count)
    first = RING * CAP

    def put_rows(numbers, values, size):
        return jnp.where(
            place[:size, None] == numbers[None, :], values.reshape(-1)[None, :], 0.0
        ).astype(jnp.bfloat16)

    put_own = put_rows(asked_own, got_coeff[:, :first], rows)
    put_far = put_rows(asked_far, got_coeff[:, first:], 3 * rows)
    far_part = passage_side(coeff_far, q_line, put_far, far_queries, scale, jnp.bfloat16, 6)
    low_terms, high_terms, passed = ring_scatter(far_part[4:], far_part[:4], "y")
    gain_part, _ = lax.optimization_barrier((gain_part, passed))
    gain_grad = all_sum(gain_part.reshape(-1, 128), z_count).reshape(-1)
    gain_grad = 2.0 * gain_grad / norm_gain

    own_part = passage_side(coeff_own, q_line, put_own, own_queries, scale, jnp.float32, 1)[0]
    own_part, query_grad = lax.optimization_barrier((own_part, query_grad))
    passage_grad = finish(passage_hidden, gain, [own_part], low_terms, high_terms)
    return (loss_rows, query_grad, passage_grad, gain_grad)


def solution(mesh):
    torus = Mesh(mesh.devices.reshape(-1, 2, RING, RING), ALL_AXES)
    return jax.shard_map(
        on_device,
        mesh=torus,
        in_specs=(
            P(ALL_AXES, None),
            P(ALL_AXES, None),
            P(),
            P(ALL_AXES),
            P(ALL_AXES, None),
        ),
        out_specs=(
            P(ALL_AXES),
            P(ALL_AXES, None),
            P(ALL_AXES, None),
            P(),
        ),
        check_vma=False,
    )
```

```python
import math

import jax
import jax.numpy as jnp
from jax import lax
from jax.experimental import pallas as pl
from jax.experimental.pallas import tpu as pltpu
from jax.sharding import Mesh, PartitionSpec as P

EPSILON = 1e-06
SOFTMAX_TEMPER = 0.28
RING = 4
CAP = 4
GROUPS = ("z", "c")
ALL_AXES = ("z", "c", "y", "x")
MIB = 1024 * 1024
LOW = -1e30


def shift(value, axis, step):
    return lax.ppermute(value, axis, [(i, (i + step) % RING) for i in range(RING)])


def axes_sum(value, axes):
    for axis in axes:
        size = lax.axis_size(axis)
        value = value + lax.ppermute(value, axis, [(i, i ^ 1) for i in range(size)])
        if size > 2:
            value = value + lax.ppermute(value, axis, [(i, size - 1 - i) for i in range(size)])
    return value


def group_rows(rows, group_count):
    blocks = rows.reshape(group_count, rows.shape[0] // group_count, rows.shape[1])
    return lax.all_to_all(blocks, GROUPS, 0, 0, tiled=True).reshape(rows.shape)


def group_table(table, group_count):
    z_count = group_count // 2
    z_place, c_place = lax.axis_index("z"), lax.axis_index("c")
    got = jnp.zeros_like(table)
    places = jnp.arange(group_count, dtype=jnp.int32)[:, None]
    for z_step in range(z_count):
        for c_step in range(2):
            to_group = ((z_place + z_step) % z_count) * 2 + (c_place ^ c_step)
            from_group = ((z_place + z_count - z_step) % z_count) * 2 + (c_place ^ c_step)
            row = jnp.sum(jnp.where(places == to_group, table, 0), axis=0, keepdims=True)
            if z_step or c_step:
                row = lax.ppermute(
                    row,
                    GROUPS,
                    [
                        (z * 2 + c, ((z + z_step) % z_count) * 2 + (c ^ c_step))
                        for z in range(z_count)
                        for c in range(2)
                    ],
                )
            got = got + jnp.where(places == from_group, row, 0)
    return got


def line_table(table):
    x_place = lax.axis_index("x")
    places = jnp.arange(RING, dtype=jnp.int32)[:, None]
    got = jnp.where(places == x_place, table, 0)
    for step in range(1, RING):
        chosen = places == (x_place + step) % RING
        row = jnp.sum(jnp.where(chosen, table, 0), axis=0, keepdims=True)
        row = shift(row, "x", step)
        got = got + jnp.where(places == (x_place + RING - step) % RING, row, 0)
    return got


def mxu(left, right, left_dim=1, right_dim=0):
    return lax.dot_general(
        left, right, (((left_dim,), (right_dim,)), ((), ())), preferred_element_type=jnp.float32
    )


def params(mib):
    return pltpu.CompilerParams(dimension_semantics=("arbitrary",), vmem_limit_bytes=mib * MIB)


SMALL = pl.CostEstimate(flops=1, bytes_accessed=1, transcendentals=0)
LARGE = pl.CostEstimate(flops=10**11, bytes_accessed=10**8, transcendentals=0)


def tile(width):
    return min(1024, width)


def whole(shape):
    return pl.BlockSpec(shape, lambda i: (0,) * len(shape))


def columns(rows, width):
    return pl.BlockSpec((rows, tile(width)), lambda i: (0, i))


def joined(refs):
    blocks = [ref[...] for ref in refs]
    return blocks[0] if len(blocks) == 1 else jnp.concatenate(blocks, axis=0)


def inverse_norm(values):
    return lax.rsqrt(jnp.mean(values * values, axis=-1, keepdims=True) + EPSILON)


def embed(hidden, gain):
    def body(hidden_ref, gain_ref, out_ref):
        values = hidden_ref[...].astype(jnp.float32)
        unit_rows = values * inverse_norm(values)
        out_ref[...] = (unit_rows * gain_ref[...]).astype(jnp.bfloat16)

    rows, width = hidden.shape
    step = rows // 4
    block = pl.BlockSpec((step, width), lambda i: (i, 0))
    return pl.pallas_call(
        body,
        grid=(rows // step,),
        in_specs=[block, whole((1, width))],
        out_specs=block,
        out_shape=jax.ShapeDtypeStruct((rows, width), jnp.bfloat16),
        compiler_params=params(12),
        cost_estimate=SMALL,
        name="embed",
    )(hidden, gain)


def finish(hidden, gain, terms):
    rows, width = hidden.shape
    step = rows // 4

    def body(hidden_ref, gain_ref, *refs):
        total = refs[0][...].astype(jnp.float32)
        for ref in refs[1:-1]:
            total += ref[...].astype(jnp.float32)
        values = hidden_ref[...].astype(jnp.float32)
        inverse = inverse_norm(values)
        unit_rows = values * inverse
        scaled = total * gain_ref[...]
        inner = jnp.mean(scaled * unit_rows, axis=-1, keepdims=True)
        refs[-1][...] = (inverse * (scaled - unit_rows * inner)).astype(jnp.bfloat16)

    block = pl.BlockSpec((step, width), lambda i: (i, 0))
    return pl.pallas_call(
        body,
        grid=(rows // step,),
        in_specs=[block, whole((1, width))] + [block] * len(terms),
        out_specs=block,
        out_shape=jax.ShapeDtypeStruct((rows, width), jnp.bfloat16),
        compiler_params=params(16),
        cost_estimate=SMALL,
        name="finish",
    )(hidden, gain, *terms)


def pick_rows(matrix, sources, cost=SMALL):
    width = sources[0].shape[1]

    def body(matrix_ref, *refs):
        refs[-1][...] = mxu(matrix_ref[...], joined(refs[:-1])).astype(jnp.bfloat16)

    return pl.pallas_call(
        body,
        grid=(width // tile(width),),
        in_specs=[whole(matrix.shape)] + [columns(s.shape[0], width) for s in sources],
        out_specs=columns(matrix.shape[0], width),
        out_shape=jax.ShapeDtypeStruct((matrix.shape[0], width), jnp.bfloat16),
        compiler_params=params(16),
        cost_estimate=cost,
        name="pick_rows",
    )(matrix, *sources)


def pick_into(matrix, sources, shape, at, held=None):
    width = sources[0].shape[1]
    groups = shape[0]
    size = matrix.shape[0] // groups

    def body(matrix_ref, *refs):
        picked = mxu(matrix_ref[...], joined(refs[: len(sources)])).astype(jnp.bfloat16)
        refs[-1][...] = picked.reshape(groups, size, picked.shape[1])

    place = pl.BlockSpec((groups, size, tile(width)), lambda i: (0, at // size, i))
    more = () if held is None else (held,)
    return pl.pallas_call(
        body,
        grid=(width // tile(width),),
        in_specs=[whole(matrix.shape)]
        + [columns(s.shape[0], width) for s in sources]
        + [pl.BlockSpec(memory_space=pl.ANY)] * len(more),
        out_specs=place,
        out_shape=jax.ShapeDtypeStruct(shape, jnp.bfloat16),
        input_output_aliases={1 + len(sources): 0} if more else {},
        compiler_params=params(16),
        cost_estimate=SMALL,
        name="pick_into",
    )(matrix, *sources, *more)


def line_scores(sources, queries, scale):
    width = queries.shape[1]
    steps = width // tile(width)

    def body(query_ref, *refs):
        step = pl.program_id(0)
        out_ref = refs[-1]

        @pl.when(step == 0)
        def _():
            out_ref[...] = jnp.zeros_like(out_ref)

        out_ref[...] += scale * mxu(joined(refs[:-1]), query_ref[...], 1, 1)

    out = (sum(s.shape[0] for s in sources), queries.shape[0])
    return pl.pallas_call(
        body,
        grid=(steps,),
        in_specs=[columns(queries.shape[0], width)]
        + [columns(s.shape[0], width) for s in sources],
        out_specs=whole(out),
        out_shape=jax.ShapeDtypeStruct(out, jnp.float32),
        compiler_params=params(20),
        cost_estimate=SMALL,
        name="line_scores",
    )(queries, *sources)


def far_scores(near, sources, queries, asked_by, line, scale):
    width = queries.shape[1]
    query_count = queries.shape[0]
    steps = width // tile(width)
    near_slots = near.shape[0] - line
    far_slots = asked_by.shape[0] - near_slots

    def body(near_ref, mask_ref, query_ref, *refs):
        out_ref, log_ref = refs[-2:]
        step = pl.program_id(0)

        @pl.when(step == 0)
        def _():
            out_ref[...] = jnp.zeros_like(out_ref)

        out_ref[...] += scale * mxu(joined(refs[:-2]), query_ref[...], 1, 1)

        @pl.when(step == steps - 1)
        def _():
            inner = near_ref[:line, :]
            own = jnp.where(mask_ref[:near_slots, :] > 0, near_ref[line:, :], LOW)
            far = jnp.where(mask_ref[near_slots:, :] > 0, out_ref[...], LOW)
            parts = (inner, own, far)
            top = jnp.max(inner, axis=0, keepdims=True)
            for part in parts[1:]:
                top = jnp.maximum(top, jnp.max(part, axis=0, keepdims=True))
            total = jnp.zeros_like(top)
            for part in parts:
                total += jnp.sum(jnp.exp(part - top), axis=0, keepdims=True)
            log_ref[...] = top + jnp.log(total)

    return pl.pallas_call(
        body,
        grid=(steps,),
        in_specs=[
            whole(near.shape),
            whole(asked_by.shape),
            columns(query_count, width),
        ]
        + [columns(s.shape[0], width) for s in sources],
        out_specs=[whole((far_slots, query_count)), whole((1, query_count))],
        out_shape=[
            jax.ShapeDtypeStruct((far_slots, query_count), jnp.float32),
            jax.ShapeDtypeStruct((1, query_count), jnp.float32),
        ],
        compiler_params=params(28),
        cost_estimate=LARGE,
        name="far_scores",
    )(near, asked_by, queries, *sources)


def query_side(near, far, asked_by, log_total, weight, target, queries, sources, line, scale):
    width = queries.shape[1]
    query_count = queries.shape[0]
    near_slots = near.shape[0] - line
    slot_count = asked_by.shape[0]
    count = len(sources)
    rows = line // RING
    cuts = (rows, 3 * rows)

    def body(near_ref, far_ref, mask_ref, log_ref, weight_ref, target_ref, query_ref, *refs):
        source_refs = refs[:count]
        part_ref, gain_ref, slot_ref, positive_ref = refs[count : count + 4]
        coeff_refs, turned_ref = refs[count + 4 : -1], refs[-1]

        @pl.when(pl.program_id(0) == 0)
        def _():
            log_row, weight_row = log_ref[...], weight_ref[...]
            inner = near_ref[:line, :]
            row_place = lax.broadcasted_iota(jnp.int32, inner.shape, 0)
            hit = row_place == target_ref[...]
            positive_ref[...] = jnp.sum(jnp.where(hit, inner, 0.0), axis=0, keepdims=True)
            inner_coeff = weight_row * (jnp.exp(inner - log_row) - jnp.where(hit, 1.0, 0.0))
            at = 0
            for coeff_ref, size in zip(coeff_refs, cuts):
                coeff_ref[...] = inner_coeff[at : at + size].astype(jnp.bfloat16)
                at += size
            own = jnp.where(mask_ref[:near_slots, :] > 0, near_ref[line:, :], LOW)
            slots = jnp.where(mask_ref[near_slots:, :] > 0, far_ref[...], LOW)
            own_coeff = (weight_row * jnp.exp(own - log_row)).astype(jnp.bfloat16)
            far_coeff = (weight_row * jnp.exp(slots - log_row)).astype(jnp.bfloat16)
            ones = jnp.ones((8, query_count), jnp.bfloat16)
            slot_ref[:, :near_slots] = mxu(ones, own_coeff, 1, 1)
            slot_ref[:, near_slots:] = mxu(ones, far_coeff, 1, 1)
            turned_ref[:, :line] = jnp.transpose(inner_coeff).astype(jnp.bfloat16)
            turned_ref[:, line : line + near_slots] = jnp.transpose(
                own_coeff.astype(jnp.float32)
            ).astype(jnp.bfloat16)
            turned_ref[:, line + near_slots :] = jnp.transpose(
                far_coeff.astype(jnp.float32)
            ).astype(jnp.bfloat16)

        total = scale * mxu(turned_ref[...], joined(source_refs))
        part_ref[...] = total.astype(jnp.bfloat16)
        gain_ref[...] = jnp.sum(total * query_ref[...].astype(jnp.float32), axis=0, keepdims=True)

    row = whole((1, query_count))
    return pl.pallas_call(
        body,
        grid=(width // tile(width),),
        in_specs=[
            whole(near.shape),
            whole(far.shape),
            whole(asked_by.shape),
            row,
            row,
            row,
            columns(query_count, width),
        ]
        + [columns(s.shape[0], width) for s in sources],
        out_specs=[
            columns(query_count, width),
            columns(1, width),
            whole((8, slot_count)),
            row,
        ]
        + [whole((size, query_count)) for size in cuts],
        out_shape=[
            jax.ShapeDtypeStruct((query_count, width), jnp.bfloat16),
            jax.ShapeDtypeStruct((1, width), jnp.float32),
            jax.ShapeDtypeStruct((8, slot_count), jnp.float32),
            jax.ShapeDtypeStruct((1, query_count), jnp.float32),
        ]
        + [jax.ShapeDtypeStruct((size, query_count), jnp.bfloat16) for size in cuts],
        scratch_shapes=[pltpu.VMEM((query_count, line + slot_count), jnp.bfloat16)],
        compiler_params=params(32),
        cost_estimate=SMALL,
        name="query_side",
    )(near, far, asked_by, log_total, weight, target, queries, *sources)


def passage_side(coeff, queries, put, arrived, scale, out_type, pieces):
    width = queries.shape[1]
    rows = coeff.shape[0] // pieces

    def body(coeff_ref, query_ref, put_ref, arrived_ref, *out_refs):
        total = mxu(coeff_ref[...], query_ref[...]) + mxu(put_ref[...], arrived_ref[...])
        total = scale * total
        for i, out_ref in enumerate(out_refs):
            out_ref[...] = total[i * rows : (i + 1) * rows].astype(out_type)

    return pl.pallas_call(
        body,
        grid=(width // tile(width),),
        in_specs=[
            whole(coeff.shape),
            columns(queries.shape[0], width),
            whole(put.shape),
            columns(arrived.shape[0], width),
        ],
        out_specs=[columns(rows, width)] * pieces,
        out_shape=[jax.ShapeDtypeStruct((rows, width), out_type)] * pieces,
        compiler_params=params(20),
        cost_estimate=LARGE if pieces > 1 else SMALL,
        name="passage_side",
    )(coeff, queries, put, arrived)


def on_device(query_hidden, passage_hidden, norm_gain, query_weight, hneg_ids):
    rows, width = query_hidden.shape
    neg_count = hneg_ids.shape[1]
    z_count = lax.axis_size("z")
    group_count = 2 * z_count
    line = RING * rows
    scale = 1.0 / (SOFTMAX_TEMPER * math.sqrt(width))
    y_place, x_place = lax.axis_index("y"), lax.axis_index("x")

    gain = norm_gain.reshape(1, width)
    p_own = embed(passage_hidden, gain)
    p_mid = [shift(p_own, "y", -1), shift(p_own, "y", 1)]
    p_opp = shift(p_own, "y", 2)

    flat_ids = hneg_ids.reshape(-1)
    id_count = rows * neg_count
    owners = flat_ids // rows
    local_row = flat_ids % rows
    number = jnp.arange(id_count, dtype=jnp.int32)
    same = (owners[:, None] == owners[None, :]) & (number[None, :] < number[:, None])
    rank = jnp.sum(same.astype(jnp.int32), axis=1)
    y_step = (owners // RING - y_place) % RING
    line_of = (owners // (RING * RING)) * RING + owners % RING
    slot = (line_of * RING + y_step) * CAP + rank
    slot_count = group_count * RING * RING * CAP
    hit = slot[None, :] == jnp.arange(slot_count, dtype=jnp.int32)[:, None]
    slot_row = jnp.sum(jnp.where(hit, local_row[None, :] + 1, 0), axis=1) - 1
    slot_query = jnp.sum(jnp.where(hit, number[None, :] // neg_count + 1, 0), axis=1)
    asked = lax.all_to_all(
        slot_row.reshape(group_count * RING, RING * CAP), ("z", "c", "x"), 0, 0, tiled=True
    )
    asked = asked.reshape(group_count, RING, RING, CAP).transpose(0, 2, 1, 3)
    place = jnp.arange(line, dtype=jnp.int32)
    asked, _ = lax.optimization_barrier((asked, p_mid[0]))
    asked_own = asked[:, 0].reshape(-1)
    above = jnp.where(asked[:, 3:] < 0, -1, asked[:, 3:] + rows)
    asked_mid = jnp.concatenate([asked[:, 1:2], above], axis=1)
    opposite = jnp.where(asked[:, 2:3] < 0, -1, asked[:, 2:3] + 2 * rows)
    asked_far = jnp.concatenate([asked_mid, opposite], axis=1).reshape(-1)

    def one_hot(numbers, size):
        return (numbers[:, None] == place[None, :size]).astype(jnp.bfloat16)

    hard_own = group_rows(pick_rows(one_hot(asked_own, rows), [p_own]), group_count)
    per_owner = RING * CAP
    shape = (group_count, 3 * per_owner, width)
    chosen = pick_into(one_hot(asked_mid.reshape(-1), 2 * rows), p_mid, shape, 0)
    chosen = pick_into(
        one_hot(asked[:, 2].reshape(-1), rows), [p_opp], shape, 2 * per_owner, chosen
    )
    hard_far = group_rows(chosen.reshape(-1, width), group_count)

    q_emb = embed(query_hidden, gain)
    q_line = lax.all_gather(q_emb, "x", axis=0, tiled=True)

    by_x = slot_query.reshape(group_count, RING, RING * CAP).transpose(1, 0, 2)
    asker = line_table(by_x.reshape(RING, -1)).reshape(RING, group_count, RING, CAP)
    x_base = rows * jnp.arange(RING, dtype=jnp.int32)
    asker = jnp.where(asker == 0, -1, asker - 1 + x_base[:, None, None, None])
    asker = asker.transpose(1, 2, 0, 3)
    far_asker = jnp.concatenate([asker[:, 1:2], asker[:, 3:], asker[:, 2:3]], axis=1)
    send_own = one_hot(asker[:, 0].reshape(-1), line)
    send_far = one_hot(far_asker.reshape(-1), line)
    asked_by = jnp.concatenate([send_own, send_far], axis=0)
    leave_far = pick_rows(send_far, [q_line])
    leave_own = pick_rows(send_own, [q_line])
    q_line, leave_far, leave_own = lax.optimization_barrier((q_line, leave_far, leave_own))
    far_queries = group_rows(leave_far, group_count)
    own_queries = group_rows(leave_own, group_count)

    near = line_scores([p_own, *p_mid, p_opp, hard_own], q_line, scale)
    far, part_log = far_scores(near, [hard_far], q_line, asked_by, line, scale)
    part_log = part_log.reshape(RING, rows)
    own_place = jnp.arange(RING, dtype=jnp.int32)[:, None] == x_place
    own_weight = jnp.where(own_place, query_weight[None, :], 0.0)
    message = jnp.concatenate([part_log, own_weight], axis=0)
    messages = [message] + [shift(message, "x", step) for step in (1, 3, 2)]
    logs = [m[:RING] for m in messages]
    weight = sum(m[RING:] for m in messages).reshape(1, line)
    top = jnp.maximum(jnp.maximum(logs[0], logs[1]), jnp.maximum(logs[2], logs[3]))
    log_total = (top + jnp.log(sum(jnp.exp(part - top) for part in logs))).reshape(1, line)
    first_row = x_place * rows
    target = place[None, :] - first_row
    target = jnp.where((target >= 0) & (target < rows), target, -1)

    part, gain_part, slot_coeff, positive, coeff_own, coeff_far = query_side(
        near, far, asked_by, log_total, weight, target, q_line,
        [p_own, *p_mid, p_opp, hard_own, hard_far], line, scale,
    )
    loss_rows = lax.dynamic_slice(log_total - positive, (0, first_row), (1, rows)).reshape(-1)
    query_up = lax.psum_scatter(part, "x", scatter_dimension=0, tiled=True)
    query_grad = finish(query_hidden, gain, [query_up])

    own_end = group_count * RING * CAP
    pieces = (
        slot_coeff[0, :own_end].reshape(group_count, -1),
        slot_coeff[0, own_end:].reshape(group_count, -1),
    )
    got_coeff = group_table(jnp.concatenate(pieces, axis=1), group_count)
    first = RING * CAP

    def put_rows(numbers, values, size):
        return jnp.where(
            place[:size, None] == numbers[None, :], values.reshape(-1)[None, :], 0.0
        ).astype(jnp.bfloat16)

    put_own = put_rows(asked_own, got_coeff[:, :first], rows)
    put_far = put_rows(asked_far, got_coeff[:, first:], 3 * rows)
    above, below, far = passage_side(
        coeff_far, q_line, put_far, far_queries, scale, jnp.bfloat16, 3
    )
    arrived = [shift(above, "y", 1), shift(below, "y", -1), shift(far, "y", 2)]
    gain_part, own_queries = lax.optimization_barrier((gain_part, own_queries))
    gain_part = axes_sum(gain_part.reshape(-1, 128), ("c", "x", "z", "y"))
    gain_grad = 2.0 * gain_part.reshape(-1) / norm_gain

    own_part = passage_side(coeff_own, q_line, put_own, own_queries, scale, jnp.float32, 1)[0]
    own_part, query_grad = lax.optimization_barrier((own_part, query_grad))
    passage_grad = finish(passage_hidden, gain, [own_part, *arrived])
    return (loss_rows, query_grad, passage_grad, gain_grad)


def solution(mesh):
    torus = Mesh(mesh.devices.reshape(-1, 2, RING, RING), ALL_AXES)
    return jax.shard_map(
        on_device,
        mesh=torus,
        in_specs=(
            P(ALL_AXES, None),
            P(ALL_AXES, None),
            P(),
            P(ALL_AXES),
            P(ALL_AXES, None),
        ),
        out_specs=(
            P(ALL_AXES),
            P(ALL_AXES, None),
            P(ALL_AXES, None),
            P(),
        ),
        check_vma=False,
    )
```

```python
import math

import jax
import jax.numpy as jnp
from jax import lax
from jax.experimental import pallas as pl
from jax.experimental.pallas import tpu as pltpu
from jax.sharding import Mesh, PartitionSpec as P

EPSILON = 1e-06
SOFTMAX_TEMPER = 0.28
RING = 4
CAP = 4
GROUPS = ("z", "c")
ALL_AXES = ("z", "c", "y", "x")
MIB = 1024 * 1024
LOW = -1e30


def shift(value, axis, step):
    return lax.ppermute(value, axis, [(i, (i + step) % RING) for i in range(RING)])


def ring_pieces(block, axis):
    half = block.shape[0] // 2
    low, high = block[:half], block[half:]
    up_low = shift(low, axis, -1)
    down_high = shift(high, axis, 1)
    up_high = shift(high, axis, -1)
    down_low = shift(low, axis, 1)
    far_low = shift(up_low, axis, -1)
    far_high = shift(down_high, axis, 1)
    return [low, high, up_low, up_high, down_low, down_high, far_low, far_high]


def ring_scatter(blocks, axis):
    low_1, high_1, low_3, high_3, low_2, high_2 = blocks
    passing_low = shift(low_2, axis, 1)
    passing_high = shift(high_2, axis, -1)
    from_below_high = shift(high_1, axis, 1)
    from_above_low = shift(low_3, axis, -1)
    wide = jnp.float32
    both_low = (low_1.astype(wide) + passing_low.astype(wide)).astype(jnp.bfloat16)
    both_high = (high_3.astype(wide) + passing_high.astype(wide)).astype(jnp.bfloat16)
    from_below_low = shift(both_low, axis, 1)
    from_above_high = shift(both_high, axis, -1)
    return [from_below_low, from_above_low], [from_below_high, from_above_high], both_high


def axes_sum(value, axes):
    for axis in axes:
        size = lax.axis_size(axis)
        value = value + lax.ppermute(value, axis, [(i, i ^ 1) for i in range(size)])
        if size > 2:
            value = value + lax.ppermute(value, axis, [(i, size - 1 - i) for i in range(size)])
    return value


def group_rows(rows, group_count):
    blocks = rows.reshape(group_count, rows.shape[0] // group_count, rows.shape[1])
    return lax.all_to_all(blocks, GROUPS, 0, 0, tiled=True).reshape(rows.shape)


def group_table(table, group_count):
    z_count = group_count // 2
    z_place, c_place = lax.axis_index("z"), lax.axis_index("c")
    got = jnp.zeros_like(table)
    places = jnp.arange(group_count, dtype=jnp.int32)[:, None]
    for z_step in range(z_count):
        for c_step in range(2):
            to_group = ((z_place + z_step) % z_count) * 2 + (c_place ^ c_step)
            from_group = ((z_place + z_count - z_step) % z_count) * 2 + (c_place ^ c_step)
            row = jnp.sum(jnp.where(places == to_group, table, 0), axis=0, keepdims=True)
            if z_step or c_step:
                row = lax.ppermute(
                    row,
                    GROUPS,
                    [
                        (z * 2 + c, ((z + z_step) % z_count) * 2 + (c ^ c_step))
                        for z in range(z_count)
                        for c in range(2)
                    ],
                )
            got = got + jnp.where(places == from_group, row, 0)
    return got


def line_table(table):
    x_place = lax.axis_index("x")
    places = jnp.arange(RING, dtype=jnp.int32)[:, None]
    got = jnp.where(places == x_place, table, 0)
    for step in range(1, RING):
        chosen = places == (x_place + step) % RING
        row = jnp.sum(jnp.where(chosen, table, 0), axis=0, keepdims=True)
        row = shift(row, "x", step)
        got = got + jnp.where(places == (x_place + RING - step) % RING, row, 0)
    return got


def mxu(left, right, left_dim=1, right_dim=0):
    return lax.dot_general(
        left, right, (((left_dim,), (right_dim,)), ((), ())), preferred_element_type=jnp.float32
    )


def params(mib):
    return pltpu.CompilerParams(dimension_semantics=("arbitrary",), vmem_limit_bytes=mib * MIB)


SMALL = pl.CostEstimate(flops=1, bytes_accessed=1, transcendentals=0)
LARGE = pl.CostEstimate(flops=10**11, bytes_accessed=10**8, transcendentals=0)


def tile(width):
    return min(1024, width)


def whole(shape):
    return pl.BlockSpec(shape, lambda i: (0,) * len(shape))


def columns(rows, width):
    return pl.BlockSpec((rows, tile(width)), lambda i: (0, i))


def joined(refs):
    blocks = [ref[...] for ref in refs]
    return blocks[0] if len(blocks) == 1 else jnp.concatenate(blocks, axis=0)


def inverse_norm(values):
    return lax.rsqrt(jnp.mean(values * values, axis=-1, keepdims=True) + EPSILON)


def embed(hidden, gain):
    def body(hidden_ref, gain_ref, out_ref):
        values = hidden_ref[...].astype(jnp.float32)
        unit_rows = values * inverse_norm(values)
        out_ref[...] = (unit_rows * gain_ref[...]).astype(jnp.bfloat16)

    rows, width = hidden.shape
    step = rows // 4
    block = pl.BlockSpec((step, width), lambda i: (i, 0))
    return pl.pallas_call(
        body,
        grid=(rows // step,),
        in_specs=[block, whole((1, width))],
        out_specs=block,
        out_shape=jax.ShapeDtypeStruct((rows, width), jnp.bfloat16),
        compiler_params=params(12),
        cost_estimate=SMALL,
        name="embed",
    )(hidden, gain)


def finish(hidden, gain, terms, low_terms, high_terms):
    rows, width = hidden.shape
    half = rows // 2
    step = half // 2
    count, low_count = len(terms), len(low_terms)

    def body(hidden_ref, gain_ref, *refs):
        out_ref = refs[-1]
        upstream = refs[0][...].astype(jnp.float32)
        for ref in refs[1:count]:
            upstream += ref[...].astype(jnp.float32)

        def done(total):
            values = hidden_ref[...].astype(jnp.float32)
            inverse = inverse_norm(values)
            unit_rows = values * inverse
            scaled = total * gain_ref[...]
            inner = jnp.mean(scaled * unit_rows, axis=-1, keepdims=True)
            out_ref[...] = (inverse * (scaled - unit_rows * inner)).astype(jnp.bfloat16)

        def add(total, extra):
            for ref in extra:
                total += ref[...].astype(jnp.float32)
            return total

        if low_count:
            low_half = pl.program_id(0) < half // step

            @pl.when(low_half)
            def _():
                done(add(upstream, refs[count : count + low_count]))

            @pl.when(jnp.logical_not(low_half))
            def _():
                done(add(upstream, refs[count + low_count : -1]))

        else:
            done(upstream)

    block = pl.BlockSpec((step, width), lambda i: (i, 0))
    per_half = half // step
    low = pl.BlockSpec((step, width), lambda i: (jnp.minimum(i, per_half - 1), 0))
    high = pl.BlockSpec((step, width), lambda i: (jnp.maximum(i - per_half, 0), 0))
    return pl.pallas_call(
        body,
        grid=(rows // step,),
        in_specs=[block, whole((1, width))]
        + [block] * count
        + [low] * low_count
        + [high] * len(high_terms),
        out_specs=block,
        out_shape=jax.ShapeDtypeStruct((rows, width), jnp.bfloat16),
        compiler_params=params(16),
        cost_estimate=SMALL,
        name="finish",
    )(hidden, gain, *terms, *low_terms, *high_terms)


def pick_rows(matrix, sources, cost=SMALL):
    width = sources[0].shape[1]

    def body(matrix_ref, *refs):
        refs[-1][...] = mxu(matrix_ref[...], joined(refs[:-1])).astype(jnp.bfloat16)

    return pl.pallas_call(
        body,
        grid=(width // tile(width),),
        in_specs=[whole(matrix.shape)] + [columns(s.shape[0], width) for s in sources],
        out_specs=columns(matrix.shape[0], width),
        out_shape=jax.ShapeDtypeStruct((matrix.shape[0], width), jnp.bfloat16),
        compiler_params=params(16),
        cost_estimate=cost,
        name="pick_rows",
    )(matrix, *sources)


def in_order(pieces, x_place):
    half, width = pieces[0].shape

    def body(place_ref, *refs):
        out_ref = refs[-1]
        for i, ref in enumerate(refs[:-1]):
            step = (0, 1, RING - 1, 2)[i // 2]
            block = lax.rem(place_ref[0] + step, RING)
            first = pl.multiple_of((2 * block + i % 2) * half, half)
            out_ref[pl.ds(first, half), :] = ref[...]

    rows = half * len(pieces)
    return pl.pallas_call(
        body,
        grid=(width // tile(width),),
        in_specs=[pl.BlockSpec(memory_space=pltpu.SMEM)]
        + [columns(half, width) for _ in pieces],
        out_specs=columns(rows, width),
        out_shape=jax.ShapeDtypeStruct((rows, width), jnp.bfloat16),
        compiler_params=params(12),
        cost_estimate=SMALL,
        name="in_order",
    )(x_place.reshape(1), *pieces)


def line_scores(sources, queries, scale):
    width = queries.shape[1]
    steps = width // tile(width)

    def body(query_ref, *refs):
        step = pl.program_id(0)
        out_ref = refs[-1]

        @pl.when(step == 0)
        def _():
            out_ref[...] = jnp.zeros_like(out_ref)

        out_ref[...] += scale * mxu(joined(refs[:-1]), query_ref[...], 1, 1)

    out = (sum(s.shape[0] for s in sources), queries.shape[0])
    return pl.pallas_call(
        body,
        grid=(steps,),
        in_specs=[columns(queries.shape[0], width)]
        + [columns(s.shape[0], width) for s in sources],
        out_specs=whole(out),
        out_shape=jax.ShapeDtypeStruct(out, jnp.float32),
        compiler_params=params(20),
        cost_estimate=SMALL,
        name="line_scores",
    )(queries, *sources)


def far_scores(near, sources, queries, asked_by, line, scale):
    width = queries.shape[1]
    query_count = queries.shape[0]
    steps = width // tile(width)
    near_slots = near.shape[0] - line
    far_slots = asked_by.shape[0] - near_slots

    def body(near_ref, mask_ref, query_ref, *refs):
        out_ref, log_ref = refs[-2:]
        step = pl.program_id(0)

        @pl.when(step == 0)
        def _():
            out_ref[...] = jnp.zeros_like(out_ref)

        out_ref[...] += scale * mxu(joined(refs[:-2]), query_ref[...], 1, 1)

        @pl.when(step == steps - 1)
        def _():
            inner = near_ref[:line, :]
            own = jnp.where(mask_ref[:near_slots, :] > 0, near_ref[line:, :], LOW)
            far = jnp.where(mask_ref[near_slots:, :] > 0, out_ref[...], LOW)
            parts = (inner, own, far)
            top = jnp.max(inner, axis=0, keepdims=True)
            for part in parts[1:]:
                top = jnp.maximum(top, jnp.max(part, axis=0, keepdims=True))
            total = jnp.zeros_like(top)
            for part in parts:
                total += jnp.sum(jnp.exp(part - top), axis=0, keepdims=True)
            log_ref[...] = top + jnp.log(total)

    return pl.pallas_call(
        body,
        grid=(steps,),
        in_specs=[
            whole(near.shape),
            whole(asked_by.shape),
            columns(query_count, width),
        ]
        + [columns(s.shape[0], width) for s in sources],
        out_specs=[whole((far_slots, query_count)), whole((1, query_count))],
        out_shape=[
            jax.ShapeDtypeStruct((far_slots, query_count), jnp.float32),
            jax.ShapeDtypeStruct((1, query_count), jnp.float32),
        ],
        compiler_params=params(28),
        cost_estimate=LARGE,
        name="far_scores",
    )(near, asked_by, queries, *sources)


def query_side(near, far, asked_by, log_total, weight, target, y_place, queries, sources, line, scale):
    width = queries.shape[1]
    query_count = queries.shape[0]
    near_slots = near.shape[0] - line
    slot_count = asked_by.shape[0]
    count = len(sources)
    rows = line // RING
    cuts = ((0,), (1, 3, 2))

    def body(near_ref, far_ref, mask_ref, log_ref, weight_ref, target_ref, place_ref, query_ref, *refs):
        source_refs = refs[:count]
        part_ref, gain_ref, slot_ref, positive_ref = refs[count : count + 4]
        coeff_refs, (turned_ref, kept_ref) = refs[count + 4 : -2], refs[-2:]

        @pl.when(pl.program_id(0) == 0)
        def _():
            log_row, weight_row = log_ref[...], weight_ref[...]
            inner = near_ref[:line, :]
            row_place = lax.broadcasted_iota(jnp.int32, inner.shape, 0)
            hit = row_place == target_ref[...]
            positive_ref[...] = jnp.sum(jnp.where(hit, inner, 0.0), axis=0, keepdims=True)
            inner_coeff = weight_row * (jnp.exp(inner - log_row) - jnp.where(hit, 1.0, 0.0))
            kept_ref[...] = inner_coeff.astype(jnp.bfloat16)
            for coeff_ref, cut in zip(coeff_refs, cuts):
                for i, step in enumerate(cut):
                    block = lax.rem(place_ref[0] + step, RING)
                    first = pl.multiple_of(block * rows, rows)
                    coeff_ref[i * rows : (i + 1) * rows] = kept_ref[pl.ds(first, rows), :]
            own = jnp.where(mask_ref[:near_slots, :] > 0, near_ref[line:, :], LOW)
            slots = jnp.where(mask_ref[near_slots:, :] > 0, far_ref[...], LOW)
            own_coeff = (weight_row * jnp.exp(own - log_row)).astype(jnp.bfloat16)
            far_coeff = (weight_row * jnp.exp(slots - log_row)).astype(jnp.bfloat16)
            ones = jnp.ones((8, query_count), jnp.bfloat16)
            slot_ref[:, :near_slots] = mxu(ones, own_coeff, 1, 1)
            slot_ref[:, near_slots:] = mxu(ones, far_coeff, 1, 1)
            turned_ref[:, :line] = jnp.transpose(inner_coeff).astype(jnp.bfloat16)
            turned_ref[:, line : line + near_slots] = jnp.transpose(
                own_coeff.astype(jnp.float32)
            ).astype(jnp.bfloat16)
            turned_ref[:, line + near_slots :] = jnp.transpose(
                far_coeff.astype(jnp.float32)
            ).astype(jnp.bfloat16)

        total = scale * mxu(turned_ref[...], joined(source_refs))
        part_ref[...] = total.astype(jnp.bfloat16)
        gain_ref[...] = jnp.sum(total * query_ref[...].astype(jnp.float32), axis=0, keepdims=True)

    row = whole((1, query_count))
    return pl.pallas_call(
        body,
        grid=(width // tile(width),),
        in_specs=[
            whole(near.shape),
            whole(far.shape),
            whole(asked_by.shape),
            row,
            row,
            row,
            pl.BlockSpec(memory_space=pltpu.SMEM),
            columns(query_count, width),
        ]
        + [columns(s.shape[0], width) for s in sources],
        out_specs=[
            columns(query_count, width),
            columns(1, width),
            whole((8, slot_count)),
            row,
        ]
        + [whole((rows * len(cut), query_count)) for cut in cuts],
        out_shape=[
            jax.ShapeDtypeStruct((query_count, width), jnp.bfloat16),
            jax.ShapeDtypeStruct((1, width), jnp.float32),
            jax.ShapeDtypeStruct((8, slot_count), jnp.float32),
            jax.ShapeDtypeStruct((1, query_count), jnp.float32),
        ]
        + [jax.ShapeDtypeStruct((rows * len(cut), query_count), jnp.bfloat16) for cut in cuts],
        scratch_shapes=[
            pltpu.VMEM((query_count, line + slot_count), jnp.bfloat16),
            pltpu.VMEM((line, query_count), jnp.bfloat16),
        ],
        compiler_params=params(32),
        cost_estimate=SMALL,
        name="query_side",
    )(near, far, asked_by, log_total, weight, target, y_place, queries, *sources)


def passage_side(coeff, queries, put, arrived, scale, out_type, pieces):
    width = queries.shape[1]
    rows = coeff.shape[0] // pieces

    def body(coeff_ref, query_ref, put_ref, arrived_ref, *out_refs):
        total = mxu(coeff_ref[...], query_ref[...]) + mxu(put_ref[...], arrived_ref[...])
        total = scale * total
        for i, out_ref in enumerate(out_refs):
            out_ref[...] = total[i * rows : (i + 1) * rows].astype(out_type)

    return pl.pallas_call(
        body,
        grid=(width // tile(width),),
        in_specs=[
            whole(coeff.shape),
            columns(queries.shape[0], width),
            whole(put.shape),
            columns(arrived.shape[0], width),
        ],
        out_specs=[columns(rows, width)] * pieces,
        out_shape=[jax.ShapeDtypeStruct((rows, width), out_type)] * pieces,
        compiler_params=params(20),
        cost_estimate=LARGE if pieces > 1 else SMALL,
        name="passage_side",
    )(coeff, queries, put, arrived)


def on_device(query_hidden, passage_hidden, norm_gain, query_weight, hneg_ids):
    rows, width = query_hidden.shape
    neg_count = hneg_ids.shape[1]
    z_count = lax.axis_size("z")
    group_count = 2 * z_count
    line = RING * rows
    scale = 1.0 / (SOFTMAX_TEMPER * math.sqrt(width))
    y_place, x_place = lax.axis_index("y"), lax.axis_index("x")

    gain = norm_gain.reshape(1, width)
    p_own = embed(passage_hidden, gain)
    p_line = lax.all_gather(p_own, "y", axis=0, tiled=True)
    q_pieces = ring_pieces(embed(query_hidden, gain), "x")

    flat_ids = hneg_ids.reshape(-1)
    id_count = rows * neg_count
    owners = flat_ids // rows
    local_row = flat_ids % rows
    number = jnp.arange(id_count, dtype=jnp.int32)
    same = (owners[:, None] == owners[None, :]) & (number[None, :] < number[:, None])
    rank = jnp.sum(same.astype(jnp.int32), axis=1)
    y_step = (owners // RING - y_place) % RING
    line_of = (owners // (RING * RING)) * RING + owners % RING
    slot = (line_of * RING + y_step) * CAP + rank
    slot_count = group_count * RING * RING * CAP
    hit = slot[None, :] == jnp.arange(slot_count, dtype=jnp.int32)[:, None]
    slot_row = jnp.sum(jnp.where(hit, local_row[None, :] + 1, 0), axis=1) - 1
    slot_query = jnp.sum(jnp.where(hit, number[None, :] // neg_count + 1, 0), axis=1)
    slot_row, p_own = lax.optimization_barrier((slot_row, p_own))
    asked = lax.all_to_all(
        slot_row.reshape(group_count * RING, RING * CAP), ("z", "c", "x"), 0, 0, tiled=True
    )
    asked = asked.reshape(group_count, RING, RING, CAP).transpose(0, 2, 1, 3)
    asked, _ = lax.optimization_barrier((asked, q_pieces[2:6]))
    place = jnp.arange(line, dtype=jnp.int32)
    asked_own = asked[:, 0].reshape(-1)
    far_steps = [1, RING - 1, 2]
    asked_far = jnp.stack([asked[:, step] for step in far_steps], axis=1)

    def numbered(blocks):
        blocks = jnp.stack(blocks).astype(jnp.int32)[None, :, None, None]
        return jnp.where(asked_far < 0, -1, asked_far + rows * blocks).reshape(-1)

    asked_line = numbered([(y_place + step) % RING for step in far_steps])
    asked_far = numbered([jnp.int32(i) for i in range(RING - 1)])

    def one_hot(numbers, size):
        return (numbers[:, None] == place[None, :size]).astype(jnp.bfloat16)

    hard_own = group_rows(pick_rows(one_hot(asked_own, rows), [p_own]), group_count)
    hard_far = group_rows(pick_rows(one_hot(asked_line, line), [p_line]), group_count)

    q_line = in_order(q_pieces, x_place)

    by_x = slot_query.reshape(group_count, RING, RING * CAP).transpose(1, 0, 2)
    asker = line_table(by_x.reshape(RING, -1)).reshape(RING, group_count, RING, CAP)
    x_base = rows * jnp.arange(RING, dtype=jnp.int32)
    asker = jnp.where(asker == 0, -1, asker - 1 + x_base[:, None, None, None])
    asker = asker.transpose(1, 2, 0, 3)
    far_asker = jnp.concatenate([asker[:, 1:2], asker[:, 3:], asker[:, 2:3]], axis=1)
    send_own = one_hot(asker[:, 0].reshape(-1), line)
    send_far = one_hot(far_asker.reshape(-1), line)
    asked_by = jnp.concatenate([send_own, send_far], axis=0)
    leave_far = pick_rows(send_far, [q_line])
    leave_own = pick_rows(send_own, [q_line])
    q_line, leave_far, leave_own = lax.optimization_barrier((q_line, leave_far, leave_own))
    far_queries = group_rows(leave_far, group_count)
    own_queries = group_rows(leave_own, group_count)

    near = line_scores([p_line, hard_own], q_line, scale)
    far, part_log = far_scores(near, [hard_far], q_line, asked_by, line, scale)
    part_log = part_log.reshape(RING, rows)
    own_place = jnp.arange(RING, dtype=jnp.int32)[:, None] == x_place
    own_weight = jnp.where(own_place, query_weight[None, :], 0.0)
    message = jnp.concatenate([part_log, own_weight], axis=0)
    messages = [message] + [shift(message, "x", step) for step in (1, 3, 2)]
    logs = [m[:RING] for m in messages]
    weight = sum(m[RING:] for m in messages).reshape(1, line)
    top = jnp.maximum(jnp.maximum(logs[0], logs[1]), jnp.maximum(logs[2], logs[3]))
    log_total = (top + jnp.log(sum(jnp.exp(part - top) for part in logs))).reshape(1, line)
    first_row = x_place * rows
    target = place[None, :] - first_row
    target = jnp.where((target >= 0) & (target < rows), target + y_place * rows, -1)

    part, gain_part, slot_coeff, positive, coeff_own, coeff_far = query_side(
        near, far, asked_by, log_total, weight, target, y_place.reshape(1), q_line,
        [p_line, hard_own, hard_far], line, scale,
    )
    loss_rows = lax.dynamic_slice(log_total - positive, (0, first_row), (1, rows)).reshape(-1)
    query_up = lax.psum_scatter(part, "x", scatter_dimension=0, tiled=True)
    query_grad = finish(query_hidden, gain, [query_up], [], [])

    own_end = group_count * RING * CAP
    pieces = (
        slot_coeff[0, :own_end].reshape(group_count, -1),
        slot_coeff[0, own_end:].reshape(group_count, -1),
    )
    got_coeff = group_table(jnp.concatenate(pieces, axis=1), group_count)
    first = RING * CAP

    def put_rows(numbers, values, size):
        return jnp.where(
            place[:size, None] == numbers[None, :], values.reshape(-1)[None, :], 0.0
        ).astype(jnp.bfloat16)

    put_own = put_rows(asked_own, got_coeff[:, :first], rows)
    put_far = put_rows(asked_far, got_coeff[:, first:], 3 * rows)
    far_part = passage_side(coeff_far, q_line, put_far, far_queries, scale, jnp.bfloat16, 6)
    low_terms, high_terms, sent = ring_scatter(far_part, "y")
    gain_part, own_queries = lax.optimization_barrier((gain_part, own_queries))
    gain_part = axes_sum(gain_part.reshape(-1, 128), ("c", "x", "z"))
    gain_part, _ = lax.optimization_barrier((gain_part, sent))
    gain_grad = 2.0 * axes_sum(gain_part, ("y",)).reshape(-1) / norm_gain

    own_part = passage_side(coeff_own, q_line, put_own, own_queries, scale, jnp.float32, 1)[0]
    own_part, query_grad = lax.optimization_barrier((own_part, query_grad))
    passage_grad = finish(passage_hidden, gain, [own_part], low_terms, high_terms)
    return (loss_rows, query_grad, passage_grad, gain_grad)


def solution(mesh):
    torus = Mesh(mesh.devices.reshape(-1, 2, RING, RING), ALL_AXES)
    return jax.shard_map(
        on_device,
        mesh=torus,
        in_specs=(
            P(ALL_AXES, None),
            P(ALL_AXES, None),
            P(),
            P(ALL_AXES),
            P(ALL_AXES, None),
        ),
        out_specs=(
            P(ALL_AXES),
            P(ALL_AXES, None),
            P(ALL_AXES, None),
            P(),
        ),
        check_vma=False,
    )
```

```python
import math

import jax
import jax.numpy as jnp
from jax import lax
from jax.experimental import pallas as pl
from jax.experimental.pallas import tpu as pltpu
from jax.sharding import Mesh, PartitionSpec as P

EPSILON = 1e-06
SOFTMAX_TEMPER = 0.28
RING = 4
CAP = 4
GROUPS = ("z", "c")
ALL_AXES = ("z", "c", "y", "x")
MIB = 1024 * 1024
LOW = -1e30


def shift(value, axis, step):
    return lax.ppermute(value, axis, [(i, (i + step) % RING) for i in range(RING)])


def ring_gather(block, axis):
    half = block.shape[0] // 2
    up = shift(block, axis, -1)
    down = shift(block, axis, 1)
    return [up, down], [shift(up[:half], axis, -1), shift(down[half:], axis, 1)]


def pair_sum(value, axis, turn):
    size = lax.axis_size(axis)
    pairs = [(i, size - 1 - i if turn else i ^ 1) for i in range(size)]
    return value + lax.ppermute(value, axis, pairs)


def group_rows(rows, group_count):
    blocks = rows.reshape(group_count, rows.shape[0] // group_count, rows.shape[1])
    return lax.all_to_all(blocks, GROUPS, 0, 0, tiled=True).reshape(rows.shape)


def group_table(table, group_count):
    z_count = group_count // 2
    z_place, c_place = lax.axis_index("z"), lax.axis_index("c")
    got = jnp.zeros_like(table)
    places = jnp.arange(group_count, dtype=jnp.int32)[:, None]
    for z_step in range(z_count):
        for c_step in range(2):
            to_group = ((z_place + z_step) % z_count) * 2 + (c_place ^ c_step)
            from_group = ((z_place + z_count - z_step) % z_count) * 2 + (c_place ^ c_step)
            row = jnp.sum(jnp.where(places == to_group, table, 0), axis=0, keepdims=True)
            if z_step or c_step:
                row = lax.ppermute(
                    row,
                    GROUPS,
                    [
                        (z * 2 + c, ((z + z_step) % z_count) * 2 + (c ^ c_step))
                        for z in range(z_count)
                        for c in range(2)
                    ],
                )
            got = got + jnp.where(places == from_group, row, 0)
    return got


def line_table(table):
    x_place = lax.axis_index("x")
    places = jnp.arange(RING, dtype=jnp.int32)[:, None]
    got = jnp.where(places == x_place, table, 0)
    for step in range(1, RING):
        chosen = places == (x_place + step) % RING
        row = jnp.sum(jnp.where(chosen, table, 0), axis=0, keepdims=True)
        row = shift(row, "x", step)
        got = got + jnp.where(places == (x_place + RING - step) % RING, row, 0)
    return got


def mxu(left, right, left_dim=1, right_dim=0):
    return lax.dot_general(
        left, right, (((left_dim,), (right_dim,)), ((), ())), preferred_element_type=jnp.float32
    )


def params(mib):
    return pltpu.CompilerParams(dimension_semantics=("arbitrary",), vmem_limit_bytes=mib * MIB)


SMALL = pl.CostEstimate(flops=1, bytes_accessed=1, transcendentals=0)
LARGE = pl.CostEstimate(flops=10**11, bytes_accessed=10**8, transcendentals=0)


def tile(width):
    return min(1024, width)


def whole(shape):
    return pl.BlockSpec(shape, lambda i: (0,) * len(shape))


def columns(rows, width):
    return pl.BlockSpec((rows, tile(width)), lambda i: (0, i))


def joined(refs):
    blocks = [ref[...] for ref in refs]
    return blocks[0] if len(blocks) == 1 else jnp.concatenate(blocks, axis=0)


def inverse_norm(values):
    return lax.rsqrt(jnp.mean(values * values, axis=-1, keepdims=True) + EPSILON)


def embed(hidden, gain):
    def body(hidden_ref, gain_ref, out_ref):
        values = hidden_ref[...].astype(jnp.float32)
        unit_rows = values * inverse_norm(values)
        out_ref[...] = (unit_rows * gain_ref[...]).astype(jnp.bfloat16)

    rows, width = hidden.shape
    step = rows // 4
    block = pl.BlockSpec((step, width), lambda i: (i, 0))
    return pl.pallas_call(
        body,
        grid=(rows // step,),
        in_specs=[block, whole((1, width))],
        out_specs=block,
        out_shape=jax.ShapeDtypeStruct((rows, width), jnp.bfloat16),
        compiler_params=params(12),
        cost_estimate=SMALL,
        name="embed",
    )(hidden, gain)


def finish(hidden, gain, terms):
    rows, width = hidden.shape
    step = rows // 4

    def body(hidden_ref, gain_ref, *refs):
        total = refs[0][...].astype(jnp.float32)
        for ref in refs[1:-1]:
            total += ref[...].astype(jnp.float32)
        values = hidden_ref[...].astype(jnp.float32)
        inverse = inverse_norm(values)
        unit_rows = values * inverse
        scaled = total * gain_ref[...]
        inner = jnp.mean(scaled * unit_rows, axis=-1, keepdims=True)
        refs[-1][...] = (inverse * (scaled - unit_rows * inner)).astype(jnp.bfloat16)

    block = pl.BlockSpec((step, width), lambda i: (i, 0))
    return pl.pallas_call(
        body,
        grid=(rows // step,),
        in_specs=[block, whole((1, width))] + [block] * len(terms),
        out_specs=block,
        out_shape=jax.ShapeDtypeStruct((rows, width), jnp.bfloat16),
        compiler_params=params(16),
        cost_estimate=SMALL,
        name="finish",
    )(hidden, gain, *terms)


def pick_rows(matrix, sources):
    width = sources[0].shape[1]

    def body(matrix_ref, *refs):
        refs[-1][...] = mxu(matrix_ref[...], joined(refs[:-1])).astype(jnp.bfloat16)

    return pl.pallas_call(
        body,
        grid=(width // tile(width),),
        in_specs=[whole(matrix.shape)] + [columns(s.shape[0], width) for s in sources],
        out_specs=columns(matrix.shape[0], width),
        out_shape=jax.ShapeDtypeStruct((matrix.shape[0], width), jnp.bfloat16),
        compiler_params=params(16),
        cost_estimate=SMALL,
        name="pick_rows",
    )(matrix, *sources)


def line_scores(sources, queries, scale):
    width = queries.shape[1]
    steps = width // tile(width)

    def body(query_ref, *refs):
        step = pl.program_id(0)
        out_ref = refs[-1]

        @pl.when(step == 0)
        def _():
            out_ref[...] = jnp.zeros_like(out_ref)

        out_ref[...] += scale * mxu(joined(refs[:-1]), query_ref[...], 1, 1)

    out = (sum(s.shape[0] for s in sources), queries.shape[0])
    return pl.pallas_call(
        body,
        grid=(steps,),
        in_specs=[columns(queries.shape[0], width)]
        + [columns(s.shape[0], width) for s in sources],
        out_specs=whole(out),
        out_shape=jax.ShapeDtypeStruct(out, jnp.float32),
        compiler_params=params(20),
        cost_estimate=SMALL,
        name="line_scores",
    )(queries, *sources)


def far_scores(near, sources, queries, asked_by, line, scale):
    width = queries.shape[1]
    query_count = queries.shape[0]
    steps = width // tile(width)
    near_slots = near.shape[0] - line
    far_slots = asked_by.shape[0] - near_slots

    def body(near_ref, mask_ref, query_ref, *refs):
        out_ref, log_ref = refs[-2:]
        step = pl.program_id(0)

        @pl.when(step == 0)
        def _():
            out_ref[...] = jnp.zeros_like(out_ref)

        out_ref[...] += scale * mxu(joined(refs[:-2]), query_ref[...], 1, 1)

        @pl.when(step == steps - 1)
        def _():
            inner = near_ref[:line, :]
            own = jnp.where(mask_ref[:near_slots, :] > 0, near_ref[line:, :], LOW)
            far = jnp.where(mask_ref[near_slots:, :] > 0, out_ref[...], LOW)
            parts = (inner, own, far)
            top = jnp.max(inner, axis=0, keepdims=True)
            for part in parts[1:]:
                top = jnp.maximum(top, jnp.max(part, axis=0, keepdims=True))
            total = jnp.zeros_like(top)
            for part in parts:
                total += jnp.sum(jnp.exp(part - top), axis=0, keepdims=True)
            log_ref[...] = top + jnp.log(total)

    return pl.pallas_call(
        body,
        grid=(steps,),
        in_specs=[
            whole(near.shape),
            whole(asked_by.shape),
            columns(query_count, width),
        ]
        + [columns(s.shape[0], width) for s in sources],
        out_specs=[whole((far_slots, query_count)), whole((1, query_count))],
        out_shape=[
            jax.ShapeDtypeStruct((far_slots, query_count), jnp.float32),
            jax.ShapeDtypeStruct((1, query_count), jnp.float32),
        ],
        compiler_params=params(28),
        cost_estimate=LARGE,
        name="far_scores",
    )(near, asked_by, queries, *sources)


def query_side(near, far, asked_by, log_total, weight, target, queries, sources, line, scale):
    width = queries.shape[1]
    query_count = queries.shape[0]
    near_slots = near.shape[0] - line
    slot_count = asked_by.shape[0]
    count = len(sources)
    rows = line // RING
    cuts = (rows, 3 * rows)

    def body(near_ref, far_ref, mask_ref, log_ref, weight_ref, target_ref, query_ref, *refs):
        source_refs = refs[:count]
        part_ref, gain_ref, slot_ref, positive_ref = refs[count : count + 4]
        coeff_refs, turned_ref = refs[count + 4 : -1], refs[-1]

        @pl.when(pl.program_id(0) == 0)
        def _():
            log_row, weight_row = log_ref[...], weight_ref[...]
            inner = near_ref[:line, :]
            row_place = lax.broadcasted_iota(jnp.int32, inner.shape, 0)
            hit = row_place == target_ref[...]
            positive_ref[...] = jnp.sum(jnp.where(hit, inner, 0.0), axis=0, keepdims=True)
            inner_coeff = weight_row * (jnp.exp(inner - log_row) - jnp.where(hit, 1.0, 0.0))
            at = 0
            for coeff_ref, size in zip(coeff_refs, cuts):
                coeff_ref[...] = inner_coeff[at : at + size].astype(jnp.bfloat16)
                at += size
            own = jnp.where(mask_ref[:near_slots, :] > 0, near_ref[line:, :], LOW)
            slots = jnp.where(mask_ref[near_slots:, :] > 0, far_ref[...], LOW)
            own_coeff = (weight_row * jnp.exp(own - log_row)).astype(jnp.bfloat16)
            far_coeff = (weight_row * jnp.exp(slots - log_row)).astype(jnp.bfloat16)
            ones = jnp.ones((8, query_count), jnp.bfloat16)
            slot_ref[:, :near_slots] = mxu(ones, own_coeff, 1, 1)
            slot_ref[:, near_slots:] = mxu(ones, far_coeff, 1, 1)
            turned_ref[:, :line] = jnp.transpose(inner_coeff).astype(jnp.bfloat16)
            turned_ref[:, line : line + near_slots] = jnp.transpose(
                own_coeff.astype(jnp.float32)
            ).astype(jnp.bfloat16)
            turned_ref[:, line + near_slots :] = jnp.transpose(
                far_coeff.astype(jnp.float32)
            ).astype(jnp.bfloat16)

        total = scale * mxu(turned_ref[...], joined(source_refs))
        part_ref[...] = total.astype(jnp.bfloat16)
        gain_ref[...] = jnp.sum(total * query_ref[...].astype(jnp.float32), axis=0, keepdims=True)

    row = whole((1, query_count))
    return pl.pallas_call(
        body,
        grid=(width // tile(width),),
        in_specs=[
            whole(near.shape),
            whole(far.shape),
            whole(asked_by.shape),
            row,
            row,
            row,
            columns(query_count, width),
        ]
        + [columns(s.shape[0], width) for s in sources],
        out_specs=[
            columns(query_count, width),
            columns(1, width),
            whole((8, slot_count)),
            row,
        ]
        + [whole((size, query_count)) for size in cuts],
        out_shape=[
            jax.ShapeDtypeStruct((query_count, width), jnp.bfloat16),
            jax.ShapeDtypeStruct((1, width), jnp.float32),
            jax.ShapeDtypeStruct((8, slot_count), jnp.float32),
            jax.ShapeDtypeStruct((1, query_count), jnp.float32),
        ]
        + [jax.ShapeDtypeStruct((size, query_count), jnp.bfloat16) for size in cuts],
        scratch_shapes=[pltpu.VMEM((query_count, line + slot_count), jnp.bfloat16)],
        compiler_params=params(32),
        cost_estimate=SMALL,
        name="query_side",
    )(near, far, asked_by, log_total, weight, target, queries, *sources)


def passage_side(coeff, queries, put, arrived, scale, out_type, layout, cost):
    width = queries.shape[1]
    sizes = [sum(high - low for low, high in ranges) for ranges in layout]

    def body(coeff_ref, query_ref, put_ref, arrived_ref, *out_refs):
        total = mxu(coeff_ref[...], query_ref[...]) + mxu(put_ref[...], arrived_ref[...])
        total = scale * total
        for ranges, out_ref in zip(layout, out_refs):
            at = 0
            for low, high in ranges:
                out_ref[at : at + high - low] = total[low:high].astype(out_type)
                at += high - low

    return pl.pallas_call(
        body,
        grid=(width // tile(width),),
        in_specs=[
            whole(coeff.shape),
            columns(queries.shape[0], width),
            whole(put.shape),
            columns(arrived.shape[0], width),
        ],
        out_specs=[columns(size, width) for size in sizes],
        out_shape=[jax.ShapeDtypeStruct((size, width), out_type) for size in sizes],
        compiler_params=params(20),
        cost_estimate=cost,
        name="passage_side",
    )(coeff, queries, put, arrived)


def add_passing(up, passing_low, down, passing_high):
    half, width = passing_low.shape

    def body(up_ref, low_ref, down_ref, high_ref, up_out, down_out):
        wide = jnp.float32
        up_out[...] = (up_ref[...].astype(wide) + low_ref[...].astype(wide)).astype(up.dtype)
        down_out[...] = (down_ref[...].astype(wide) + high_ref[...].astype(wide)).astype(up.dtype)

    low = pl.BlockSpec((half, tile(width)), lambda i: (0, i))
    high = pl.BlockSpec((half, tile(width)), lambda i: (1, i))
    return pl.pallas_call(
        body,
        grid=(width // tile(width),),
        in_specs=[low, low, high, low],
        out_specs=[low, high],
        out_shape=[jax.ShapeDtypeStruct(up.shape, up.dtype)] * 2,
        input_output_aliases={0: 0, 2: 1},
        compiler_params=params(12),
        cost_estimate=SMALL,
        name="add_passing",
    )(up, passing_low, down, passing_high)


def on_device(query_hidden, passage_hidden, norm_gain, query_weight, hneg_ids):
    rows, width = query_hidden.shape
    neg_count = hneg_ids.shape[1]
    z_count = lax.axis_size("z")
    group_count = 2 * z_count
    line = RING * rows
    scale = 1.0 / (SOFTMAX_TEMPER * math.sqrt(width))
    y_place, x_place = lax.axis_index("y"), lax.axis_index("x")

    gain = norm_gain.reshape(1, width)
    p_own = embed(passage_hidden, gain)
    p_mid, p_opp = ring_gather(p_own, "y")

    flat_ids = hneg_ids.reshape(-1)
    id_count = rows * neg_count
    owners = flat_ids // rows
    local_row = flat_ids % rows
    number = jnp.arange(id_count, dtype=jnp.int32)
    same = (owners[:, None] == owners[None, :]) & (number[None, :] < number[:, None])
    rank = jnp.sum(same.astype(jnp.int32), axis=1)
    y_step = (owners // RING - y_place) % RING
    line_of = (owners // (RING * RING)) * RING + owners % RING
    slot = (line_of * RING + y_step) * CAP + rank
    slot_count = group_count * RING * RING * CAP
    hit = slot[None, :] == jnp.arange(slot_count, dtype=jnp.int32)[:, None]
    slot_row = jnp.sum(jnp.where(hit, local_row[None, :] + 1, 0), axis=1) - 1
    slot_query = jnp.sum(jnp.where(hit, number[None, :] // neg_count + 1, 0), axis=1)
    asked = lax.all_to_all(
        slot_row.reshape(group_count * RING, RING * CAP), ("z", "c", "x"), 0, 0, tiled=True
    )
    asked = asked.reshape(group_count, RING, RING, CAP).transpose(0, 2, 1, 3)
    place = jnp.arange(line, dtype=jnp.int32)
    asked, _ = lax.optimization_barrier((asked, p_mid))
    asked_own = asked[:, 0].reshape(-1)
    above = jnp.where(asked[:, 3:] < 0, -1, asked[:, 3:] + rows)
    opposite = jnp.where(asked[:, 2:3] < 0, -1, asked[:, 2:3] + 2 * rows)
    asked_far = jnp.concatenate([asked[:, 1:2], above, opposite], axis=1).reshape(-1)

    def one_hot(numbers, size):
        return (numbers[:, None] == place[None, :size]).astype(jnp.bfloat16)

    chosen_own = pick_rows(one_hot(asked_own, rows), [p_own])
    hard_own = group_rows(chosen_own, group_count)
    chosen_far = pick_rows(one_hot(asked_far, 3 * rows), [*p_mid, *p_opp])
    hard_far = group_rows(chosen_far, group_count)

    q_emb = embed(query_hidden, gain)
    q_line = lax.all_gather(q_emb, "x", axis=0, tiled=True)

    by_x = slot_query.reshape(group_count, RING, RING * CAP).transpose(1, 0, 2)
    asker = line_table(by_x.reshape(RING, -1)).reshape(RING, group_count, RING, CAP)
    x_base = rows * jnp.arange(RING, dtype=jnp.int32)
    asker = jnp.where(asker == 0, -1, asker - 1 + x_base[:, None, None, None])
    asker = asker.transpose(1, 2, 0, 3)
    far_asker = jnp.concatenate([asker[:, 1:2], asker[:, 3:], asker[:, 2:3]], axis=1)
    send_own = one_hot(asker[:, 0].reshape(-1), line)
    send_far = one_hot(far_asker.reshape(-1), line)
    asked_by = jnp.concatenate([send_own, send_far], axis=0)
    leave_far = pick_rows(send_far, [q_line])
    leave_own = pick_rows(send_own, [q_line])
    q_line, leave_far, leave_own = lax.optimization_barrier((q_line, leave_far, leave_own))
    far_queries = group_rows(leave_far, group_count)
    own_queries = group_rows(leave_own, group_count)

    near = line_scores([p_own, *p_mid, *p_opp, hard_own], q_line, scale)
    far, part_log = far_scores(near, [hard_far], q_line, asked_by, line, scale)
    part_log = part_log.reshape(RING, rows)
    own_place = jnp.arange(RING, dtype=jnp.int32)[:, None] == x_place
    own_weight = jnp.where(own_place, query_weight[None, :], 0.0)
    message = jnp.concatenate([part_log, own_weight], axis=0)
    messages = [message] + [shift(message, "x", step) for step in (1, 3, 2)]
    logs = [m[:RING] for m in messages]
    weight = sum(m[RING:] for m in messages).reshape(1, line)
    top = jnp.maximum(jnp.maximum(logs[0], logs[1]), jnp.maximum(logs[2], logs[3]))
    log_total = (top + jnp.log(sum(jnp.exp(part - top) for part in logs))).reshape(1, line)
    first_row = x_place * rows
    target = place[None, :] - first_row
    target = jnp.where((target >= 0) & (target < rows), target, -1)

    part, gain_part, slot_coeff, positive, coeff_own, coeff_far = query_side(
        near, far, asked_by, log_total, weight, target, q_line,
        [p_own, *p_mid, *p_opp, hard_own, hard_far], line, scale,
    )
    loss_rows = lax.dynamic_slice(log_total - positive, (0, first_row), (1, rows)).reshape(-1)
    query_up = lax.psum_scatter(part, "x", scatter_dimension=0, tiled=True)
    query_grad = finish(query_hidden, gain, [query_up])

    own_end = group_count * RING * CAP
    pieces = (
        slot_coeff[0, :own_end].reshape(group_count, -1),
        slot_coeff[0, own_end:].reshape(group_count, -1),
    )
    got_coeff = group_table(jnp.concatenate(pieces, axis=1), group_count)
    first = RING * CAP

    def put_rows(numbers, values, size):
        return jnp.where(
            place[:size, None] == numbers[None, :], values.reshape(-1)[None, :], 0.0
        ).astype(jnp.bfloat16)

    put_own = put_rows(asked_own, got_coeff[:, :first], rows)
    put_far = put_rows(asked_far, got_coeff[:, first:], 3 * rows)
    half = rows // 2
    low_1, high_1, low_3, high_3, low_2, high_2 = [(i * half, (i + 1) * half) for i in range(6)]
    for_above, for_below, pass_up, pass_down = passage_side(
        coeff_far, q_line, put_far, far_queries, scale, jnp.bfloat16,
        [[low_1, high_1], [low_3, high_3], [low_2], [high_2]], LARGE,
    )
    for_above, for_below = add_passing(
        for_above, shift(pass_up, "y", 1), for_below, shift(pass_down, "y", -1)
    )
    from_below = shift(for_above, "y", 1)
    from_above = shift(for_below, "y", -1)
    gain_part, _ = lax.optimization_barrier((gain_part.reshape(-1, 128), for_above))
    gain_part = pair_sum(gain_part, "c", False)
    for axis in ("x", "z", "y"):
        gain_part = pair_sum(pair_sum(gain_part, axis, False), axis, True)
    gain_grad = 2.0 * gain_part.reshape(-1) / norm_gain

    own_part = passage_side(
        coeff_own, q_line, put_own, own_queries, scale, jnp.float32, [[(0, rows)]], SMALL
    )[0]
    own_part, query_grad = lax.optimization_barrier((own_part, query_grad))
    passage_grad = finish(passage_hidden, gain, [own_part, from_below, from_above])
    return (loss_rows, query_grad, passage_grad, gain_grad)


def solution(mesh):
    torus = Mesh(mesh.devices.reshape(-1, 2, RING, RING), ALL_AXES)
    return jax.shard_map(
        on_device,
        mesh=torus,
        in_specs=(
            P(ALL_AXES, None),
            P(ALL_AXES, None),
            P(),
            P(ALL_AXES),
            P(ALL_AXES, None),
        ),
        out_specs=(
            P(ALL_AXES),
            P(ALL_AXES, None),
            P(ALL_AXES, None),
            P(),
        ),
        check_vma=False,
    )
```

```python
import math

import jax
import jax.numpy as jnp
from jax import lax
from jax.experimental import pallas as pl
from jax.experimental.pallas import tpu as pltpu
from jax.sharding import Mesh, PartitionSpec as P

EPSILON = 1e-06
SOFTMAX_TEMPER = 0.28
RING = 4
CAP = 4
GROUPS = ("z", "c")
ALL_AXES = ("z", "c", "y", "x")
MIB = 1024 * 1024
LOW = -1e30


def shift(value, axis, step):
    return lax.ppermute(value, axis, [(i, (i + step) % RING) for i in range(RING)])


def ring_gather(block, axis):
    half = block.shape[0] // 2
    up = shift(block, axis, -1)
    down = shift(block, axis, 1)
    return [up, down], [shift(up[:half], axis, -1), shift(down[half:], axis, 1)]


def pair_sum(value, axis, turn):
    size = lax.axis_size(axis)
    pairs = [(i, size - 1 - i if turn else i ^ 1) for i in range(size)]
    return value + lax.ppermute(value, axis, pairs)


def group_rows(rows, group_count):
    blocks = rows.reshape(group_count, rows.shape[0] // group_count, rows.shape[1])
    return lax.all_to_all(blocks, GROUPS, 0, 0, tiled=True).reshape(rows.shape)


def group_table(table, group_count):
    z_count = group_count // 2
    z_place, c_place = lax.axis_index("z"), lax.axis_index("c")
    got = jnp.zeros_like(table)
    places = jnp.arange(group_count, dtype=jnp.int32)[:, None]
    for z_step in range(z_count):
        for c_step in range(2):
            to_group = ((z_place + z_step) % z_count) * 2 + (c_place ^ c_step)
            from_group = ((z_place + z_count - z_step) % z_count) * 2 + (c_place ^ c_step)
            row = jnp.sum(jnp.where(places == to_group, table, 0), axis=0, keepdims=True)
            if z_step or c_step:
                row = lax.ppermute(
                    row,
                    GROUPS,
                    [
                        (z * 2 + c, ((z + z_step) % z_count) * 2 + (c ^ c_step))
                        for z in range(z_count)
                        for c in range(2)
                    ],
                )
            got = got + jnp.where(places == from_group, row, 0)
    return got


def line_table(table):
    x_place = lax.axis_index("x")
    places = jnp.arange(RING, dtype=jnp.int32)[:, None]
    got = jnp.where(places == x_place, table, 0)
    for step in range(1, RING):
        chosen = places == (x_place + step) % RING
        row = jnp.sum(jnp.where(chosen, table, 0), axis=0, keepdims=True)
        row = shift(row, "x", step)
        got = got + jnp.where(places == (x_place + RING - step) % RING, row, 0)
    return got


def mxu(left, right, left_dim=1, right_dim=0):
    return lax.dot_general(
        left, right, (((left_dim,), (right_dim,)), ((), ())), preferred_element_type=jnp.float32
    )


def params(mib):
    return pltpu.CompilerParams(dimension_semantics=("arbitrary",), vmem_limit_bytes=mib * MIB)


SMALL = pl.CostEstimate(flops=1, bytes_accessed=1, transcendentals=0)
LARGE = pl.CostEstimate(flops=10**11, bytes_accessed=10**8, transcendentals=0)


def tile(width):
    return min(1024, width)


def whole(shape):
    return pl.BlockSpec(shape, lambda i: (0,) * len(shape))


def columns(rows, width):
    return pl.BlockSpec((rows, tile(width)), lambda i: (0, i))


def joined(refs):
    blocks = [ref[...] for ref in refs]
    return blocks[0] if len(blocks) == 1 else jnp.concatenate(blocks, axis=0)


def inverse_norm(values):
    return lax.rsqrt(jnp.mean(values * values, axis=-1, keepdims=True) + EPSILON)


def embed(hidden, gain):
    def body(hidden_ref, gain_ref, out_ref):
        values = hidden_ref[...].astype(jnp.float32)
        unit_rows = values * inverse_norm(values)
        out_ref[...] = (unit_rows * gain_ref[...]).astype(jnp.bfloat16)

    rows, width = hidden.shape
    step = rows // 4
    block = pl.BlockSpec((step, width), lambda i: (i, 0))
    return pl.pallas_call(
        body,
        grid=(rows // step,),
        in_specs=[block, whole((1, width))],
        out_specs=block,
        out_shape=jax.ShapeDtypeStruct((rows, width), jnp.bfloat16),
        compiler_params=params(12),
        cost_estimate=SMALL,
        name="embed",
    )(hidden, gain)


def finish(hidden, gain, terms, put=None, arrived=None, scale=1.0):
    rows, width = hidden.shape
    step = rows // 4
    product = () if put is None else (put, arrived)

    def body(hidden_ref, gain_ref, *refs):
        total = refs[0][...].astype(jnp.float32)
        for ref in refs[1 : len(terms)]:
            total += ref[...].astype(jnp.float32)
        if product:
            total += scale * mxu(refs[-3][...], refs[-2][...])
        values = hidden_ref[...].astype(jnp.float32)
        inverse = inverse_norm(values)
        unit_rows = values * inverse
        scaled = total * gain_ref[...]
        inner = jnp.mean(scaled * unit_rows, axis=-1, keepdims=True)
        refs[-1][...] = (inverse * (scaled - unit_rows * inner)).astype(jnp.bfloat16)

    block = pl.BlockSpec((step, width), lambda i: (i, 0))
    extra = []
    if product:
        extra = [pl.BlockSpec((step, put.shape[1]), lambda i: (i, 0)), whole(arrived.shape)]
    return pl.pallas_call(
        body,
        grid=(rows // step,),
        in_specs=[block, whole((1, width))] + [block] * len(terms) + extra,
        out_specs=block,
        out_shape=jax.ShapeDtypeStruct((rows, width), jnp.bfloat16),
        compiler_params=params(20),
        cost_estimate=SMALL,
        name="finish",
    )(hidden, gain, *terms, *product)


def pick_rows(matrix, sources):
    width = sources[0].shape[1]

    def body(matrix_ref, *refs):
        refs[-1][...] = mxu(matrix_ref[...], joined(refs[:-1])).astype(jnp.bfloat16)

    return pl.pallas_call(
        body,
        grid=(width // tile(width),),
        in_specs=[whole(matrix.shape)] + [columns(s.shape[0], width) for s in sources],
        out_specs=columns(matrix.shape[0], width),
        out_shape=jax.ShapeDtypeStruct((matrix.shape[0], width), jnp.bfloat16),
        compiler_params=params(16),
        cost_estimate=SMALL,
        name="pick_rows",
    )(matrix, *sources)


def line_scores(sources, queries, scale):
    width = queries.shape[1]
    steps = width // tile(width)

    def body(query_ref, *refs):
        step = pl.program_id(0)
        out_ref = refs[-1]

        @pl.when(step == 0)
        def _():
            out_ref[...] = jnp.zeros_like(out_ref)

        out_ref[...] += scale * mxu(joined(refs[:-1]), query_ref[...], 1, 1)

    out = (sum(s.shape[0] for s in sources), queries.shape[0])
    return pl.pallas_call(
        body,
        grid=(steps,),
        in_specs=[columns(queries.shape[0], width)]
        + [columns(s.shape[0], width) for s in sources],
        out_specs=whole(out),
        out_shape=jax.ShapeDtypeStruct(out, jnp.float32),
        compiler_params=params(20),
        cost_estimate=SMALL,
        name="line_scores",
    )(queries, *sources)


def far_scores(near, sources, queries, asked_by, line, scale):
    width = queries.shape[1]
    query_count = queries.shape[0]
    steps = width // tile(width)
    near_slots = near.shape[0] - line
    far_slots = asked_by.shape[0] - near_slots

    def body(near_ref, mask_ref, query_ref, *refs):
        out_ref, log_ref = refs[-2:]
        step = pl.program_id(0)

        @pl.when(step == 0)
        def _():
            out_ref[...] = jnp.zeros_like(out_ref)

        out_ref[...] += scale * mxu(joined(refs[:-2]), query_ref[...], 1, 1)

        @pl.when(step == steps - 1)
        def _():
            inner = near_ref[:line, :]
            own = jnp.where(mask_ref[:near_slots, :] > 0, near_ref[line:, :], LOW)
            far = jnp.where(mask_ref[near_slots:, :] > 0, out_ref[...], LOW)
            parts = (inner, own, far)
            top = jnp.max(inner, axis=0, keepdims=True)
            for part in parts[1:]:
                top = jnp.maximum(top, jnp.max(part, axis=0, keepdims=True))
            total = jnp.zeros_like(top)
            for part in parts:
                total += jnp.sum(jnp.exp(part - top), axis=0, keepdims=True)
            log_ref[...] = top + jnp.log(total)

    return pl.pallas_call(
        body,
        grid=(steps,),
        in_specs=[
            whole(near.shape),
            whole(asked_by.shape),
            columns(query_count, width),
        ]
        + [columns(s.shape[0], width) for s in sources],
        out_specs=[whole((far_slots, query_count)), whole((1, query_count))],
        out_shape=[
            jax.ShapeDtypeStruct((far_slots, query_count), jnp.float32),
            jax.ShapeDtypeStruct((1, query_count), jnp.float32),
        ],
        compiler_params=params(28),
        cost_estimate=LARGE,
        name="far_scores",
    )(near, asked_by, queries, *sources)


def query_side(near, far, asked_by, log_total, weight, target, queries, sources, line, scale):
    width = queries.shape[1]
    query_count = queries.shape[0]
    near_slots = near.shape[0] - line
    slot_count = asked_by.shape[0]
    count = len(sources)
    rows = line // RING
    cuts = (line,)

    def body(near_ref, far_ref, mask_ref, log_ref, weight_ref, target_ref, query_ref, *refs):
        source_refs = refs[:count]
        part_ref, gain_ref, slot_ref, positive_ref = refs[count : count + 4]
        coeff_refs, turned_ref = refs[count + 4 : -1], refs[-1]

        @pl.when(pl.program_id(0) == 0)
        def _():
            log_row, weight_row = log_ref[...], weight_ref[...]
            inner = near_ref[:line, :]
            row_place = lax.broadcasted_iota(jnp.int32, inner.shape, 0)
            hit = row_place == target_ref[...]
            positive_ref[...] = jnp.sum(jnp.where(hit, inner, 0.0), axis=0, keepdims=True)
            inner_coeff = weight_row * (jnp.exp(inner - log_row) - jnp.where(hit, 1.0, 0.0))
            at = 0
            for coeff_ref, size in zip(coeff_refs, cuts):
                coeff_ref[...] = inner_coeff[at : at + size].astype(jnp.bfloat16)
                at += size
            own = jnp.where(mask_ref[:near_slots, :] > 0, near_ref[line:, :], LOW)
            slots = jnp.where(mask_ref[near_slots:, :] > 0, far_ref[...], LOW)
            own_coeff = (weight_row * jnp.exp(own - log_row)).astype(jnp.bfloat16)
            far_coeff = (weight_row * jnp.exp(slots - log_row)).astype(jnp.bfloat16)
            ones = jnp.ones((8, query_count), jnp.bfloat16)
            slot_ref[:, :near_slots] = mxu(ones, own_coeff, 1, 1)
            slot_ref[:, near_slots:] = mxu(ones, far_coeff, 1, 1)
            turned_ref[:, :line] = jnp.transpose(inner_coeff).astype(jnp.bfloat16)
            turned_ref[:, line : line + near_slots] = jnp.transpose(
                own_coeff.astype(jnp.float32)
            ).astype(jnp.bfloat16)
            turned_ref[:, line + near_slots :] = jnp.transpose(
                far_coeff.astype(jnp.float32)
            ).astype(jnp.bfloat16)

        total = scale * mxu(turned_ref[...], joined(source_refs))
        part_ref[...] = total.astype(jnp.bfloat16)
        gain_ref[...] = jnp.sum(total * query_ref[...].astype(jnp.float32), axis=0, keepdims=True)

    row = whole((1, query_count))
    return pl.pallas_call(
        body,
        grid=(width // tile(width),),
        in_specs=[
            whole(near.shape),
            whole(far.shape),
            whole(asked_by.shape),
            row,
            row,
            row,
            columns(query_count, width),
        ]
        + [columns(s.shape[0], width) for s in sources],
        out_specs=[
            columns(query_count, width),
            columns(1, width),
            whole((8, slot_count)),
            row,
        ]
        + [whole((size, query_count)) for size in cuts],
        out_shape=[
            jax.ShapeDtypeStruct((query_count, width), jnp.bfloat16),
            jax.ShapeDtypeStruct((1, width), jnp.float32),
            jax.ShapeDtypeStruct((8, slot_count), jnp.float32),
            jax.ShapeDtypeStruct((1, query_count), jnp.float32),
        ]
        + [jax.ShapeDtypeStruct((size, query_count), jnp.bfloat16) for size in cuts],
        scratch_shapes=[pltpu.VMEM((query_count, line + slot_count), jnp.bfloat16)],
        compiler_params=params(32),
        cost_estimate=SMALL,
        name="query_side",
    )(near, far, asked_by, log_total, weight, target, queries, *sources)


def passage_side(coeff, queries, put, arrived, scale, layout):
    width = queries.shape[1]
    sizes = [sum(high - low for low, high in ranges) for ranges in layout]
    own = coeff.shape[0] - put.shape[0]

    def body(coeff_ref, query_ref, put_ref, arrived_ref, own_ref, *out_refs):
        total = mxu(coeff_ref[own:], query_ref[...]) + mxu(put_ref[...], arrived_ref[...])
        total = (scale * total).astype(jnp.bfloat16)
        for ranges, out_ref in zip(layout, out_refs):
            at = 0
            for low, high in ranges:
                out_ref[at : at + high - low] = total[low:high]
                at += high - low
        own_ref[...] = scale * mxu(coeff_ref[:own], query_ref[...])

    return pl.pallas_call(
        body,
        grid=(width // tile(width),),
        in_specs=[
            whole(coeff.shape),
            columns(queries.shape[0], width),
            whole(put.shape),
            columns(arrived.shape[0], width),
        ],
        out_specs=[columns(own, width)] + [columns(size, width) for size in sizes],
        out_shape=[jax.ShapeDtypeStruct((own, width), jnp.float32)]
        + [jax.ShapeDtypeStruct((size, width), jnp.bfloat16) for size in sizes],
        compiler_params=params(20),
        cost_estimate=LARGE,
        name="passage_side",
    )(coeff, queries, put, arrived)


def add_passing(up, passing_low, down, passing_high):
    half, width = passing_low.shape
    rows = 2 * half

    def body(up_ref, low_ref, down_ref, high_ref, up_out, down_out):
        wide = jnp.float32
        up_out[:half] = (up_ref[:half].astype(wide) + low_ref[...].astype(wide)).astype(up.dtype)
        up_out[half:] = up_ref[half:]
        down_out[:half] = down_ref[:half]
        down_out[half:] = (down_ref[half:].astype(wide) + high_ref[...].astype(wide)).astype(
            up.dtype
        )

    return pl.pallas_call(
        body,
        grid=(width // tile(width),),
        in_specs=[
            columns(rows, width),
            columns(half, width),
            columns(rows, width),
            columns(half, width),
        ],
        out_specs=[columns(rows, width)] * 2,
        out_shape=[jax.ShapeDtypeStruct(up.shape, up.dtype)] * 2,
        compiler_params=params(12),
        cost_estimate=SMALL,
        name="add_passing",
    )(up, passing_low, down, passing_high)


def on_device(query_hidden, passage_hidden, norm_gain, query_weight, hneg_ids):
    rows, width = query_hidden.shape
    neg_count = hneg_ids.shape[1]
    z_count = lax.axis_size("z")
    group_count = 2 * z_count
    line = RING * rows
    scale = 1.0 / (SOFTMAX_TEMPER * math.sqrt(width))
    y_place, x_place = lax.axis_index("y"), lax.axis_index("x")

    gain = norm_gain.reshape(1, width)
    p_own = embed(passage_hidden, gain)
    p_mid, p_opp = ring_gather(p_own, "y")

    flat_ids = hneg_ids.reshape(-1)
    id_count = rows * neg_count
    owners = flat_ids // rows
    local_row = flat_ids % rows
    number = jnp.arange(id_count, dtype=jnp.int32)
    same = (owners[:, None] == owners[None, :]) & (number[None, :] < number[:, None])
    rank = jnp.sum(same.astype(jnp.int32), axis=1)
    y_step = (owners // RING - y_place) % RING
    line_of = (owners // (RING * RING)) * RING + owners % RING
    slot = (line_of * RING + y_step) * CAP + rank
    slot_count = group_count * RING * RING * CAP
    hit = slot[None, :] == jnp.arange(slot_count, dtype=jnp.int32)[:, None]
    slot_row = jnp.sum(jnp.where(hit, local_row[None, :] + 1, 0), axis=1) - 1
    slot_query = jnp.sum(jnp.where(hit, number[None, :] // neg_count + 1, 0), axis=1)
    asked = lax.all_to_all(
        slot_row.reshape(group_count * RING, RING * CAP), ("z", "c", "x"), 0, 0, tiled=True
    )
    asked = asked.reshape(group_count, RING, RING, CAP).transpose(0, 2, 1, 3)
    place = jnp.arange(line, dtype=jnp.int32)
    asked, _ = lax.optimization_barrier((asked, p_mid))
    asked_own = asked[:, 0].reshape(-1)
    above = jnp.where(asked[:, 3:] < 0, -1, asked[:, 3:] + rows)
    opposite = jnp.where(asked[:, 2:3] < 0, -1, asked[:, 2:3] + 2 * rows)
    asked_far = jnp.concatenate([asked[:, 1:2], above, opposite], axis=1).reshape(-1)

    def one_hot(numbers, size):
        return (numbers[:, None] == place[None, :size]).astype(jnp.bfloat16)

    chosen_own = pick_rows(one_hot(asked_own, rows), [p_own])
    hard_own = group_rows(chosen_own, group_count)
    chosen_far = pick_rows(one_hot(asked_far, 3 * rows), [*p_mid, *p_opp])
    hard_far = group_rows(chosen_far, group_count)

    q_emb = embed(query_hidden, gain)
    q_line = lax.all_gather(q_emb, "x", axis=0, tiled=True)

    by_x = slot_query.reshape(group_count, RING, RING * CAP).transpose(1, 0, 2)
    asker = line_table(by_x.reshape(RING, -1)).reshape(RING, group_count, RING, CAP)
    x_base = rows * jnp.arange(RING, dtype=jnp.int32)
    asker = jnp.where(asker == 0, -1, asker - 1 + x_base[:, None, None, None])
    asker = asker.transpose(1, 2, 0, 3)
    far_asker = jnp.concatenate([asker[:, 1:2], asker[:, 3:], asker[:, 2:3]], axis=1)
    send_own = one_hot(asker[:, 0].reshape(-1), line)
    send_far = one_hot(far_asker.reshape(-1), line)
    asked_by = jnp.concatenate([send_own, send_far], axis=0)
    leave_far = pick_rows(send_far, [q_line])
    leave_own = pick_rows(send_own, [q_line])
    q_line, leave_far, leave_own = lax.optimization_barrier((q_line, leave_far, leave_own))
    far_queries = group_rows(leave_far, group_count)
    own_queries = group_rows(leave_own, group_count)

    near = line_scores([p_own, *p_mid, *p_opp, hard_own], q_line, scale)
    far, part_log = far_scores(near, [hard_far], q_line, asked_by, line, scale)
    part_log = part_log.reshape(RING, rows)
    own_place = jnp.arange(RING, dtype=jnp.int32)[:, None] == x_place
    own_weight = jnp.where(own_place, query_weight[None, :], 0.0)
    message = jnp.concatenate([part_log, own_weight], axis=0)
    messages = [message] + [shift(message, "x", step) for step in (1, 3, 2)]
    logs = [m[:RING] for m in messages]
    weight = sum(m[RING:] for m in messages).reshape(1, line)
    top = jnp.maximum(jnp.maximum(logs[0], logs[1]), jnp.maximum(logs[2], logs[3]))
    log_total = (top + jnp.log(sum(jnp.exp(part - top) for part in logs))).reshape(1, line)
    first_row = x_place * rows
    target = place[None, :] - first_row
    target = jnp.where((target >= 0) & (target < rows), target, -1)

    part, gain_part, slot_coeff, positive, coeff = query_side(
        near, far, asked_by, log_total, weight, target, q_line,
        [p_own, *p_mid, *p_opp, hard_own, hard_far], line, scale,
    )
    loss_rows = lax.dynamic_slice(log_total - positive, (0, first_row), (1, rows)).reshape(-1)
    query_up = lax.psum_scatter(part, "x", scatter_dimension=0, tiled=True)
    query_grad = finish(query_hidden, gain, [query_up])

    own_end = group_count * RING * CAP
    pieces = (
        slot_coeff[0, :own_end].reshape(group_count, -1),
        slot_coeff[0, own_end:].reshape(group_count, -1),
    )
    got_coeff = group_table(jnp.concatenate(pieces, axis=1), group_count)
    first = RING * CAP

    def put_rows(numbers, values, size):
        return jnp.where(
            place[:size, None] == numbers[None, :], values.reshape(-1)[None, :], 0.0
        ).astype(jnp.bfloat16)

    put_own = put_rows(asked_own, got_coeff[:, :first], rows)
    put_far = put_rows(asked_far, got_coeff[:, first:], 3 * rows)
    half = rows // 2
    low_1, high_1, low_3, high_3, low_2, high_2 = [(i * half, (i + 1) * half) for i in range(6)]
    own_part, for_above, for_below, pass_up, pass_down = passage_side(
        coeff, q_line, put_far, far_queries, scale,
        [[low_1, high_1], [low_3, high_3], [low_2], [high_2]],
    )
    passing_low = shift(pass_up, "y", 1)
    passing_high = shift(pass_down, "y", -1)
    gain_part = pair_sum(pair_sum(gain_part.reshape(-1, 128), "z", False), "z", True)
    gain_part, passing_low = lax.optimization_barrier((gain_part, passing_low))
    for_above, for_below = add_passing(for_above, passing_low, for_below, passing_high)
    from_below = shift(for_above, "y", 1)
    from_above = shift(for_below, "y", -1)
    gain_part, _ = lax.optimization_barrier((gain_part, for_above))
    gain_part = pair_sum(gain_part, "c", False)
    gain_part = pair_sum(pair_sum(gain_part, "x", False), "x", True)
    gain_part, query_grad = lax.optimization_barrier((gain_part, query_grad))
    gain_part = pair_sum(pair_sum(gain_part, "y", False), "y", True)
    gain_grad = 2.0 * gain_part.reshape(-1) / norm_gain
    passage_grad = finish(
        passage_hidden, gain, [own_part, from_below, from_above], put_own, own_queries, scale
    )
    return (loss_rows, query_grad, passage_grad, gain_grad)


def solution(mesh):
    torus = Mesh(mesh.devices.reshape(-1, 2, RING, RING), ALL_AXES)
    return jax.shard_map(
        on_device,
        mesh=torus,
        in_specs=(
            P(ALL_AXES, None),
            P(ALL_AXES, None),
            P(),
            P(ALL_AXES),
            P(ALL_AXES, None),
        ),
        out_specs=(
            P(ALL_AXES),
            P(ALL_AXES, None),
            P(ALL_AXES, None),
            P(),
        ),
        check_vma=False,
    )
```

```python
import math

import jax
import jax.numpy as jnp
from jax import lax
from jax.experimental import pallas as pl
from jax.experimental.pallas import tpu as pltpu
from jax.sharding import Mesh, PartitionSpec as P

EPSILON = 1e-06
SOFTMAX_TEMPER = 0.28
RING = 4
CAP = 4
GROUPS = ("z", "c")
ALL_AXES = ("z", "c", "y", "x")
MIB = 1024 * 1024
LOW = -1e30


def shift(value, axis, step):
    return lax.ppermute(value, axis, [(i, (i + step) % RING) for i in range(RING)])


def ring_gather(low, high, axis):
    up_low = shift(low, axis, -1)
    down_high = shift(high, axis, 1)
    up_more = shift(jnp.concatenate([high, up_low], axis=0), axis, -1)
    down_more = shift(jnp.concatenate([low, down_high], axis=0), axis, 1)
    return [up_low, up_more, down_more, down_high]


def pair_sum(value, axis, turn):
    size = lax.axis_size(axis)
    pairs = [(i, size - 1 - i if turn else i ^ 1) for i in range(size)]
    return value + lax.ppermute(value, axis, pairs)


def group_rows(rows, group_count):
    blocks = rows.reshape(group_count, rows.shape[0] // group_count, rows.shape[1])
    return lax.all_to_all(blocks, GROUPS, 0, 0, tiled=True).reshape(rows.shape)


def group_table(table, group_count):
    z_count = group_count // 2
    z_place, c_place = lax.axis_index("z"), lax.axis_index("c")
    got = jnp.zeros_like(table)
    places = jnp.arange(group_count, dtype=jnp.int32)[:, None]
    for z_step in range(z_count):
        for c_step in range(2):
            to_group = ((z_place + z_step) % z_count) * 2 + (c_place ^ c_step)
            from_group = ((z_place + z_count - z_step) % z_count) * 2 + (c_place ^ c_step)
            row = jnp.sum(jnp.where(places == to_group, table, 0), axis=0, keepdims=True)
            if z_step or c_step:
                row = lax.ppermute(
                    row,
                    GROUPS,
                    [
                        (z * 2 + c, ((z + z_step) % z_count) * 2 + (c ^ c_step))
                        for z in range(z_count)
                        for c in range(2)
                    ],
                )
            got = got + jnp.where(places == from_group, row, 0)
    return got


def line_table(table):
    x_place = lax.axis_index("x")
    places = jnp.arange(RING, dtype=jnp.int32)[:, None]
    got = jnp.where(places == x_place, table, 0)
    for step in range(1, RING):
        chosen = places == (x_place + step) % RING
        row = jnp.sum(jnp.where(chosen, table, 0), axis=0, keepdims=True)
        row = shift(row, "x", step)
        got = got + jnp.where(places == (x_place + RING - step) % RING, row, 0)
    return got


def mxu(left, right, left_dim=1, right_dim=0):
    return lax.dot_general(
        left, right, (((left_dim,), (right_dim,)), ((), ())), preferred_element_type=jnp.float32
    )


def params(mib):
    return pltpu.CompilerParams(dimension_semantics=("arbitrary",), vmem_limit_bytes=mib * MIB)


SMALL = pl.CostEstimate(flops=1, bytes_accessed=1, transcendentals=0)
LARGE = pl.CostEstimate(flops=10**11, bytes_accessed=10**8, transcendentals=0)


def tile(width):
    return min(1024, width)


def whole(shape):
    return pl.BlockSpec(shape, lambda i: (0,) * len(shape))


def columns(rows, width):
    return pl.BlockSpec((rows, tile(width)), lambda i: (0, i))


def joined(refs):
    blocks = [ref[...] for ref in refs]
    return blocks[0] if len(blocks) == 1 else jnp.concatenate(blocks, axis=0)


def inverse_norm(values):
    return lax.rsqrt(jnp.mean(values * values, axis=-1, keepdims=True) + EPSILON)


def embed(hidden, gain, pieces):
    def body(hidden_ref, gain_ref, *out_refs):
        values = hidden_ref[...].astype(jnp.float32)
        unit_rows = values * inverse_norm(values)
        rounded_rows = (unit_rows * gain_ref[...]).astype(jnp.bfloat16)
        for i, out_ref in enumerate(out_refs):

            @pl.when(pl.program_id(0) // per_piece == i)
            def _(out_ref=out_ref):
                out_ref[...] = rounded_rows

    rows, width = hidden.shape
    step = min(32, rows // pieces)
    per_piece = rows // pieces // step
    block = pl.BlockSpec((step, width), lambda i: (i, 0))

    def piece(at):
        return pl.BlockSpec(
            (step, width), lambda i: (jnp.clip(i - at * per_piece, 0, per_piece - 1), 0)
        )

    return pl.pallas_call(
        body,
        grid=(rows // step,),
        in_specs=[block, whole((1, width))],
        out_specs=[piece(at) for at in range(pieces)],
        out_shape=[jax.ShapeDtypeStruct((rows // pieces, width), jnp.bfloat16)] * pieces,
        compiler_params=params(12),
        cost_estimate=SMALL,
        name="embed",
    )(hidden, gain)


def finish(hidden, gain, terms, put=None, arrived=None, scale=1.0):
    rows, width = hidden.shape
    step = rows // 4
    product = () if put is None else (put, arrived)

    def body(hidden_ref, gain_ref, *refs):
        total = refs[0][...].astype(jnp.float32)
        for ref in refs[1 : len(terms)]:
            total += ref[...].astype(jnp.float32)
        if product:
            total += scale * mxu(refs[-3][...], refs[-2][...])
        values = hidden_ref[...].astype(jnp.float32)
        inverse = inverse_norm(values)
        unit_rows = values * inverse
        scaled = total * gain_ref[...]
        inner = jnp.mean(scaled * unit_rows, axis=-1, keepdims=True)
        refs[-1][...] = (inverse * (scaled - unit_rows * inner)).astype(jnp.bfloat16)

    block = pl.BlockSpec((step, width), lambda i: (i, 0))
    extra = []
    if product:
        extra = [pl.BlockSpec((step, put.shape[1]), lambda i: (i, 0)), whole(arrived.shape)]
    return pl.pallas_call(
        body,
        grid=(rows // step,),
        in_specs=[block, whole((1, width))] + [block] * len(terms) + extra,
        out_specs=block,
        out_shape=jax.ShapeDtypeStruct((rows, width), jnp.bfloat16),
        compiler_params=params(20),
        cost_estimate=SMALL,
        name="finish",
    )(hidden, gain, *terms, *product)


def pick_rows(matrix, sources):
    width = sources[0].shape[1]

    def body(matrix_ref, *refs):
        refs[-1][...] = mxu(matrix_ref[...], joined(refs[:-1])).astype(jnp.bfloat16)

    return pl.pallas_call(
        body,
        grid=(width // tile(width),),
        in_specs=[whole(matrix.shape)] + [columns(s.shape[0], width) for s in sources],
        out_specs=columns(matrix.shape[0], width),
        out_shape=jax.ShapeDtypeStruct((matrix.shape[0], width), jnp.bfloat16),
        compiler_params=params(16),
        cost_estimate=SMALL,
        name="pick_rows",
    )(matrix, *sources)


def line_scores(sources, queries, scale):
    width = queries.shape[1]
    steps = width // tile(width)

    def body(query_ref, *refs):
        step = pl.program_id(0)
        out_ref = refs[-1]

        @pl.when(step == 0)
        def _():
            out_ref[...] = jnp.zeros_like(out_ref)

        out_ref[...] += scale * mxu(joined(refs[:-1]), query_ref[...], 1, 1)

    out = (sum(s.shape[0] for s in sources), queries.shape[0])
    return pl.pallas_call(
        body,
        grid=(steps,),
        in_specs=[columns(queries.shape[0], width)]
        + [columns(s.shape[0], width) for s in sources],
        out_specs=whole(out),
        out_shape=jax.ShapeDtypeStruct(out, jnp.float32),
        compiler_params=params(20),
        cost_estimate=SMALL,
        name="line_scores",
    )(queries, *sources)


def far_scores(near, sources, queries, asked_by, line, scale):
    width = queries.shape[1]
    query_count = queries.shape[0]
    steps = width // tile(width)
    near_slots = near.shape[0] - line
    far_slots = asked_by.shape[0] - near_slots

    def body(near_ref, mask_ref, query_ref, *refs):
        out_ref, log_ref = refs[-2:]
        step = pl.program_id(0)

        @pl.when(step == 0)
        def _():
            out_ref[...] = jnp.zeros_like(out_ref)

        out_ref[...] += scale * mxu(joined(refs[:-2]), query_ref[...], 1, 1)

        @pl.when(step == steps - 1)
        def _():
            inner = near_ref[:line, :]
            own = jnp.where(mask_ref[:near_slots, :] > 0, near_ref[line:, :], LOW)
            far = jnp.where(mask_ref[near_slots:, :] > 0, out_ref[...], LOW)
            parts = (inner, own, far)
            top = jnp.max(inner, axis=0, keepdims=True)
            for part in parts[1:]:
                top = jnp.maximum(top, jnp.max(part, axis=0, keepdims=True))
            total = jnp.zeros_like(top)
            for part in parts:
                total += jnp.sum(jnp.exp(part - top), axis=0, keepdims=True)
            log_ref[...] = top + jnp.log(total)

    return pl.pallas_call(
        body,
        grid=(steps,),
        in_specs=[
            whole(near.shape),
            whole(asked_by.shape),
            columns(query_count, width),
        ]
        + [columns(s.shape[0], width) for s in sources],
        out_specs=[whole((far_slots, query_count)), whole((1, query_count))],
        out_shape=[
            jax.ShapeDtypeStruct((far_slots, query_count), jnp.float32),
            jax.ShapeDtypeStruct((1, query_count), jnp.float32),
        ],
        compiler_params=params(28),
        cost_estimate=LARGE,
        name="far_scores",
    )(near, asked_by, queries, *sources)


def query_side(near, far, asked_by, log_total, weight, target, queries, sources, line, scale):
    width = queries.shape[1]
    query_count = queries.shape[0]
    near_slots = near.shape[0] - line
    slot_count = asked_by.shape[0]
    count = len(sources)
    rows = line // RING
    cuts = (line,)

    def body(near_ref, far_ref, mask_ref, log_ref, weight_ref, target_ref, query_ref, *refs):
        source_refs = refs[:count]
        part_ref, gain_ref, slot_ref, positive_ref = refs[count : count + 4]
        coeff_refs, turned_ref = refs[count + 4 : -1], refs[-1]

        @pl.when(pl.program_id(0) == 0)
        def _():
            log_row, weight_row = log_ref[...], weight_ref[...]
            inner = near_ref[:line, :]
            row_place = lax.broadcasted_iota(jnp.int32, inner.shape, 0)
            hit = row_place == target_ref[...]
            positive_ref[...] = jnp.sum(jnp.where(hit, inner, 0.0), axis=0, keepdims=True)
            inner_coeff = weight_row * (jnp.exp(inner - log_row) - jnp.where(hit, 1.0, 0.0))
            at = 0
            for coeff_ref, size in zip(coeff_refs, cuts):
                coeff_ref[...] = inner_coeff[at : at + size].astype(jnp.bfloat16)
                at += size
            own = jnp.where(mask_ref[:near_slots, :] > 0, near_ref[line:, :], LOW)
            slots = jnp.where(mask_ref[near_slots:, :] > 0, far_ref[...], LOW)
            own_coeff = (weight_row * jnp.exp(own - log_row)).astype(jnp.bfloat16)
            far_coeff = (weight_row * jnp.exp(slots - log_row)).astype(jnp.bfloat16)
            ones = jnp.ones((8, query_count), jnp.bfloat16)
            slot_ref[:, :near_slots] = mxu(ones, own_coeff, 1, 1)
            slot_ref[:, near_slots:] = mxu(ones, far_coeff, 1, 1)
            turned_ref[:, :line] = jnp.transpose(inner_coeff).astype(jnp.bfloat16)
            turned_ref[:, line : line + near_slots] = jnp.transpose(
                own_coeff.astype(jnp.float32)
            ).astype(jnp.bfloat16)
            turned_ref[:, line + near_slots :] = jnp.transpose(
                far_coeff.astype(jnp.float32)
            ).astype(jnp.bfloat16)

        total = scale * mxu(turned_ref[...], joined(source_refs))
        part_ref[...] = total.astype(jnp.bfloat16)
        gain_ref[...] = jnp.sum(total * query_ref[...].astype(jnp.float32), axis=0, keepdims=True)

    row = whole((1, query_count))
    return pl.pallas_call(
        body,
        grid=(width // tile(width),),
        in_specs=[
            whole(near.shape),
            whole(far.shape),
            whole(asked_by.shape),
            row,
            row,
            row,
            columns(query_count, width),
        ]
        + [columns(s.shape[0], width) for s in sources],
        out_specs=[
            columns(query_count, width),
            columns(1, width),
            whole((8, slot_count)),
            row,
        ]
        + [whole((size, query_count)) for size in cuts],
        out_shape=[
            jax.ShapeDtypeStruct((query_count, width), jnp.bfloat16),
            jax.ShapeDtypeStruct((1, width), jnp.float32),
            jax.ShapeDtypeStruct((8, slot_count), jnp.float32),
            jax.ShapeDtypeStruct((1, query_count), jnp.float32),
        ]
        + [jax.ShapeDtypeStruct((size, query_count), jnp.bfloat16) for size in cuts],
        scratch_shapes=[pltpu.VMEM((query_count, line + slot_count), jnp.bfloat16)],
        compiler_params=params(32),
        cost_estimate=SMALL,
        name="query_side",
    )(near, far, asked_by, log_total, weight, target, queries, *sources)


def passage_side(coeff, queries, put, arrived, scale, layout):
    width = queries.shape[1]
    sizes = [sum(high - low for low, high in ranges) for ranges in layout]
    own = coeff.shape[0] - put.shape[0]

    def body(coeff_ref, query_ref, put_ref, arrived_ref, own_ref, *out_refs):
        total = mxu(coeff_ref[own:], query_ref[...]) + mxu(put_ref[...], arrived_ref[...])
        total = (scale * total).astype(jnp.bfloat16)
        for ranges, out_ref in zip(layout, out_refs):
            at = 0
            for low, high in ranges:
                out_ref[at : at + high - low] = total[low:high]
                at += high - low
        own_ref[...] = scale * mxu(coeff_ref[:own], query_ref[...])

    return pl.pallas_call(
        body,
        grid=(width // tile(width),),
        in_specs=[
            whole(coeff.shape),
            columns(queries.shape[0], width),
            whole(put.shape),
            columns(arrived.shape[0], width),
        ],
        out_specs=[columns(own, width)] + [columns(size, width) for size in sizes],
        out_shape=[jax.ShapeDtypeStruct((own, width), jnp.float32)]
        + [jax.ShapeDtypeStruct((size, width), jnp.bfloat16) for size in sizes],
        compiler_params=params(20),
        cost_estimate=LARGE,
        name="passage_side",
    )(coeff, queries, put, arrived)


def add_passing(up, passing_low, down, passing_high):
    half, width = passing_low.shape
    rows = 2 * half

    def body(up_ref, low_ref, down_ref, high_ref, up_out, down_out):
        wide = jnp.float32
        up_out[:half] = (up_ref[:half].astype(wide) + low_ref[...].astype(wide)).astype(up.dtype)
        up_out[half:] = up_ref[half:]
        down_out[:half] = down_ref[:half]
        down_out[half:] = (down_ref[half:].astype(wide) + high_ref[...].astype(wide)).astype(
            up.dtype
        )

    return pl.pallas_call(
        body,
        grid=(width // tile(width),),
        in_specs=[
            columns(rows, width),
            columns(half, width),
            columns(rows, width),
            columns(half, width),
        ],
        out_specs=[columns(rows, width)] * 2,
        out_shape=[jax.ShapeDtypeStruct(up.shape, up.dtype)] * 2,
        compiler_params=params(12),
        cost_estimate=SMALL,
        name="add_passing",
    )(up, passing_low, down, passing_high)


def on_device(query_hidden, passage_hidden, norm_gain, query_weight, hneg_ids):
    rows, width = query_hidden.shape
    neg_count = hneg_ids.shape[1]
    z_count = lax.axis_size("z")
    group_count = 2 * z_count
    line = RING * rows
    scale = 1.0 / (SOFTMAX_TEMPER * math.sqrt(width))
    y_place, x_place = lax.axis_index("y"), lax.axis_index("x")

    gain = norm_gain.reshape(1, width)
    p_own = embed(passage_hidden, gain, 2)
    p_far = ring_gather(*p_own, "y")

    flat_ids = hneg_ids.reshape(-1)
    id_count = rows * neg_count
    owners = flat_ids // rows
    local_row = flat_ids % rows
    number = jnp.arange(id_count, dtype=jnp.int32)
    same = (owners[:, None] == owners[None, :]) & (number[None, :] < number[:, None])
    rank = jnp.sum(same.astype(jnp.int32), axis=1)
    y_step = (owners // RING - y_place) % RING
    line_of = (owners // (RING * RING)) * RING + owners % RING
    slot = (line_of * RING + y_step) * CAP + rank
    slot_count = group_count * RING * RING * CAP
    hit = slot[None, :] == jnp.arange(slot_count, dtype=jnp.int32)[:, None]
    slot_row = jnp.sum(jnp.where(hit, local_row[None, :] + 1, 0), axis=1) - 1
    slot_query = jnp.sum(jnp.where(hit, number[None, :] // neg_count + 1, 0), axis=1)
    asked = lax.all_to_all(
        slot_row.reshape(group_count * RING, RING * CAP), ("z", "c", "x"), 0, 0, tiled=True
    )
    asked = asked.reshape(group_count, RING, RING, CAP).transpose(0, 2, 1, 3)
    place = jnp.arange(line, dtype=jnp.int32)
    asked, _ = lax.optimization_barrier((asked, [p_far[0], p_far[-1]]))
    asked_own = asked[:, 0].reshape(-1)
    half = rows // 2

    def moved(block, base):
        return jnp.where(block < 0, -1, block + base + jnp.where(block >= half, half, 0))

    asked_far = jnp.concatenate(
        [asked[:, 1:2], moved(asked[:, 3:], rows + half), moved(asked[:, 2:3], rows)], axis=1
    ).reshape(-1)

    def one_hot(numbers, size):
        return (numbers[:, None] == place[None, :size]).astype(jnp.bfloat16)

    chosen_own = pick_rows(one_hot(asked_own, rows), p_own)
    hard_own = group_rows(chosen_own, group_count)
    chosen_far = pick_rows(one_hot(asked_far, 3 * rows), p_far)
    hard_far = group_rows(chosen_far, group_count)

    q_emb = embed(query_hidden, gain, 1)[0]
    q_line = lax.all_gather(q_emb, "x", axis=0, tiled=True)

    by_x = slot_query.reshape(group_count, RING, RING * CAP).transpose(1, 0, 2)
    asker = line_table(by_x.reshape(RING, -1)).reshape(RING, group_count, RING, CAP)
    x_base = rows * jnp.arange(RING, dtype=jnp.int32)
    asker = jnp.where(asker == 0, -1, asker - 1 + x_base[:, None, None, None])
    asker = asker.transpose(1, 2, 0, 3)
    far_asker = jnp.concatenate([asker[:, 1:2], asker[:, 3:], asker[:, 2:3]], axis=1)
    send_own = one_hot(asker[:, 0].reshape(-1), line)
    send_far = one_hot(far_asker.reshape(-1), line)
    asked_by = jnp.concatenate([send_own, send_far], axis=0)
    leave_far = pick_rows(send_far, [q_line])
    leave_own = pick_rows(send_own, [q_line])
    q_line, leave_far, leave_own = lax.optimization_barrier((q_line, leave_far, leave_own))
    far_queries = group_rows(leave_far, group_count)
    own_queries = group_rows(leave_own, group_count)

    near = line_scores([*p_own, *p_far, hard_own], q_line, scale)
    far, part_log = far_scores(near, [hard_far], q_line, asked_by, line, scale)
    part_log = part_log.reshape(RING, rows)
    own_place = jnp.arange(RING, dtype=jnp.int32)[:, None] == x_place
    own_weight = jnp.where(own_place, query_weight[None, :], 0.0)
    message = jnp.concatenate([part_log, own_weight], axis=0)
    messages = [message] + [shift(message, "x", step) for step in (1, 3, 2)]
    logs = [m[:RING] for m in messages]
    weight = sum(m[RING:] for m in messages).reshape(1, line)
    top = jnp.maximum(jnp.maximum(logs[0], logs[1]), jnp.maximum(logs[2], logs[3]))
    log_total = (top + jnp.log(sum(jnp.exp(part - top) for part in logs))).reshape(1, line)
    first_row = x_place * rows
    target = place[None, :] - first_row
    target = jnp.where((target >= 0) & (target < rows), target, -1)

    part, gain_part, slot_coeff, positive, coeff = query_side(
        near, far, asked_by, log_total, weight, target, q_line,
        [*p_own, *p_far, hard_own, hard_far], line, scale,
    )
    loss_rows = lax.dynamic_slice(log_total - positive, (0, first_row), (1, rows)).reshape(-1)
    query_up = lax.psum_scatter(part, "x", scatter_dimension=0, tiled=True)
    query_grad = finish(query_hidden, gain, [query_up])

    own_end = group_count * RING * CAP
    pieces = (
        slot_coeff[0, :own_end].reshape(group_count, -1),
        slot_coeff[0, own_end:].reshape(group_count, -1),
    )
    got_coeff = group_table(jnp.concatenate(pieces, axis=1), group_count)
    first = RING * CAP

    def put_rows(numbers, values, size):
        return jnp.where(
            place[:size, None] == numbers[None, :], values.reshape(-1)[None, :], 0.0
        ).astype(jnp.bfloat16)

    put_own = put_rows(asked_own, got_coeff[:, :first], rows)
    put_far = put_rows(asked_far, got_coeff[:, first:], 3 * rows)
    low_1, high_1, low_2, low_3, high_2, high_3 = [(i * half, (i + 1) * half) for i in range(6)]
    own_part, for_above, for_below, pass_up, pass_down = passage_side(
        coeff, q_line, put_far, far_queries, scale,
        [[low_1, high_1], [low_3, high_3], [low_2], [high_2]],
    )
    passing_low = shift(pass_up, "y", 1)
    passing_high = shift(pass_down, "y", -1)
    gain_part = pair_sum(pair_sum(gain_part.reshape(-1, 128), "z", False), "z", True)
    gain_part, passing_low = lax.optimization_barrier((gain_part, passing_low))
    for_above, for_below = add_passing(for_above, passing_low, for_below, passing_high)
    from_below = shift(for_above, "y", 1)
    from_above = shift(for_below, "y", -1)
    gain_part, _ = lax.optimization_barrier((gain_part, for_above))
    gain_part = pair_sum(gain_part, "c", False)
    gain_part = pair_sum(pair_sum(gain_part, "x", False), "x", True)
    gain_part, query_grad = lax.optimization_barrier((gain_part, query_grad))
    gain_part = pair_sum(pair_sum(gain_part, "y", False), "y", True)
    gain_grad = 2.0 * gain_part.reshape(-1) / norm_gain
    passage_grad = finish(
        passage_hidden, gain, [own_part, from_below, from_above], put_own, own_queries, scale
    )
    return (loss_rows, query_grad, passage_grad, gain_grad)


def solution(mesh):
    torus = Mesh(mesh.devices.reshape(-1, 2, RING, RING), ALL_AXES)
    return jax.shard_map(
        on_device,
        mesh=torus,
        in_specs=(
            P(ALL_AXES, None),
            P(ALL_AXES, None),
            P(),
            P(ALL_AXES),
            P(ALL_AXES, None),
        ),
        out_specs=(
            P(ALL_AXES),
            P(ALL_AXES, None),
            P(ALL_AXES, None),
            P(),
        ),
        check_vma=False,
    )
```

```python
import math

import jax
import jax.numpy as jnp
from jax import lax
from jax.experimental import pallas as pl
from jax.experimental.pallas import tpu as pltpu
from jax.sharding import Mesh, PartitionSpec as P

EPSILON = 1e-06
SOFTMAX_TEMPER = 0.28
RING = 4
CAP = 4
GROUPS = ("z", "c")
ALL_AXES = ("z", "c", "y", "x")
MIB = 1024 * 1024
LOW = -1e30


def shift(value, axis, step):
    return lax.ppermute(value, axis, [(i, (i + step) % RING) for i in range(RING)])


def ring_gather(low, high, axis):
    up_low = shift(low, axis, -1)
    down_high = shift(high, axis, 1)
    to_below = jnp.concatenate([high, up_low], axis=0)
    to_above = jnp.concatenate([low, down_high], axis=0)
    up_more = shift(to_below, axis, -1)
    down_more = shift(to_above, axis, 1)
    return [up_low, up_more, down_more, down_high], [to_below, to_above]


def pair_sum(value, axis, turn):
    size = lax.axis_size(axis)
    pairs = [(i, size - 1 - i if turn else i ^ 1) for i in range(size)]
    return value + lax.ppermute(value, axis, pairs)


def group_rows(rows, group_count):
    blocks = rows.reshape(group_count, rows.shape[0] // group_count, rows.shape[1])
    return lax.all_to_all(blocks, GROUPS, 0, 0, tiled=True).reshape(rows.shape)


def group_table(table, group_count):
    z_count = group_count // 2
    z_place, c_place = lax.axis_index("z"), lax.axis_index("c")
    got = jnp.zeros_like(table)
    places = jnp.arange(group_count, dtype=jnp.int32)[:, None]
    for z_step in range(z_count):
        for c_step in range(2):
            to_group = ((z_place + z_step) % z_count) * 2 + (c_place ^ c_step)
            from_group = ((z_place + z_count - z_step) % z_count) * 2 + (c_place ^ c_step)
            row = jnp.sum(jnp.where(places == to_group, table, 0), axis=0, keepdims=True)
            if z_step or c_step:
                row = lax.ppermute(
                    row,
                    GROUPS,
                    [
                        (z * 2 + c, ((z + z_step) % z_count) * 2 + (c ^ c_step))
                        for z in range(z_count)
                        for c in range(2)
                    ],
                )
            got = got + jnp.where(places == from_group, row, 0)
    return got


def line_table(table):
    x_place = lax.axis_index("x")
    places = jnp.arange(RING, dtype=jnp.int32)[:, None]
    got = jnp.where(places == x_place, table, 0)
    for step in range(1, RING):
        chosen = places == (x_place + step) % RING
        row = jnp.sum(jnp.where(chosen, table, 0), axis=0, keepdims=True)
        row = shift(row, "x", step)
        got = got + jnp.where(places == (x_place + RING - step) % RING, row, 0)
    return got


def mxu(left, right, left_dim=1, right_dim=0):
    return lax.dot_general(
        left, right, (((left_dim,), (right_dim,)), ((), ())), preferred_element_type=jnp.float32
    )


def params(mib):
    return pltpu.CompilerParams(dimension_semantics=("arbitrary",), vmem_limit_bytes=mib * MIB)


SMALL = pl.CostEstimate(flops=1, bytes_accessed=1, transcendentals=0)
LARGE = pl.CostEstimate(flops=10**11, bytes_accessed=10**8, transcendentals=0)


def tile(width):
    return min(1024, width)


def whole(shape):
    return pl.BlockSpec(shape, lambda i: (0,) * len(shape))


def columns(rows, width):
    return pl.BlockSpec((rows, tile(width)), lambda i: (0, i))


def joined(refs):
    blocks = [ref[...] for ref in refs]
    return blocks[0] if len(blocks) == 1 else jnp.concatenate(blocks, axis=0)


def inverse_norm(values):
    return lax.rsqrt(jnp.mean(values * values, axis=-1, keepdims=True) + EPSILON)


def embed(hidden, gain, pieces):
    def body(hidden_ref, gain_ref, *out_refs):
        values = hidden_ref[...].astype(jnp.float32)
        unit_rows = values * inverse_norm(values)
        rounded_rows = (unit_rows * gain_ref[...]).astype(jnp.bfloat16)
        for i, out_ref in enumerate(out_refs):

            @pl.when(pl.program_id(0) // per_piece == i)
            def _(out_ref=out_ref):
                out_ref[...] = rounded_rows

    rows, width = hidden.shape
    step = min(32, rows // pieces)
    per_piece = rows // pieces // step
    block = pl.BlockSpec((step, width), lambda i: (i, 0))

    def piece(at):
        return pl.BlockSpec(
            (step, width), lambda i: (jnp.clip(i - at * per_piece, 0, per_piece - 1), 0)
        )

    return pl.pallas_call(
        body,
        grid=(rows // step,),
        in_specs=[block, whole((1, width))],
        out_specs=[piece(at) for at in range(pieces)],
        out_shape=[jax.ShapeDtypeStruct((rows // pieces, width), jnp.bfloat16)] * pieces,
        compiler_params=params(12),
        cost_estimate=SMALL,
        name="embed",
    )(hidden, gain)


def finish(hidden, gain, terms, put=None, arrived=None, scale=1.0):
    rows, width = hidden.shape
    step = rows // 8
    product = () if put is None else (put, arrived)

    def body(hidden_ref, gain_ref, *refs):
        total = refs[0][...].astype(jnp.float32)
        for ref in refs[1 : len(terms)]:
            total += ref[...].astype(jnp.float32)
        if product:
            total += scale * mxu(refs[-3][...], refs[-2][...])
        values = hidden_ref[...].astype(jnp.float32)
        inverse = inverse_norm(values)
        unit_rows = values * inverse
        scaled = total * gain_ref[...]
        inner = jnp.mean(scaled * unit_rows, axis=-1, keepdims=True)
        refs[-1][...] = (inverse * (scaled - unit_rows * inner)).astype(jnp.bfloat16)

    block = pl.BlockSpec((step, width), lambda i: (i, 0))
    extra = []
    if product:
        extra = [pl.BlockSpec((step, put.shape[1]), lambda i: (i, 0)), whole(arrived.shape)]
    return pl.pallas_call(
        body,
        grid=(rows // step,),
        in_specs=[block, whole((1, width))] + [block] * len(terms) + extra,
        out_specs=block,
        out_shape=jax.ShapeDtypeStruct((rows, width), jnp.bfloat16),
        compiler_params=params(20),
        cost_estimate=SMALL,
        name="finish",
    )(hidden, gain, *terms, *product)


def pick_rows(matrix, sources):
    width = sources[0].shape[1]

    def body(matrix_ref, *refs):
        refs[-1][...] = mxu(matrix_ref[...], joined(refs[:-1])).astype(jnp.bfloat16)

    return pl.pallas_call(
        body,
        grid=(width // tile(width),),
        in_specs=[whole(matrix.shape)] + [columns(s.shape[0], width) for s in sources],
        out_specs=columns(matrix.shape[0], width),
        out_shape=jax.ShapeDtypeStruct((matrix.shape[0], width), jnp.bfloat16),
        compiler_params=params(16),
        cost_estimate=SMALL,
        name="pick_rows",
    )(matrix, *sources)


def line_scores(sources, queries, scale):
    width = queries.shape[1]
    steps = width // tile(width)

    def body(query_ref, *refs):
        step = pl.program_id(0)
        out_ref = refs[-1]

        @pl.when(step == 0)
        def _():
            out_ref[...] = jnp.zeros_like(out_ref)

        out_ref[...] += scale * mxu(joined(refs[:-1]), query_ref[...], 1, 1)

    out = (sum(s.shape[0] for s in sources), queries.shape[0])
    return pl.pallas_call(
        body,
        grid=(steps,),
        in_specs=[columns(queries.shape[0], width)]
        + [columns(s.shape[0], width) for s in sources],
        out_specs=whole(out),
        out_shape=jax.ShapeDtypeStruct(out, jnp.float32),
        compiler_params=params(20),
        cost_estimate=SMALL,
        name="line_scores",
    )(queries, *sources)


def far_scores(near, sources, queries, asked_by, line, scale):
    width = queries.shape[1]
    query_count = queries.shape[0]
    steps = width // tile(width)
    near_slots = near.shape[0] - line
    far_slots = asked_by.shape[0] - near_slots

    def body(near_ref, mask_ref, query_ref, *refs):
        out_ref, log_ref = refs[-2:]
        step = pl.program_id(0)

        @pl.when(step == 0)
        def _():
            out_ref[...] = jnp.zeros_like(out_ref)

        out_ref[...] += scale * mxu(joined(refs[:-2]), query_ref[...], 1, 1)

        @pl.when(step == steps - 1)
        def _():
            inner = near_ref[:line, :]
            own = jnp.where(mask_ref[:near_slots, :] > 0, near_ref[line:, :], LOW)
            far = jnp.where(mask_ref[near_slots:, :] > 0, out_ref[...], LOW)
            parts = (inner, own, far)
            top = jnp.max(inner, axis=0, keepdims=True)
            for part in parts[1:]:
                top = jnp.maximum(top, jnp.max(part, axis=0, keepdims=True))
            total = jnp.zeros_like(top)
            for part in parts:
                total += jnp.sum(jnp.exp(part - top), axis=0, keepdims=True)
            log_ref[...] = top + jnp.log(total)

    return pl.pallas_call(
        body,
        grid=(steps,),
        in_specs=[
            whole(near.shape),
            whole(asked_by.shape),
            columns(query_count, width),
        ]
        + [columns(s.shape[0], width) for s in sources],
        out_specs=[whole((far_slots, query_count)), whole((1, query_count))],
        out_shape=[
            jax.ShapeDtypeStruct((far_slots, query_count), jnp.float32),
            jax.ShapeDtypeStruct((1, query_count), jnp.float32),
        ],
        compiler_params=params(28),
        cost_estimate=LARGE,
        name="far_scores",
    )(near, asked_by, queries, *sources)


def query_side(near, far, asked_by, log_total, weight, target, queries, sources, line, scale):
    width = queries.shape[1]
    query_count = queries.shape[0]
    near_slots = near.shape[0] - line
    slot_count = asked_by.shape[0]
    count = len(sources)
    rows = line // RING
    cuts = (line,)

    def body(near_ref, far_ref, mask_ref, log_ref, weight_ref, target_ref, query_ref, *refs):
        source_refs = refs[:count]
        part_ref, gain_ref, slot_ref, positive_ref = refs[count : count + 4]
        coeff_refs, turned_ref = refs[count + 4 : -1], refs[-1]

        @pl.when(pl.program_id(0) == 0)
        def _():
            log_row, weight_row = log_ref[...], weight_ref[...]
            inner = near_ref[:line, :]
            row_place = lax.broadcasted_iota(jnp.int32, inner.shape, 0)
            hit = row_place == target_ref[...]
            positive_ref[...] = jnp.sum(jnp.where(hit, inner, 0.0), axis=0, keepdims=True)
            inner_coeff = weight_row * (jnp.exp(inner - log_row) - jnp.where(hit, 1.0, 0.0))
            at = 0
            for coeff_ref, size in zip(coeff_refs, cuts):
                coeff_ref[...] = inner_coeff[at : at + size].astype(jnp.bfloat16)
                at += size
            own = jnp.where(mask_ref[:near_slots, :] > 0, near_ref[line:, :], LOW)
            slots = jnp.where(mask_ref[near_slots:, :] > 0, far_ref[...], LOW)
            own_coeff = (weight_row * jnp.exp(own - log_row)).astype(jnp.bfloat16)
            far_coeff = (weight_row * jnp.exp(slots - log_row)).astype(jnp.bfloat16)
            ones = jnp.ones((8, query_count), jnp.bfloat16)
            slot_ref[:, :near_slots] = mxu(ones, own_coeff, 1, 1)
            slot_ref[:, near_slots:] = mxu(ones, far_coeff, 1, 1)
            turned_ref[:, :line] = jnp.transpose(inner_coeff).astype(jnp.bfloat16)
            turned_ref[:, line : line + near_slots] = jnp.transpose(
                own_coeff.astype(jnp.float32)
            ).astype(jnp.bfloat16)
            turned_ref[:, line + near_slots :] = jnp.transpose(
                far_coeff.astype(jnp.float32)
            ).astype(jnp.bfloat16)

        total = scale * mxu(turned_ref[...], joined(source_refs))
        part_ref[...] = total.astype(jnp.bfloat16)
        gain_ref[...] = jnp.sum(total * query_ref[...].astype(jnp.float32), axis=0, keepdims=True)

    row = whole((1, query_count))
    return pl.pallas_call(
        body,
        grid=(width // tile(width),),
        in_specs=[
            whole(near.shape),
            whole(far.shape),
            whole(asked_by.shape),
            row,
            row,
            row,
            columns(query_count, width),
        ]
        + [columns(s.shape[0], width) for s in sources],
        out_specs=[
            columns(query_count, width),
            columns(1, width),
            whole((8, slot_count)),
            row,
        ]
        + [whole((size, query_count)) for size in cuts],
        out_shape=[
            jax.ShapeDtypeStruct((query_count, width), jnp.bfloat16),
            jax.ShapeDtypeStruct((1, width), jnp.float32),
            jax.ShapeDtypeStruct((8, slot_count), jnp.float32),
            jax.ShapeDtypeStruct((1, query_count), jnp.float32),
        ]
        + [jax.ShapeDtypeStruct((size, query_count), jnp.bfloat16) for size in cuts],
        scratch_shapes=[pltpu.VMEM((query_count, line + slot_count), jnp.bfloat16)],
        compiler_params=params(32),
        cost_estimate=SMALL,
        name="query_side",
    )(near, far, asked_by, log_total, weight, target, queries, *sources)


def passage_side(coeff, queries, put, arrived, scale, layout):
    width = queries.shape[1]
    sizes = [sum(high - low for low, high in ranges) for ranges in layout]
    own = coeff.shape[0] - put.shape[0]

    def body(coeff_ref, query_ref, put_ref, arrived_ref, own_ref, *out_refs):
        total = mxu(coeff_ref[own:], query_ref[...]) + mxu(put_ref[...], arrived_ref[...])
        total = (scale * total).astype(jnp.bfloat16)
        for ranges, out_ref in zip(layout, out_refs):
            at = 0
            for low, high in ranges:
                out_ref[at : at + high - low] = total[low:high]
                at += high - low
        own_ref[...] = (scale * mxu(coeff_ref[:own], query_ref[...])).astype(jnp.bfloat16)

    return pl.pallas_call(
        body,
        grid=(width // tile(width),),
        in_specs=[
            whole(coeff.shape),
            columns(queries.shape[0], width),
            whole(put.shape),
            columns(arrived.shape[0], width),
        ],
        out_specs=[columns(own, width)] + [columns(size, width) for size in sizes],
        out_shape=[
            jax.ShapeDtypeStruct((size, width), jnp.bfloat16) for size in (own, *sizes)
        ],
        compiler_params=params(20),
        cost_estimate=LARGE,
        name="passage_side",
    )(coeff, queries, put, arrived)


def add_passing(up, passing_low, down, passing_high):
    half, width = passing_low.shape
    rows = 2 * half

    def body(up_ref, low_ref, down_ref, high_ref, up_out, down_out):
        wide = jnp.float32
        up_out[:half] = (up_ref[:half].astype(wide) + low_ref[...].astype(wide)).astype(up.dtype)
        up_out[half:] = up_ref[half:]
        down_out[:half] = down_ref[:half]
        down_out[half:] = (down_ref[half:].astype(wide) + high_ref[...].astype(wide)).astype(
            up.dtype
        )

    return pl.pallas_call(
        body,
        grid=(width // tile(width),),
        in_specs=[
            columns(rows, width),
            columns(half, width),
            columns(rows, width),
            columns(half, width),
        ],
        out_specs=[columns(rows, width)] * 2,
        out_shape=[jax.ShapeDtypeStruct(up.shape, up.dtype)] * 2,
        compiler_params=params(12),
        cost_estimate=SMALL,
        name="add_passing",
    )(up, passing_low, down, passing_high)


def on_device(query_hidden, passage_hidden, norm_gain, query_weight, hneg_ids):
    rows, width = query_hidden.shape
    neg_count = hneg_ids.shape[1]
    z_count = lax.axis_size("z")
    group_count = 2 * z_count
    line = RING * rows
    scale = 1.0 / (SOFTMAX_TEMPER * math.sqrt(width))
    y_place, x_place = lax.axis_index("y"), lax.axis_index("x")

    gain = norm_gain.reshape(1, width)
    p_own = embed(passage_hidden, gain, 2)
    p_far, p_sent = ring_gather(*p_own, "y")

    flat_ids = hneg_ids.reshape(-1)
    id_count = rows * neg_count
    owners = flat_ids // rows
    local_row = flat_ids % rows
    number = jnp.arange(id_count, dtype=jnp.int32)
    same = (owners[:, None] == owners[None, :]) & (number[None, :] < number[:, None])
    rank = jnp.sum(same.astype(jnp.int32), axis=1)
    y_step = (owners // RING - y_place) % RING
    line_of = (owners // (RING * RING)) * RING + owners % RING
    slot = (line_of * RING + y_step) * CAP + rank
    slot_count = group_count * RING * RING * CAP
    hit = slot[None, :] == jnp.arange(slot_count, dtype=jnp.int32)[:, None]
    slot_row = jnp.sum(jnp.where(hit, local_row[None, :] + 1, 0), axis=1) - 1
    slot_query = jnp.sum(jnp.where(hit, number[None, :] // neg_count + 1, 0), axis=1)
    asked = lax.all_to_all(
        slot_row.reshape(group_count * RING, RING * CAP), ("z", "c", "x"), 0, 0, tiled=True
    )
    asked = asked.reshape(group_count, RING, RING, CAP).transpose(0, 2, 1, 3)
    place = jnp.arange(line, dtype=jnp.int32)
    asked, query_hidden, _ = lax.optimization_barrier((asked, query_hidden, p_sent))
    asked_own = asked[:, 0].reshape(-1)
    half = rows // 2

    def moved(block, base):
        return jnp.where(block < 0, -1, block + base + jnp.where(block >= half, half, 0))

    asked_far = jnp.concatenate(
        [asked[:, 1:2], moved(asked[:, 3:], rows + half), moved(asked[:, 2:3], rows)], axis=1
    ).reshape(-1)

    def one_hot(numbers, size):
        return (numbers[:, None] == place[None, :size]).astype(jnp.bfloat16)

    chosen_own = pick_rows(one_hot(asked_own, rows), p_own)
    hard_own = group_rows(chosen_own, group_count)
    chosen_far = pick_rows(one_hot(asked_far, 3 * rows), p_far)
    hard_far = group_rows(chosen_far, group_count)

    q_emb = embed(query_hidden, gain, 1)[0]
    q_line = lax.all_gather(q_emb, "x", axis=0, tiled=True)

    by_x = slot_query.reshape(group_count, RING, RING * CAP).transpose(1, 0, 2)
    asker = line_table(by_x.reshape(RING, -1)).reshape(RING, group_count, RING, CAP)
    x_base = rows * jnp.arange(RING, dtype=jnp.int32)
    asker = jnp.where(asker == 0, -1, asker - 1 + x_base[:, None, None, None])
    asker = asker.transpose(1, 2, 0, 3)
    far_asker = jnp.concatenate([asker[:, 1:2], asker[:, 3:], asker[:, 2:3]], axis=1)
    send_own = one_hot(asker[:, 0].reshape(-1), line)
    send_far = one_hot(far_asker.reshape(-1), line)
    asked_by = jnp.concatenate([send_own, send_far], axis=0)
    leave_far = pick_rows(send_far, [q_line])
    leave_own = pick_rows(send_own, [q_line])
    q_line, leave_far, leave_own = lax.optimization_barrier((q_line, leave_far, leave_own))
    far_queries = group_rows(leave_far, group_count)
    own_queries = group_rows(leave_own, group_count)

    near = line_scores([*p_own, *p_far, hard_own], q_line, scale)
    far, part_log = far_scores(near, [hard_far], q_line, asked_by, line, scale)
    part_log = part_log.reshape(RING, rows)
    own_place = jnp.arange(RING, dtype=jnp.int32)[:, None] == x_place
    own_weight = jnp.where(own_place, query_weight[None, :], 0.0)
    message = jnp.concatenate([part_log, own_weight], axis=0)
    messages = [message] + [shift(message, "x", step) for step in (1, 3, 2)]
    logs = [m[:RING] for m in messages]
    weight = sum(m[RING:] for m in messages).reshape(1, line)
    top = jnp.maximum(jnp.maximum(logs[0], logs[1]), jnp.maximum(logs[2], logs[3]))
    log_total = (top + jnp.log(sum(jnp.exp(part - top) for part in logs))).reshape(1, line)
    first_row = x_place * rows
    target = place[None, :] - first_row
    target = jnp.where((target >= 0) & (target < rows), target, -1)

    part, gain_part, slot_coeff, positive, coeff = query_side(
        near, far, asked_by, log_total, weight, target, q_line,
        [*p_own, *p_far, hard_own, hard_far], line, scale,
    )
    loss_rows = lax.dynamic_slice(log_total - positive, (0, first_row), (1, rows)).reshape(-1)
    query_up = lax.psum_scatter(part, "x", scatter_dimension=0, tiled=True)
    query_grad = finish(query_hidden, gain, [query_up])

    own_end = group_count * RING * CAP
    pieces = (
        slot_coeff[0, :own_end].reshape(group_count, -1),
        slot_coeff[0, own_end:].reshape(group_count, -1),
    )
    got_coeff = group_table(jnp.concatenate(pieces, axis=1), group_count)
    first = RING * CAP

    def put_rows(numbers, values, size):
        return jnp.where(
            place[:size, None] == numbers[None, :], values.reshape(-1)[None, :], 0.0
        ).astype(jnp.bfloat16)

    put_own = put_rows(asked_own, got_coeff[:, :first], rows)
    put_far = put_rows(asked_far, got_coeff[:, first:], 3 * rows)
    low_1, high_1, low_2, low_3, high_2, high_3 = [(i * half, (i + 1) * half) for i in range(6)]
    own_part, for_above, for_below, pass_up, pass_down = passage_side(
        coeff, q_line, put_far, far_queries, scale,
        [[low_1, high_1], [low_3, high_3], [low_2], [high_2]],
    )
    passing_low = shift(pass_up, "y", 1)
    passing_high = shift(pass_down, "y", -1)
    gain_part = pair_sum(pair_sum(gain_part.reshape(-1, 128), "z", False), "z", True)
    gain_part, passing_low = lax.optimization_barrier((gain_part, passing_low))
    for_above, for_below = add_passing(for_above, passing_low, for_below, passing_high)
    from_below = shift(for_above, "y", 1)
    from_above = shift(for_below, "y", -1)
    gain_part, _ = lax.optimization_barrier((gain_part, for_above))
    gain_part = pair_sum(gain_part, "c", False)
    gain_part = pair_sum(pair_sum(gain_part, "x", False), "x", True)
    gain_part, query_grad = lax.optimization_barrier((gain_part, query_grad))
    gain_part = pair_sum(pair_sum(gain_part, "y", False), "y", True)
    gain_grad = 2.0 * gain_part.reshape(-1) / norm_gain
    passage_grad = finish(
        passage_hidden, gain, [own_part, from_below, from_above], put_own, own_queries, scale
    )
    return (loss_rows, query_grad, passage_grad, gain_grad)


def solution(mesh):
    torus = Mesh(mesh.devices.reshape(-1, 2, RING, RING), ALL_AXES)
    return jax.shard_map(
        on_device,
        mesh=torus,
        in_specs=(
            P(ALL_AXES, None),
            P(ALL_AXES, None),
            P(),
            P(ALL_AXES),
            P(ALL_AXES, None),
        ),
        out_specs=(
            P(ALL_AXES),
            P(ALL_AXES, None),
            P(ALL_AXES, None),
            P(),
        ),
        check_vma=False,
    )
```

```python
import math

import jax
import jax.numpy as jnp
from jax import lax
from jax.experimental import pallas as pl
from jax.experimental.pallas import tpu as pltpu
from jax.sharding import Mesh, PartitionSpec as P

EPSILON = 1e-06
SOFTMAX_TEMPER = 0.28
RING = 4
CAP = 4
GROUPS = ("z", "c")
ALL_AXES = ("z", "c", "y", "x")
MIB = 1024 * 1024
LOW = -1e30


def shift(value, axis, step):
    return lax.ppermute(value, axis, [(i, (i + step) % RING) for i in range(RING)])


def ring_gather(low, high, axis):
    up_low = shift(low, axis, -1)
    down_high = shift(high, axis, 1)
    to_below = jnp.concatenate([high, up_low], axis=0)
    to_above = jnp.concatenate([low, down_high], axis=0)
    up_more = shift(to_below, axis, -1)
    down_more = shift(to_above, axis, 1)
    return [up_low, up_more, down_more, down_high], [to_below, to_above]


def pair_sum(value, axis, turn):
    size = lax.axis_size(axis)
    pairs = [(i, size - 1 - i if turn else i ^ 1) for i in range(size)]
    return value + lax.ppermute(value, axis, pairs)


def group_rows(rows, group_count):
    blocks = rows.reshape(group_count, rows.shape[0] // group_count, rows.shape[1])
    return lax.all_to_all(blocks, GROUPS, 0, 0, tiled=True).reshape(rows.shape)


def group_table(table, group_count):
    z_count = group_count // 2
    z_place, c_place = lax.axis_index("z"), lax.axis_index("c")
    got = jnp.zeros_like(table)
    places = jnp.arange(group_count, dtype=jnp.int32)[:, None]
    for z_step in range(z_count):
        for c_step in range(2):
            to_group = ((z_place + z_step) % z_count) * 2 + (c_place ^ c_step)
            from_group = ((z_place + z_count - z_step) % z_count) * 2 + (c_place ^ c_step)
            row = jnp.sum(jnp.where(places == to_group, table, 0), axis=0, keepdims=True)
            if z_step or c_step:
                row = lax.ppermute(
                    row,
                    GROUPS,
                    [
                        (z * 2 + c, ((z + z_step) % z_count) * 2 + (c ^ c_step))
                        for z in range(z_count)
                        for c in range(2)
                    ],
                )
            got = got + jnp.where(places == from_group, row, 0)
    return got


def line_table(table):
    x_place = lax.axis_index("x")
    places = jnp.arange(RING, dtype=jnp.int32)[:, None]
    got = jnp.where(places == x_place, table, 0)
    for step in range(1, RING):
        chosen = places == (x_place + step) % RING
        row = jnp.sum(jnp.where(chosen, table, 0), axis=0, keepdims=True)
        row = shift(row, "x", step)
        got = got + jnp.where(places == (x_place + RING - step) % RING, row, 0)
    return got


def mxu(left, right, left_dim=1, right_dim=0):
    return lax.dot_general(
        left, right, (((left_dim,), (right_dim,)), ((), ())), preferred_element_type=jnp.float32
    )


def params(mib):
    return pltpu.CompilerParams(dimension_semantics=("arbitrary",), vmem_limit_bytes=mib * MIB)


SMALL = pl.CostEstimate(flops=1, bytes_accessed=1, transcendentals=0)
LARGE = pl.CostEstimate(flops=10**11, bytes_accessed=10**8, transcendentals=0)


def tile(width):
    return min(1024, width)


def whole(shape):
    return pl.BlockSpec(shape, lambda i: (0,) * len(shape))


def columns(rows, width, tiles=1):
    return pl.BlockSpec((rows, tiles * tile(width)), lambda i: (0, i))


def joined(refs):
    blocks = [ref[...] for ref in refs]
    return blocks[0] if len(blocks) == 1 else jnp.concatenate(blocks, axis=0)


def inverse_norm(values):
    return lax.rsqrt(jnp.mean(values * values, axis=-1, keepdims=True) + EPSILON)


def embed(hidden, gain, pieces):
    def body(hidden_ref, gain_ref, *out_refs):
        values = hidden_ref[...].astype(jnp.float32)
        unit_rows = values * inverse_norm(values)
        rounded_rows = (unit_rows * gain_ref[...]).astype(jnp.bfloat16)
        for i, out_ref in enumerate(out_refs):

            @pl.when(pl.program_id(0) // per_piece == i)
            def _(out_ref=out_ref):
                out_ref[...] = rounded_rows

    rows, width = hidden.shape
    step = min(32, rows // pieces)
    per_piece = rows // pieces // step
    block = pl.BlockSpec((step, width), lambda i: (i, 0))

    def piece(at):
        return pl.BlockSpec(
            (step, width), lambda i: (jnp.clip(i - at * per_piece, 0, per_piece - 1), 0)
        )

    return pl.pallas_call(
        body,
        grid=(rows // step,),
        in_specs=[block, whole((1, width))],
        out_specs=[piece(at) for at in range(pieces)],
        out_shape=[jax.ShapeDtypeStruct((rows // pieces, width), jnp.bfloat16)] * pieces,
        compiler_params=params(12),
        cost_estimate=SMALL,
        name="embed",
    )(hidden, gain)


def finish(hidden, gain, terms, put=None, arrived=None, scale=1.0):
    rows, width = hidden.shape
    step = rows // 2
    product = () if put is None else (put, arrived)

    def body(hidden_ref, gain_ref, *refs):
        total = refs[0][...].astype(jnp.float32)
        for ref in refs[1 : len(terms)]:
            total += ref[...].astype(jnp.float32)
        if product:
            total += scale * mxu(refs[-3][...], refs[-2][...])
        values = hidden_ref[...].astype(jnp.float32)
        inverse = inverse_norm(values)
        unit_rows = values * inverse
        scaled = total * gain_ref[...]
        inner = jnp.mean(scaled * unit_rows, axis=-1, keepdims=True)
        refs[-1][...] = (inverse * (scaled - unit_rows * inner)).astype(jnp.bfloat16)

    block = pl.BlockSpec((step, width), lambda i: (i, 0))
    extra = []
    if product:
        extra = [pl.BlockSpec((step, put.shape[1]), lambda i: (i, 0)), whole(arrived.shape)]
    return pl.pallas_call(
        body,
        grid=(rows // step,),
        in_specs=[block, whole((1, width))] + [block] * len(terms) + extra,
        out_specs=block,
        out_shape=jax.ShapeDtypeStruct((rows, width), jnp.bfloat16),
        compiler_params=params(28),
        cost_estimate=SMALL,
        name="finish",
    )(hidden, gain, *terms, *product)


def pick_rows(matrix, sources):
    width = sources[0].shape[1]

    def body(matrix_ref, *refs):
        refs[-1][...] = mxu(matrix_ref[...], joined(refs[:-1])).astype(jnp.bfloat16)

    return pl.pallas_call(
        body,
        grid=(width // (2 * tile(width)),),
        in_specs=[whole(matrix.shape)] + [columns(s.shape[0], width, 2) for s in sources],
        out_specs=columns(matrix.shape[0], width, 2),
        out_shape=jax.ShapeDtypeStruct((matrix.shape[0], width), jnp.bfloat16),
        compiler_params=params(16),
        cost_estimate=SMALL,
        name="pick_rows",
    )(matrix, *sources)


def line_scores(sources, queries, scale):
    width = queries.shape[1]
    steps = width // tile(width)

    def body(query_ref, *refs):
        step = pl.program_id(0)
        out_ref = refs[-1]

        @pl.when(step == 0)
        def _():
            out_ref[...] = jnp.zeros_like(out_ref)

        out_ref[...] += scale * mxu(joined(refs[:-1]), query_ref[...], 1, 1)

    out = (sum(s.shape[0] for s in sources), queries.shape[0])
    return pl.pallas_call(
        body,
        grid=(steps,),
        in_specs=[columns(queries.shape[0], width)]
        + [columns(s.shape[0], width) for s in sources],
        out_specs=whole(out),
        out_shape=jax.ShapeDtypeStruct(out, jnp.float32),
        compiler_params=params(20),
        cost_estimate=SMALL,
        name="line_scores",
    )(queries, *sources)


def far_scores(near, sources, queries, asked_by, line, scale):
    width = queries.shape[1]
    query_count = queries.shape[0]
    steps = width // tile(width)
    near_slots = near.shape[0] - line
    far_slots = asked_by.shape[0] - near_slots

    def body(near_ref, mask_ref, query_ref, *refs):
        out_ref, log_ref = refs[-2:]
        step = pl.program_id(0)

        @pl.when(step == 0)
        def _():
            out_ref[...] = jnp.zeros_like(out_ref)

        out_ref[...] += scale * mxu(joined(refs[:-2]), query_ref[...], 1, 1)

        @pl.when(step == steps - 1)
        def _():
            inner = near_ref[:line, :]
            own = jnp.where(mask_ref[:near_slots, :] > 0, near_ref[line:, :], LOW)
            far = jnp.where(mask_ref[near_slots:, :] > 0, out_ref[...], LOW)
            parts = (inner, own, far)
            top = jnp.max(inner, axis=0, keepdims=True)
            for part in parts[1:]:
                top = jnp.maximum(top, jnp.max(part, axis=0, keepdims=True))
            total = jnp.zeros_like(top)
            for part in parts:
                total += jnp.sum(jnp.exp(part - top), axis=0, keepdims=True)
            log_ref[...] = top + jnp.log(total)

    return pl.pallas_call(
        body,
        grid=(steps,),
        in_specs=[
            whole(near.shape),
            whole(asked_by.shape),
            columns(query_count, width),
        ]
        + [columns(s.shape[0], width) for s in sources],
        out_specs=[whole((far_slots, query_count)), whole((1, query_count))],
        out_shape=[
            jax.ShapeDtypeStruct((far_slots, query_count), jnp.float32),
            jax.ShapeDtypeStruct((1, query_count), jnp.float32),
        ],
        compiler_params=params(28),
        cost_estimate=LARGE,
        name="far_scores",
    )(near, asked_by, queries, *sources)


def query_side(near, far, asked_by, log_total, weight, target, queries, sources, line, scale):
    width = queries.shape[1]
    query_count = queries.shape[0]
    near_slots = near.shape[0] - line
    slot_count = asked_by.shape[0]
    count = len(sources)
    rows = line // RING
    cuts = (line,)

    def body(near_ref, far_ref, mask_ref, log_ref, weight_ref, target_ref, query_ref, *refs):
        source_refs = refs[:count]
        part_ref, gain_ref, slot_ref, positive_ref = refs[count : count + 4]
        coeff_refs, turned_ref = refs[count + 4 : -1], refs[-1]

        @pl.when(pl.program_id(0) == 0)
        def _():
            log_row, weight_row = log_ref[...], weight_ref[...]
            inner = near_ref[:line, :]
            row_place = lax.broadcasted_iota(jnp.int32, inner.shape, 0)
            hit = row_place == target_ref[...]
            positive_ref[...] = jnp.sum(jnp.where(hit, inner, 0.0), axis=0, keepdims=True)
            inner_coeff = weight_row * (jnp.exp(inner - log_row) - jnp.where(hit, 1.0, 0.0))
            at = 0
            for coeff_ref, size in zip(coeff_refs, cuts):
                coeff_ref[...] = inner_coeff[at : at + size].astype(jnp.bfloat16)
                at += size
            own = jnp.where(mask_ref[:near_slots, :] > 0, near_ref[line:, :], LOW)
            slots = jnp.where(mask_ref[near_slots:, :] > 0, far_ref[...], LOW)
            own_coeff = (weight_row * jnp.exp(own - log_row)).astype(jnp.bfloat16)
            far_coeff = (weight_row * jnp.exp(slots - log_row)).astype(jnp.bfloat16)
            ones = jnp.ones((8, query_count), jnp.bfloat16)
            slot_ref[:, :near_slots] = mxu(ones, own_coeff, 1, 1)
            slot_ref[:, near_slots:] = mxu(ones, far_coeff, 1, 1)
            turned_ref[:, :line] = jnp.transpose(inner_coeff).astype(jnp.bfloat16)
            turned_ref[:, line : line + near_slots] = jnp.transpose(
                own_coeff.astype(jnp.float32)
            ).astype(jnp.bfloat16)
            turned_ref[:, line + near_slots :] = jnp.transpose(
                far_coeff.astype(jnp.float32)
            ).astype(jnp.bfloat16)

        total = scale * mxu(turned_ref[...], joined(source_refs))
        part_ref[...] = total.astype(jnp.bfloat16)
        gain_ref[...] = jnp.sum(total * query_ref[...].astype(jnp.float32), axis=0, keepdims=True)

    row = whole((1, query_count))
    return pl.pallas_call(
        body,
        grid=(width // tile(width),),
        in_specs=[
            whole(near.shape),
            whole(far.shape),
            whole(asked_by.shape),
            row,
            row,
            row,
            columns(query_count, width),
        ]
        + [columns(s.shape[0], width) for s in sources],
        out_specs=[
            columns(query_count, width),
            columns(1, width),
            whole((8, slot_count)),
            row,
        ]
        + [whole((size, query_count)) for size in cuts],
        out_shape=[
            jax.ShapeDtypeStruct((query_count, width), jnp.bfloat16),
            jax.ShapeDtypeStruct((1, width), jnp.float32),
            jax.ShapeDtypeStruct((8, slot_count), jnp.float32),
            jax.ShapeDtypeStruct((1, query_count), jnp.float32),
        ]
        + [jax.ShapeDtypeStruct((size, query_count), jnp.bfloat16) for size in cuts],
        scratch_shapes=[pltpu.VMEM((query_count, line + slot_count), jnp.bfloat16)],
        compiler_params=params(32),
        cost_estimate=SMALL,
        name="query_side",
    )(near, far, asked_by, log_total, weight, target, queries, *sources)


def passage_side(coeff, queries, put, arrived, scale, layout):
    width = queries.shape[1]
    sizes = [sum(high - low for low, high in ranges) for ranges in layout]
    own = coeff.shape[0] - put.shape[0]

    def body(coeff_ref, query_ref, put_ref, arrived_ref, own_ref, *out_refs):
        total = mxu(coeff_ref[own:], query_ref[...]) + mxu(put_ref[...], arrived_ref[...])
        total = (scale * total).astype(jnp.bfloat16)
        for ranges, out_ref in zip(layout, out_refs):
            at = 0
            for low, high in ranges:
                out_ref[at : at + high - low] = total[low:high]
                at += high - low
        own_ref[...] = (scale * mxu(coeff_ref[:own], query_ref[...])).astype(jnp.bfloat16)

    return pl.pallas_call(
        body,
        grid=(width // tile(width),),
        in_specs=[
            whole(coeff.shape),
            columns(queries.shape[0], width),
            whole(put.shape),
            columns(arrived.shape[0], width),
        ],
        out_specs=[columns(own, width)] + [columns(size, width) for size in sizes],
        out_shape=[
            jax.ShapeDtypeStruct((size, width), jnp.bfloat16) for size in (own, *sizes)
        ],
        compiler_params=params(20),
        cost_estimate=LARGE,
        name="passage_side",
    )(coeff, queries, put, arrived)


def add_passing(up, passing_low, down, passing_high):
    half, width = passing_low.shape
    rows = 2 * half

    def body(up_ref, low_ref, down_ref, high_ref, up_out, down_out):
        wide = jnp.float32
        up_out[:half] = (up_ref[:half].astype(wide) + low_ref[...].astype(wide)).astype(up.dtype)
        up_out[half:] = up_ref[half:]
        down_out[:half] = down_ref[:half]
        down_out[half:] = (down_ref[half:].astype(wide) + high_ref[...].astype(wide)).astype(
            up.dtype
        )

    return pl.pallas_call(
        body,
        grid=(width // tile(width),),
        in_specs=[
            columns(rows, width),
            columns(half, width),
            columns(rows, width),
            columns(half, width),
        ],
        out_specs=[columns(rows, width)] * 2,
        out_shape=[jax.ShapeDtypeStruct(up.shape, up.dtype)] * 2,
        compiler_params=params(12),
        cost_estimate=SMALL,
        name="add_passing",
    )(up, passing_low, down, passing_high)


def on_device(query_hidden, passage_hidden, norm_gain, query_weight, hneg_ids):
    rows, width = query_hidden.shape
    neg_count = hneg_ids.shape[1]
    z_count = lax.axis_size("z")
    group_count = 2 * z_count
    line = RING * rows
    scale = 1.0 / (SOFTMAX_TEMPER * math.sqrt(width))
    y_place, x_place = lax.axis_index("y"), lax.axis_index("x")

    gain = norm_gain.reshape(1, width)
    p_own = embed(passage_hidden, gain, 2)
    p_far, p_sent = ring_gather(*p_own, "y")

    flat_ids = hneg_ids.reshape(-1)
    id_count = rows * neg_count
    owners = flat_ids // rows
    local_row = flat_ids % rows
    number = jnp.arange(id_count, dtype=jnp.int32)
    same = (owners[:, None] == owners[None, :]) & (number[None, :] < number[:, None])
    rank = jnp.sum(same.astype(jnp.int32), axis=1)
    y_step = (owners // RING - y_place) % RING
    line_of = (owners // (RING * RING)) * RING + owners % RING
    slot = (line_of * RING + y_step) * CAP + rank
    slot_count = group_count * RING * RING * CAP
    hit = slot[None, :] == jnp.arange(slot_count, dtype=jnp.int32)[:, None]
    slot_row = jnp.sum(jnp.where(hit, local_row[None, :] + 1, 0), axis=1) - 1
    slot_query = jnp.sum(jnp.where(hit, number[None, :] // neg_count + 1, 0), axis=1)
    asked = lax.all_to_all(
        slot_row.reshape(group_count * RING, RING * CAP), ("z", "c", "x"), 0, 0, tiled=True
    )
    asked = asked.reshape(group_count, RING, RING, CAP).transpose(0, 2, 1, 3)
    place = jnp.arange(line, dtype=jnp.int32)
    asked, query_hidden, _ = lax.optimization_barrier((asked, query_hidden, p_sent))
    asked_own = asked[:, 0].reshape(-1)
    half = rows // 2

    def moved(block, base):
        return jnp.where(block < 0, -1, block + base + jnp.where(block >= half, half, 0))

    asked_far = jnp.concatenate(
        [asked[:, 1:2], moved(asked[:, 3:], rows + half), moved(asked[:, 2:3], rows)], axis=1
    ).reshape(-1)

    def one_hot(numbers, size):
        return (numbers[:, None] == place[None, :size]).astype(jnp.bfloat16)

    chosen_own = pick_rows(one_hot(asked_own, rows), p_own)
    hard_own = group_rows(chosen_own, group_count)
    chosen_far = pick_rows(one_hot(asked_far, 3 * rows), p_far)
    hard_far = group_rows(chosen_far, group_count)

    q_emb = embed(query_hidden, gain, 1)[0]
    q_line = lax.all_gather(q_emb, "x", axis=0, tiled=True)

    by_x = slot_query.reshape(group_count, RING, RING * CAP).transpose(1, 0, 2)
    asker = line_table(by_x.reshape(RING, -1)).reshape(RING, group_count, RING, CAP)
    x_base = rows * jnp.arange(RING, dtype=jnp.int32)
    asker = jnp.where(asker == 0, -1, asker - 1 + x_base[:, None, None, None])
    asker = asker.transpose(1, 2, 0, 3)
    far_asker = jnp.concatenate([asker[:, 1:2], asker[:, 3:], asker[:, 2:3]], axis=1)
    send_own = one_hot(asker[:, 0].reshape(-1), line)
    send_far = one_hot(far_asker.reshape(-1), line)
    asked_by = jnp.concatenate([send_own, send_far], axis=0)
    leave_far = pick_rows(send_far, [q_line])
    leave_own = pick_rows(send_own, [q_line])
    q_line, leave_far, leave_own = lax.optimization_barrier((q_line, leave_far, leave_own))
    far_queries = group_rows(leave_far, group_count)
    own_queries = group_rows(leave_own, group_count)

    near = line_scores([*p_own, *p_far, hard_own], q_line, scale)
    far, part_log = far_scores(near, [hard_far], q_line, asked_by, line, scale)
    part_log = part_log.reshape(RING, rows)
    own_place = jnp.arange(RING, dtype=jnp.int32)[:, None] == x_place
    own_weight = jnp.where(own_place, query_weight[None, :], 0.0)
    message = jnp.concatenate([part_log, own_weight], axis=0)
    messages = [message] + [shift(message, "x", step) for step in (1, 3, 2)]
    logs = [m[:RING] for m in messages]
    weight = sum(m[RING:] for m in messages).reshape(1, line)
    top = jnp.maximum(jnp.maximum(logs[0], logs[1]), jnp.maximum(logs[2], logs[3]))
    log_total = (top + jnp.log(sum(jnp.exp(part - top) for part in logs))).reshape(1, line)
    first_row = x_place * rows
    target = place[None, :] - first_row
    target = jnp.where((target >= 0) & (target < rows), target, -1)

    part, gain_part, slot_coeff, positive, coeff = query_side(
        near, far, asked_by, log_total, weight, target, q_line,
        [*p_own, *p_far, hard_own, hard_far], line, scale,
    )
    loss_rows = lax.dynamic_slice(log_total - positive, (0, first_row), (1, rows)).reshape(-1)
    query_up = lax.psum_scatter(part, "x", scatter_dimension=0, tiled=True)
    query_grad = finish(query_hidden, gain, [query_up])

    own_end = group_count * RING * CAP
    pieces = (
        slot_coeff[0, :own_end].reshape(group_count, -1),
        slot_coeff[0, own_end:].reshape(group_count, -1),
    )
    got_coeff = group_table(jnp.concatenate(pieces, axis=1), group_count)
    first = RING * CAP

    def put_rows(numbers, values, size):
        return jnp.where(
            place[:size, None] == numbers[None, :], values.reshape(-1)[None, :], 0.0
        ).astype(jnp.bfloat16)

    put_own = put_rows(asked_own, got_coeff[:, :first], rows)
    put_far = put_rows(asked_far, got_coeff[:, first:], 3 * rows)
    low_1, high_1, low_2, low_3, high_2, high_3 = [(i * half, (i + 1) * half) for i in range(6)]
    own_part, for_above, for_below, pass_up, pass_down = passage_side(
        coeff, q_line, put_far, far_queries, scale,
        [[low_1, high_1], [low_3, high_3], [low_2], [high_2]],
    )
    passing_low = shift(pass_up, "y", 1)
    passing_high = shift(pass_down, "y", -1)
    gain_part = pair_sum(pair_sum(gain_part.reshape(-1, 128), "z", False), "z", True)
    gain_part, passing_low = lax.optimization_barrier((gain_part, passing_low))
    for_above, for_below = add_passing(for_above, passing_low, for_below, passing_high)
    from_below = shift(for_above, "y", 1)
    from_above = shift(for_below, "y", -1)
    gain_part, _ = lax.optimization_barrier((gain_part, for_above))
    gain_part = pair_sum(gain_part, "c", False)
    gain_part = pair_sum(pair_sum(gain_part, "x", False), "x", True)
    gain_part, query_grad = lax.optimization_barrier((gain_part, query_grad))
    gain_part = pair_sum(pair_sum(gain_part, "y", False), "y", True)
    gain_grad = 2.0 * gain_part.reshape(-1) / norm_gain
    passage_grad = finish(
        passage_hidden, gain, [own_part, from_below, from_above], put_own, own_queries, scale
    )
    return (loss_rows, query_grad, passage_grad, gain_grad)


def solution(mesh):
    torus = Mesh(mesh.devices.reshape(-1, 2, RING, RING), ALL_AXES)
    return jax.shard_map(
        on_device,
        mesh=torus,
        in_specs=(
            P(ALL_AXES, None),
            P(ALL_AXES, None),
            P(),
            P(ALL_AXES),
            P(ALL_AXES, None),
        ),
        out_specs=(
            P(ALL_AXES),
            P(ALL_AXES, None),
            P(ALL_AXES, None),
            P(),
        ),
        check_vma=False,
    )
```

```python
import math

import jax
import jax.numpy as jnp
from jax import lax
from jax.experimental import pallas as pl
from jax.experimental.pallas import tpu as pltpu
from jax.sharding import Mesh, PartitionSpec as P

EPSILON = 1e-06
SOFTMAX_TEMPER = 0.28
RING = 4
CAP = 4
GROUPS = ("z", "c")
ALL_AXES = ("z", "c", "y", "x")
MIB = 1024 * 1024
LOW = -1e30


def shift(value, axis, step):
    return lax.ppermute(value, axis, [(i, (i + step) % RING) for i in range(RING)])


def ring_gather(low, high, axis):
    up_low = shift(low, axis, -1)
    down_high = shift(high, axis, 1)
    to_below = jnp.concatenate([high, up_low], axis=0)
    to_above = jnp.concatenate([low, down_high], axis=0)
    up_more = shift(to_below, axis, -1)
    down_more = shift(to_above, axis, 1)
    return [up_low, up_more, down_more, down_high], [to_below, to_above]


def pair_sum(value, axis, turn):
    size = lax.axis_size(axis)
    pairs = [(i, size - 1 - i if turn else i ^ 1) for i in range(size)]
    return value + lax.ppermute(value, axis, pairs)


def group_rows(rows, group_count):
    blocks = rows.reshape(group_count, rows.shape[0] // group_count, rows.shape[1])
    return lax.all_to_all(blocks, GROUPS, 0, 0, tiled=True).reshape(rows.shape)


def group_table(table, group_count):
    z_count = group_count // 2
    z_place, c_place = lax.axis_index("z"), lax.axis_index("c")
    got = jnp.zeros_like(table)
    places = jnp.arange(group_count, dtype=jnp.int32)[:, None]
    for z_step in range(z_count):
        for c_step in range(2):
            to_group = ((z_place + z_step) % z_count) * 2 + (c_place ^ c_step)
            from_group = ((z_place + z_count - z_step) % z_count) * 2 + (c_place ^ c_step)
            row = jnp.sum(jnp.where(places == to_group, table, 0), axis=0, keepdims=True)
            if z_step or c_step:
                row = lax.ppermute(
                    row,
                    GROUPS,
                    [
                        (z * 2 + c, ((z + z_step) % z_count) * 2 + (c ^ c_step))
                        for z in range(z_count)
                        for c in range(2)
                    ],
                )
            got = got + jnp.where(places == from_group, row, 0)
    return got


def line_table(table):
    x_place = lax.axis_index("x")
    places = jnp.arange(RING, dtype=jnp.int32)[:, None]
    got = jnp.where(places == x_place, table, 0)
    for step in range(1, RING):
        chosen = places == (x_place + step) % RING
        row = jnp.sum(jnp.where(chosen, table, 0), axis=0, keepdims=True)
        row = shift(row, "x", step)
        got = got + jnp.where(places == (x_place + RING - step) % RING, row, 0)
    return got


def mxu(left, right, left_dim=1, right_dim=0):
    return lax.dot_general(
        left, right, (((left_dim,), (right_dim,)), ((), ())), preferred_element_type=jnp.float32
    )


def params(mib):
    return pltpu.CompilerParams(dimension_semantics=("arbitrary",), vmem_limit_bytes=mib * MIB)


SMALL = pl.CostEstimate(flops=1, bytes_accessed=1, transcendentals=0)
LARGE = pl.CostEstimate(flops=10**11, bytes_accessed=10**8, transcendentals=0)


def tile(width):
    return min(1024, width)


def whole(shape):
    return pl.BlockSpec(shape, lambda i: (0,) * len(shape))


def columns(rows, width, tiles=1):
    return pl.BlockSpec((rows, tiles * tile(width)), lambda i: (0, i))


def joined(refs):
    blocks = [ref[...] for ref in refs]
    return blocks[0] if len(blocks) == 1 else jnp.concatenate(blocks, axis=0)


def inverse_norm(values):
    return lax.rsqrt(jnp.mean(values * values, axis=-1, keepdims=True) + EPSILON)


def embed(hidden, gain, pieces):
    def body(hidden_ref, gain_ref, *out_refs):
        values = hidden_ref[...].astype(jnp.float32)
        unit_rows = values * inverse_norm(values)
        rounded_rows = (unit_rows * gain_ref[...]).astype(jnp.bfloat16)
        for i, out_ref in enumerate(out_refs):

            @pl.when(pl.program_id(0) // per_piece == i)
            def _(out_ref=out_ref):
                out_ref[...] = rounded_rows

    rows, width = hidden.shape
    step = min(32, rows // pieces)
    per_piece = rows // pieces // step
    block = pl.BlockSpec((step, width), lambda i: (i, 0))

    def piece(at):
        return pl.BlockSpec(
            (step, width), lambda i: (jnp.clip(i - at * per_piece, 0, per_piece - 1), 0)
        )

    return pl.pallas_call(
        body,
        grid=(rows // step,),
        in_specs=[block, whole((1, width))],
        out_specs=[piece(at) for at in range(pieces)],
        out_shape=[jax.ShapeDtypeStruct((rows // pieces, width), jnp.bfloat16)] * pieces,
        compiler_params=params(12),
        cost_estimate=SMALL,
        name="embed",
    )(hidden, gain)


def finish(hidden, gain, terms, put=None, arrived=None, scale=1.0):
    rows, width = hidden.shape
    step = rows // 2
    product = () if put is None else (put, arrived)

    def body(hidden_ref, gain_ref, *refs):
        total = refs[0][...].astype(jnp.float32)
        for ref in refs[1 : len(terms)]:
            total += ref[...].astype(jnp.float32)
        if product:
            total += scale * mxu(refs[-3][...], refs[-2][...])
        values = hidden_ref[...].astype(jnp.float32)
        inverse = inverse_norm(values)
        unit_rows = values * inverse
        scaled = total * gain_ref[...]
        inner = jnp.mean(scaled * unit_rows, axis=-1, keepdims=True)
        refs[-1][...] = (inverse * (scaled - unit_rows * inner)).astype(jnp.bfloat16)

    block = pl.BlockSpec((step, width), lambda i: (i, 0))
    extra = []
    if product:
        extra = [pl.BlockSpec((step, put.shape[1]), lambda i: (i, 0)), whole(arrived.shape)]
    return pl.pallas_call(
        body,
        grid=(rows // step,),
        in_specs=[block, whole((1, width))] + [block] * len(terms) + extra,
        out_specs=block,
        out_shape=jax.ShapeDtypeStruct((rows, width), jnp.bfloat16),
        compiler_params=params(28),
        cost_estimate=SMALL,
        name="finish",
    )(hidden, gain, *terms, *product)


def pick_rows(matrix, sources):
    width = sources[0].shape[1]

    def body(matrix_ref, *refs):
        refs[-1][...] = mxu(matrix_ref[...], joined(refs[:-1])).astype(jnp.bfloat16)

    return pl.pallas_call(
        body,
        grid=(width // (2 * tile(width)),),
        in_specs=[whole(matrix.shape)] + [columns(s.shape[0], width, 2) for s in sources],
        out_specs=columns(matrix.shape[0], width, 2),
        out_shape=jax.ShapeDtypeStruct((matrix.shape[0], width), jnp.bfloat16),
        compiler_params=params(16),
        cost_estimate=SMALL,
        name="pick_rows",
    )(matrix, *sources)


def line_scores(sources, queries, scale):
    width = queries.shape[1]
    steps = width // tile(width)

    def body(query_ref, *refs):
        step = pl.program_id(0)
        out_ref = refs[-1]

        @pl.when(step == 0)
        def _():
            out_ref[...] = jnp.zeros_like(out_ref)

        out_ref[...] += scale * mxu(joined(refs[:-1]), query_ref[...], 1, 1)

    out = (sum(s.shape[0] for s in sources), queries.shape[0])
    return pl.pallas_call(
        body,
        grid=(steps,),
        in_specs=[columns(queries.shape[0], width)]
        + [columns(s.shape[0], width) for s in sources],
        out_specs=whole(out),
        out_shape=jax.ShapeDtypeStruct(out, jnp.float32),
        compiler_params=params(20),
        cost_estimate=SMALL,
        name="line_scores",
    )(queries, *sources)


def far_scores(near, sources, queries, asked_by, line, scale):
    width = queries.shape[1]
    query_count = queries.shape[0]
    steps = width // tile(width)
    near_slots = near.shape[0] - line
    far_slots = asked_by.shape[0] - near_slots

    def body(near_ref, mask_ref, query_ref, *refs):
        out_ref, log_ref = refs[-2:]
        step = pl.program_id(0)

        @pl.when(step == 0)
        def _():
            out_ref[...] = jnp.zeros_like(out_ref)

        out_ref[...] += scale * mxu(joined(refs[:-2]), query_ref[...], 1, 1)

        @pl.when(step == steps - 1)
        def _():
            inner = near_ref[:line, :]
            own = jnp.where(mask_ref[:near_slots, :] > 0, near_ref[line:, :], LOW)
            far = jnp.where(mask_ref[near_slots:, :] > 0, out_ref[...], LOW)
            parts = (inner, own, far)
            top = jnp.max(inner, axis=0, keepdims=True)
            for part in parts[1:]:
                top = jnp.maximum(top, jnp.max(part, axis=0, keepdims=True))
            total = jnp.zeros_like(top)
            for part in parts:
                total += jnp.sum(jnp.exp(part - top), axis=0, keepdims=True)
            log_ref[...] = top + jnp.log(total)

    return pl.pallas_call(
        body,
        grid=(steps,),
        in_specs=[
            whole(near.shape),
            whole(asked_by.shape),
            columns(query_count, width),
        ]
        + [columns(s.shape[0], width) for s in sources],
        out_specs=[whole((far_slots, query_count)), whole((1, query_count))],
        out_shape=[
            jax.ShapeDtypeStruct((far_slots, query_count), jnp.float32),
            jax.ShapeDtypeStruct((1, query_count), jnp.float32),
        ],
        compiler_params=params(28),
        cost_estimate=LARGE,
        name="far_scores",
    )(near, asked_by, queries, *sources)


def query_side(near, far, asked_by, log_total, weight, target, queries, sources, line, scale):
    width = queries.shape[1]
    query_count = queries.shape[0]
    near_slots = near.shape[0] - line
    slot_count = asked_by.shape[0]
    count = len(sources)
    rows = line // RING
    cuts = (line,)

    def body(near_ref, far_ref, mask_ref, log_ref, weight_ref, target_ref, query_ref, *refs):
        source_refs = refs[:count]
        part_ref, gain_ref, slot_ref, positive_ref = refs[count : count + 4]
        coeff_refs, turned_ref = refs[count + 4 : -1], refs[-1]

        @pl.when(pl.program_id(0) == 0)
        def _():
            log_row, weight_row = log_ref[...], weight_ref[...]
            inner = near_ref[:line, :]
            row_place = lax.broadcasted_iota(jnp.int32, inner.shape, 0)
            hit = row_place == target_ref[...]
            positive_ref[...] = jnp.sum(jnp.where(hit, inner, 0.0), axis=0, keepdims=True)
            inner_coeff = weight_row * (jnp.exp(inner - log_row) - jnp.where(hit, 1.0, 0.0))
            at = 0
            for coeff_ref, size in zip(coeff_refs, cuts):
                coeff_ref[...] = inner_coeff[at : at + size].astype(jnp.bfloat16)
                at += size
            own = jnp.where(mask_ref[:near_slots, :] > 0, near_ref[line:, :], LOW)
            slots = jnp.where(mask_ref[near_slots:, :] > 0, far_ref[...], LOW)
            own_coeff = (weight_row * jnp.exp(own - log_row)).astype(jnp.bfloat16)
            far_coeff = (weight_row * jnp.exp(slots - log_row)).astype(jnp.bfloat16)
            ones = jnp.ones((8, query_count), jnp.bfloat16)
            slot_ref[:, :near_slots] = mxu(ones, own_coeff, 1, 1)
            slot_ref[:, near_slots:] = mxu(ones, far_coeff, 1, 1)
            turned_ref[:, :line] = jnp.transpose(inner_coeff).astype(jnp.bfloat16)
            turned_ref[:, line : line + near_slots] = jnp.transpose(
                own_coeff.astype(jnp.float32)
            ).astype(jnp.bfloat16)
            turned_ref[:, line + near_slots :] = jnp.transpose(
                far_coeff.astype(jnp.float32)
            ).astype(jnp.bfloat16)

        total = scale * mxu(turned_ref[...], joined(source_refs))
        part_ref[...] = total.astype(jnp.bfloat16)
        gain_ref[...] = jnp.sum(total * query_ref[...].astype(jnp.float32), axis=0, keepdims=True)

    row = whole((1, query_count))
    return pl.pallas_call(
        body,
        grid=(width // tile(width),),
        in_specs=[
            whole(near.shape),
            whole(far.shape),
            whole(asked_by.shape),
            row,
            row,
            row,
            columns(query_count, width),
        ]
        + [columns(s.shape[0], width) for s in sources],
        out_specs=[
            columns(query_count, width),
            columns(1, width),
            whole((8, slot_count)),
            row,
        ]
        + [whole((size, query_count)) for size in cuts],
        out_shape=[
            jax.ShapeDtypeStruct((query_count, width), jnp.bfloat16),
            jax.ShapeDtypeStruct((1, width), jnp.float32),
            jax.ShapeDtypeStruct((8, slot_count), jnp.float32),
            jax.ShapeDtypeStruct((1, query_count), jnp.float32),
        ]
        + [jax.ShapeDtypeStruct((size, query_count), jnp.bfloat16) for size in cuts],
        scratch_shapes=[pltpu.VMEM((query_count, line + slot_count), jnp.bfloat16)],
        compiler_params=params(32),
        cost_estimate=SMALL,
        name="query_side",
    )(near, far, asked_by, log_total, weight, target, queries, *sources)


def passage_side(coeff, queries, put, arrived, scale, layout):
    width = queries.shape[1]
    sizes = [sum(high - low for low, high in ranges) for ranges in layout]
    own = coeff.shape[0] - put.shape[0]

    def body(coeff_ref, query_ref, put_ref, arrived_ref, own_ref, *out_refs):
        total = mxu(coeff_ref[own:], query_ref[...]) + mxu(put_ref[...], arrived_ref[...])
        total = (scale * total).astype(jnp.bfloat16)
        for ranges, out_ref in zip(layout, out_refs):
            at = 0
            for low, high in ranges:
                out_ref[at : at + high - low] = total[low:high]
                at += high - low
        own_ref[...] = (scale * mxu(coeff_ref[:own], query_ref[...])).astype(jnp.bfloat16)

    return pl.pallas_call(
        body,
        grid=(width // (2 * tile(width)),),
        in_specs=[
            whole(coeff.shape),
            columns(queries.shape[0], width, 2),
            whole(put.shape),
            columns(arrived.shape[0], width, 2),
        ],
        out_specs=[columns(own, width, 2)] + [columns(size, width, 2) for size in sizes],
        out_shape=[
            jax.ShapeDtypeStruct((size, width), jnp.bfloat16) for size in (own, *sizes)
        ],
        compiler_params=params(32),
        cost_estimate=LARGE,
        name="passage_side",
    )(coeff, queries, put, arrived)


def add_passing(up, passing_low, down, passing_high):
    half, width = passing_low.shape
    rows = 2 * half

    def body(up_ref, low_ref, down_ref, high_ref, up_out, down_out):
        wide = jnp.float32
        up_out[:half] = (up_ref[:half].astype(wide) + low_ref[...].astype(wide)).astype(up.dtype)
        up_out[half:] = up_ref[half:]
        down_out[:half] = down_ref[:half]
        down_out[half:] = (down_ref[half:].astype(wide) + high_ref[...].astype(wide)).astype(
            up.dtype
        )

    return pl.pallas_call(
        body,
        grid=(width // tile(width),),
        in_specs=[
            columns(rows, width),
            columns(half, width),
            columns(rows, width),
            columns(half, width),
        ],
        out_specs=[columns(rows, width)] * 2,
        out_shape=[jax.ShapeDtypeStruct(up.shape, up.dtype)] * 2,
        compiler_params=params(12),
        cost_estimate=SMALL,
        name="add_passing",
    )(up, passing_low, down, passing_high)


def on_device(query_hidden, passage_hidden, norm_gain, query_weight, hneg_ids):
    rows, width = query_hidden.shape
    neg_count = hneg_ids.shape[1]
    z_count = lax.axis_size("z")
    group_count = 2 * z_count
    line = RING * rows
    scale = 1.0 / (SOFTMAX_TEMPER * math.sqrt(width))
    y_place, x_place = lax.axis_index("y"), lax.axis_index("x")

    gain = norm_gain.reshape(1, width)
    p_own = embed(passage_hidden, gain, 2)
    p_far, p_sent = ring_gather(*p_own, "y")

    flat_ids = hneg_ids.reshape(-1)
    id_count = rows * neg_count
    owners = flat_ids // rows
    local_row = flat_ids % rows
    number = jnp.arange(id_count, dtype=jnp.int32)
    same = (owners[:, None] == owners[None, :]) & (number[None, :] < number[:, None])
    rank = jnp.sum(same.astype(jnp.int32), axis=1)
    y_step = (owners // RING - y_place) % RING
    line_of = (owners // (RING * RING)) * RING + owners % RING
    slot = (line_of * RING + y_step) * CAP + rank
    slot_count = group_count * RING * RING * CAP
    hit = slot[None, :] == jnp.arange(slot_count, dtype=jnp.int32)[:, None]
    slot_row = jnp.sum(jnp.where(hit, local_row[None, :] + 1, 0), axis=1) - 1
    slot_query = jnp.sum(jnp.where(hit, number[None, :] // neg_count + 1, 0), axis=1)
    asked = lax.all_to_all(
        slot_row.reshape(group_count * RING, RING * CAP), ("z", "c", "x"), 0, 0, tiled=True
    )
    asked = asked.reshape(group_count, RING, RING, CAP).transpose(0, 2, 1, 3)
    place = jnp.arange(line, dtype=jnp.int32)
    asked, query_hidden, _ = lax.optimization_barrier((asked, query_hidden, p_sent))
    asked_own = asked[:, 0].reshape(-1)
    half = rows // 2

    def moved(block, base):
        return jnp.where(block < 0, -1, block + base + jnp.where(block >= half, half, 0))

    asked_far = jnp.concatenate(
        [asked[:, 1:2], moved(asked[:, 3:], rows + half), moved(asked[:, 2:3], rows)], axis=1
    ).reshape(-1)

    def one_hot(numbers, size):
        return (numbers[:, None] == place[None, :size]).astype(jnp.bfloat16)

    chosen_own = pick_rows(one_hot(asked_own, rows), p_own)
    hard_own = group_rows(chosen_own, group_count)
    chosen_far = pick_rows(one_hot(asked_far, 3 * rows), p_far)
    hard_far = group_rows(chosen_far, group_count)

    q_emb = embed(query_hidden, gain, 1)[0]
    q_line = lax.all_gather(q_emb, "x", axis=0, tiled=True)

    by_x = slot_query.reshape(group_count, RING, RING * CAP).transpose(1, 0, 2)
    asker = line_table(by_x.reshape(RING, -1)).reshape(RING, group_count, RING, CAP)
    x_base = rows * jnp.arange(RING, dtype=jnp.int32)
    asker = jnp.where(asker == 0, -1, asker - 1 + x_base[:, None, None, None])
    asker = asker.transpose(1, 2, 0, 3)
    far_asker = jnp.concatenate([asker[:, 1:2], asker[:, 3:], asker[:, 2:3]], axis=1)
    send_own = one_hot(asker[:, 0].reshape(-1), line)
    send_far = one_hot(far_asker.reshape(-1), line)
    asked_by = jnp.concatenate([send_own, send_far], axis=0)
    leave_far = pick_rows(send_far, [q_line])
    leave_own = pick_rows(send_own, [q_line])
    q_line, leave_far, leave_own = lax.optimization_barrier((q_line, leave_far, leave_own))
    far_queries = group_rows(leave_far, group_count)
    own_queries = group_rows(leave_own, group_count)

    near = line_scores([*p_own, *p_far, hard_own], q_line, scale)
    far, part_log = far_scores(near, [hard_far], q_line, asked_by, line, scale)
    part_log = part_log.reshape(RING, rows)
    own_place = jnp.arange(RING, dtype=jnp.int32)[:, None] == x_place
    own_weight = jnp.where(own_place, query_weight[None, :], 0.0)
    message = jnp.concatenate([part_log, own_weight], axis=0)
    messages = [message] + [shift(message, "x", step) for step in (1, 3, 2)]
    logs = [m[:RING] for m in messages]
    weight = sum(m[RING:] for m in messages).reshape(1, line)
    top = jnp.maximum(jnp.maximum(logs[0], logs[1]), jnp.maximum(logs[2], logs[3]))
    log_total = (top + jnp.log(sum(jnp.exp(part - top) for part in logs))).reshape(1, line)
    first_row = x_place * rows
    target = place[None, :] - first_row
    target = jnp.where((target >= 0) & (target < rows), target, -1)

    part, gain_part, slot_coeff, positive, coeff = query_side(
        near, far, asked_by, log_total, weight, target, q_line,
        [*p_own, *p_far, hard_own, hard_far], line, scale,
    )
    loss_rows = lax.dynamic_slice(log_total - positive, (0, first_row), (1, rows)).reshape(-1)
    query_up = lax.psum_scatter(part, "x", scatter_dimension=0, tiled=True)
    query_grad = finish(query_hidden, gain, [query_up])

    own_end = group_count * RING * CAP
    pieces = (
        slot_coeff[0, :own_end].reshape(group_count, -1),
        slot_coeff[0, own_end:].reshape(group_count, -1),
    )
    got_coeff = group_table(jnp.concatenate(pieces, axis=1), group_count)
    first = RING * CAP

    def put_rows(numbers, values, size):
        return jnp.where(
            place[:size, None] == numbers[None, :], values.reshape(-1)[None, :], 0.0
        ).astype(jnp.bfloat16)

    put_own = put_rows(asked_own, got_coeff[:, :first], rows)
    put_far = put_rows(asked_far, got_coeff[:, first:], 3 * rows)
    low_1, high_1, low_2, low_3, high_2, high_3 = [(i * half, (i + 1) * half) for i in range(6)]
    own_part, for_above, for_below, pass_up, pass_down = passage_side(
        coeff, q_line, put_far, far_queries, scale,
        [[low_1, high_1], [low_3, high_3], [low_2], [high_2]],
    )
    passing_low = shift(pass_up, "y", 1)
    passing_high = shift(pass_down, "y", -1)
    gain_part = pair_sum(pair_sum(gain_part.reshape(-1, 128), "z", False), "z", True)
    gain_part, passing_low = lax.optimization_barrier((gain_part, passing_low))
    for_above, for_below = add_passing(for_above, passing_low, for_below, passing_high)
    from_below = shift(for_above, "y", 1)
    from_above = shift(for_below, "y", -1)
    gain_part, _ = lax.optimization_barrier((gain_part, for_above))
    gain_part = pair_sum(gain_part, "c", False)
    gain_part = pair_sum(pair_sum(gain_part, "x", False), "x", True)
    gain_part, query_grad = lax.optimization_barrier((gain_part, query_grad))
    gain_part = pair_sum(pair_sum(gain_part, "y", False), "y", True)
    gain_grad = 2.0 * gain_part.reshape(-1) / norm_gain
    passage_grad = finish(
        passage_hidden, gain, [own_part, from_below, from_above], put_own, own_queries, scale
    )
    return (loss_rows, query_grad, passage_grad, gain_grad)


def solution(mesh):
    torus = Mesh(mesh.devices.reshape(-1, 2, RING, RING), ALL_AXES)
    return jax.shard_map(
        on_device,
        mesh=torus,
        in_specs=(
            P(ALL_AXES, None),
            P(ALL_AXES, None),
            P(),
            P(ALL_AXES),
            P(ALL_AXES, None),
        ),
        out_specs=(
            P(ALL_AXES),
            P(ALL_AXES, None),
            P(ALL_AXES, None),
            P(),
        ),
        check_vma=False,
    )
```
